256 devices in a mesh: ia: 4 (over z_hi), ja: 16 (over x, z_lo, core), ka: 4 (over y).
Axes of the slice: x: 4, y: 4, z: 8 (z_hi: 4, z_lo: 2; z = z_hi * 2 + z_lo), core: 2. Of those that a mesh axis runs over, the one named last changes fastest.
Arguments:
- tensor: bfloat16 [512, 1024, 1024], P('ia', 'ja', 'ka'), may hold values from -80 to 80
- factor_b: float32 [16, 16, 4, 512], P('ja', ('ia', 'ka')), may hold values from -5 to 5
- factor_c: float32 [4, 64, 4, 512], P('ka', ('ia', 'ja')), may hold values from -5 to 5
Outputs:
- factor_a_new: float32 [4, 64, 2, 512], P('ia', ('ja', 'ka'))
- factor_b_new: float32 [16, 16, 4, 512], P('ja', ('ia', 'ka'))
- factor_c_new: float32 [4, 64, 4, 512], P('ka', ('ia', 'ja'))
The draws below stay inside these ranges and needn't reach their ends.
All inputs are finite; a program needn't handle non-finite values.
Results may differ from the reference program's by a relative error of at most 0.02.
Values sent between devices are 32-bit elements; how exact they have to be, the bound alone decides.
A program may use at most 128 MiB of HBM per device.

```python
import math
import jax
import jax.numpy as jnp
from jax import lax

RANK = 512
DIM_I = 512
DIM_J = 1024
DIM_K = 1024
OWN_I = 2
OWN_J = 4
OWN_K = 4
N_IA = 4
N_JA = 16
N_KA = 4


def index_scale(key, count, growth):
    position = jnp.arange(count, dtype=jnp.float32) / (count - 1)
    roughness = jax.random.uniform(key, (count,), jnp.float32, math.log(0.7), math.log(1.4))
    return jnp.exp(math.log(growth) * (position - 0.5) + roughness)


def draw_tensor(key, part):
    key = jax.random.fold_in(key, 11)
    key_i, key_j, key_k, key_v = jax.random.split(key, 4)
    shape = (DIM_I, DIM_J, DIM_K)
    growth = 3.0
    values = jax.random.truncated_normal(key_v, -4.0, 4.0, shape, jnp.float32)
    factor_i = index_scale(key_i, DIM_I, growth)[:, None, None]
    factor_j = index_scale(key_j, DIM_J, growth)[None, :, None]
    factor_k = index_scale(key_k, DIM_K, growth)[None, None, :]
    return (values * factor_i * factor_j * factor_k).astype(jnp.bfloat16)


def shared_mixing(key, width):
    mixing_key = jax.random.fold_in(key, 5)
    values = jax.random.truncated_normal(mixing_key, -3.0, 3.0, (32, width), jnp.float32)
    return values / math.sqrt(32.0)


def combine_rows(latent, noise, mixing, scales):
    common = jnp.dot(latent, mixing, precision=lax.Precision.HIGHEST, preferred_element_type=jnp.float32)
    values = 0.5 * (common + 0.35 * noise) * scales[:, None]
    return jnp.clip(values, -5.0, 5.0)


def draw_factor_b(key, part):
    mixing = shared_mixing(key, RANK)
    key = jax.random.fold_in(key, 12)
    key_z, key_n, key_r = jax.random.split(key, 3)
    growth = 4.0
    latent = jax.random.truncated_normal(key_z, -3.0, 3.0, (DIM_J, 32), jnp.float32)
    noise = jax.random.truncated_normal(key_n, -3.0, 3.0, (DIM_J, RANK), jnp.float32)
    rows = combine_rows(latent, noise, mixing, index_scale(key_r, DIM_J, growth))
    return rows.reshape(N_JA, N_IA * N_KA, OWN_J, RANK)


def draw_factor_c(key, part):
    mixing = shared_mixing(key, RANK)
    key = jax.random.fold_in(key, 13)
    key_z, key_n, key_r = jax.random.split(key, 3)
    growth = 4.0
    latent = jax.random.truncated_normal(key_z, -3.0, 3.0, (DIM_K, 32), jnp.float32)
    noise = jax.random.truncated_normal(key_n, -3.0, 3.0, (DIM_K, RANK), jnp.float32)
    rows = combine_rows(latent, noise, mixing, index_scale(key_r, DIM_K, growth))
    return rows.reshape(N_KA, N_IA * N_JA, OWN_K, RANK)


def setup_inputs(seed: int = 0) -> dict:
    arg_keys = jax.random.split(jax.random.key(seed), 4)
    return {
        "tensor": draw_tensor(jax.random.fold_in(arg_keys[3], 71), 0),
        "factor_b": draw_factor_b(jax.random.fold_in(arg_keys[3], 71), 0),
        "factor_c": draw_factor_c(jax.random.fold_in(arg_keys[3], 71), 0),
    }


RIDGE = 0.1
EPS = 1e-06

def gram_of(matrix):
    return jnp.dot(matrix.T.astype(jnp.float32), matrix.astype(jnp.float32), precision=lax.Precision.HIGHEST, preferred_element_type=jnp.float32)

def solve_rows(partial_value, gram_one, gram_two):
    hadamard = gram_one * gram_two
    ridge = RIDGE * jnp.trace(hadamard) / hadamard.shape[0]
    system = hadamard + ridge * jnp.eye(hadamard.shape[0], dtype=jnp.float32)
    return jnp.linalg.solve(system, partial_value.T).T

def normalized(raw):
    return raw / jnp.sqrt(lax.optimization_barrier(jnp.mean(raw * raw, axis=0)) + EPS)

def reference(tensor, factor_b, factor_c):
    rank = factor_b.shape[-1]
    mat_b = factor_b.reshape(DIM_J, rank)
    mat_c = factor_c.reshape(DIM_K, rank)
    gram_b = gram_of(mat_b)
    gram_c = gram_of(mat_c)
    half_b = mat_b.astype(jnp.bfloat16).astype(jnp.float32)
    half_c = mat_c.astype(jnp.bfloat16).astype(jnp.float32)
    blocks = tensor.reshape(DIM_I // 32, 32, DIM_J, DIM_K)

    def mode_one(piece):
        mixed = jnp.einsum('ijk,kr->ijr', piece.astype(jnp.float32), half_c).astype(jnp.bfloat16)
        part = jnp.einsum('ijr,jr->ir', mixed.astype(jnp.float32), half_b)
        return (mixed, part)
    mixed_k, part_a = lax.map(mode_one, blocks)
    part_a = part_a.reshape(DIM_I, rank)
    new_a = normalized(solve_rows(part_a, gram_b, gram_c))
    gram_a = gram_of(new_a)
    half_a = new_a.astype(jnp.bfloat16).astype(jnp.float32).reshape(DIM_I // 32, 32, rank)

    def add_mode_two(total, items):
        mixed, rows = items
        return (total + jnp.einsum('ijr,ir->jr', mixed.astype(jnp.float32), rows), None)
    part_b, unused = lax.scan(add_mode_two, jnp.zeros((DIM_J, rank), jnp.float32), (mixed_k, half_a))
    new_b = normalized(solve_rows(part_b, gram_a, gram_c))
    gram_b2 = gram_of(new_b)
    half_b2 = new_b.astype(jnp.bfloat16).astype(jnp.float32)
    flat_a = half_a.reshape(DIM_I, rank)

    def mode_three(offset):
        piece = lax.dynamic_slice_in_dim(tensor, offset, 64, 2).astype(jnp.float32)
        inner = jnp.einsum('ijk,ir->jkr', piece, flat_a).astype(jnp.bfloat16)
        return jnp.einsum('jkr,jr->kr', inner.astype(jnp.float32), half_b2)
    offsets = jnp.arange(DIM_K // 64, dtype=jnp.int32) * 64
    part_c = lax.map(mode_three, offsets).reshape(DIM_K, rank)
    new_c = normalized(solve_rows(part_c, gram_a, gram_b2))
    out_a = new_a.reshape(N_IA, N_JA * N_KA, OWN_I, rank)
    out_b = new_b.reshape(N_JA, N_IA * N_KA, OWN_J, rank)
    out_c = new_c.reshape(N_KA, N_IA * N_JA, OWN_K, rank)
    return (out_a, out_b, out_c)
```

```python
import functools

import jax
import jax.numpy as jnp
from jax import lax
from jax.experimental import pallas as pl
from jax.experimental.pallas import tpu as pltpu
from jax.sharding import PartitionSpec as P

RIDGE = 0.1
EPS = 1e-06
F32 = jnp.float32
BF16 = jnp.bfloat16
RANK = 512
STEPS = 9
EXACT_STEPS = 2


def dot(left, right):
    return jnp.dot(left, right, preferred_element_type=F32)


def dot_rows(left, right):
    return lax.dot_general(left, right, (((0,), (0,)), ((), ())), preferred_element_type=F32)


def split_two(value):
    high = value.astype(BF16)
    low = (value - high.astype(F32)).astype(BF16)
    return high, low


def remote(src, dst, send_sem, recv_sem, device):
    return pltpu.make_async_remote_copy(
        src_ref=src,
        dst_ref=dst,
        send_sem=send_sem,
        recv_sem=recv_sem,
        device_id=device,
        device_id_type=pl.DeviceIdType.MESH,
    )


class Sender:
    def __init__(self, sems):
        self.sems = sems
        self.used = 0
        self.pending = []

    def send(self, src, dst, recv_sem, device, cond=None):
        sem = self.sems.at[self.used]
        self.used += 1
        copy = remote(src, dst, sem, recv_sem, device)
        if cond is None:
            copy.start()
        else:
            pl.when(cond)(copy.start)
        self.pending.append((copy, cond))

    def finish(self):
        for copy, cond in self.pending:
            if cond is None:
                copy.wait_send()
            else:
                pl.when(cond)(copy.wait_send)


def kernel(
    t_hbm, fb_ref, fc_ref, a_out, b_out, c_out,
    t_ref, mixed, own8, sib8, g1, ga, gb,
    pa, pb, pc, ra1, ra2, ra3, ra4, rb1, sb, rb2, rc1, sc, rc2, tc, rc3,
    rq1, rq2, rq3, sq1, sq2, sq3,
    mh, ml, gram_b, gram_c, gram_a, gram_b2, dmat, dh, dl, d3,
    bblk, cblk, ablk, b2blk, pvec,
    send_sems, r_sib, r_p0, r_p1, r_p2, r_p3, r_a, r_b, r_c, r_q, t_sem,
):
    ia = lax.axis_index("ia")
    ja = lax.axis_index("ja")
    ka = lax.axis_index("ka")
    core = lax.rem(ja, 2)
    zlo = lax.rem(ja // 2, 2)
    x = ja // 4
    y = ka
    z = ia * 2 + zlo
    half = ia // 2
    sel0 = 1 - core
    u = x * sel0 + y * core
    v = y * sel0 + x * core

    def dev(px, py, pz, pcore):
        return (pz // 2, px * 4 + lax.rem(pz, 2) * 2 + pcore, py)

    def dev_uv(pu, pv):
        return dev(pu * sel0 + pv * core, pv * sel0 + pu * core, z, core)

    sibling = dev(x, y, z, 1 - core)

    def at_x(d):
        return dev(lax.rem(x + d, 4), y, z, core)

    def at_y(d):
        return dev(x, lax.rem(y + d, 4), z, core)

    def at_z(d):
        return dev(x, y, lax.rem(z + d, 8), core)

    load_t = pltpu.make_async_copy(t_hbm, t_ref, t_sem)
    load_t.start()
    out = Sender(send_sems)

    barrier = pltpu.get_barrier_semaphore()
    partners = [sibling]
    partners += [at_x(d) for d in (1, 2, 3)]
    partners += [at_y(d) for d in (1, 2, 3)]
    partners += [at_z(d) for d in range(1, 8)]
    for partner in partners:
        pl.semaphore_signal(
            barrier, inc=1, device_id=partner, device_id_type=pl.DeviceIdType.MESH
        )

    own8[0:4, :] = fb_ref[0, 0]
    own8[4:8, :] = fc_ref[0, 0]
    pl.semaphore_wait(barrier, len(partners))

    def gather_all(buf, slot, slots, contributes, stage):
        me_contributes = contributes
        for d in range(1, 8):
            out.send(
                buf.at[core, v, u, slot], buf.at[core, v, u, slot],
                r_p0.at[stage, slot], at_z(d), me_contributes,
            )
        for s in range(slots):
            if slots == 4:
                other = jnp.logical_or(core != half, slot != s)
            else:
                other = jnp.logical_not(jnp.logical_and(me_contributes, slot == s))
            copy = remote(
                buf.at[core, v, u, s], buf.at[core, v, u, s], send_sems.at[0],
                r_p0.at[stage, s], at_z(1),
            )
            pl.when(other)(copy.wait_recv)
        for d in (1, 3, 2):
            out.send(
                buf.at[core, v, u], buf.at[core, v, u], r_p1.at[stage, d - 1],
                dev_uv(lax.rem(u + d, 4), v),
            )
        for d in (1, 3, 2):
            copy = remote(
                buf.at[core, v, d], buf.at[core, v, d], send_sems.at[0],
                r_p1.at[stage, d - 1], at_z(1),
            )
            copy.wait_recv()
        for d in (1, 3, 2):
            out.send(
                buf.at[core, v], buf.at[core, v], r_p2.at[stage, d - 1],
                dev_uv(u, lax.rem(v + d, 4)),
            )
        out.send(buf.at[core, v], buf.at[core, v], r_p3.at[stage, 0], sibling)
        for d in (1, 3, 2):
            slab = lax.rem(v + 4 - d, 4)
            copy = remote(
                buf.at[core, slab], buf.at[core, slab], send_sems.at[0],
                r_p2.at[stage, d - 1], at_z(1),
            )
            copy.wait_recv()
            out.send(buf.at[core, slab], buf.at[core, slab], r_p3.at[stage, d], sibling)
        for d in range(4):
            copy = remote(
                buf.at[1 - core, d], buf.at[1 - core, d], send_sems.at[0],
                r_p3.at[stage, d], at_z(1),
            )
            copy.wait_recv()

    def recv(ref, sem):
        return remote(ref, ref, send_sems.at[0], sem, sibling)

    def gram(out_ref, rows):
        def body(n, carry):
            rs = pl.ds(pl.multiple_of(n * 256, 256), 256)
            high, low = mh[rs, :], ml[rs, :]
            out_ref[...] += dot_rows(high, high) + dot_rows(high, low) + dot_rows(low, high)
            return carry

        out_ref[...] = jnp.zeros_like(out_ref)
        lax.fori_loop(0, rows // 256, body, 0)

    def start_chain(one, two):
        def eye(n):
            row = lax.broadcasted_iota(jnp.int32, (64, RANK), 0) + n * 64
            col = lax.broadcasted_iota(jnp.int32, (64, RANK), 1)
            return row == col

        def first(n, carry):
            trace, frob = carry
            rs = pl.ds(pl.multiple_of(n * 64, 64), 64)
            value = one[rs, :] * two[rs, :]
            dmat[rs, :] = value
            trace += jnp.sum(jnp.where(eye(n), value, 0.0), axis=0, keepdims=True)
            frob += jnp.sum(value * value, axis=0, keepdims=True)
            return trace, frob

        zero = jnp.zeros((1, RANK), F32)
        trace, frob = lax.fori_loop(0, 8, first, (zero, zero))
        ridge = RIDGE * jnp.sum(trace, axis=1, keepdims=True) / RANK
        top = ridge + jnp.sqrt(jnp.sum(frob, axis=1, keepdims=True))
        scale = 2.0 / (top + ridge)
        sigma = (top + ridge) / (top - ridge)

        def second(n, carry):
            rs = pl.ds(pl.multiple_of(n * 64, 64), 64)
            value = (dmat[rs, :] + jnp.where(eye(n), ridge, 0.0)) * scale
            dmat[rs, :] = value
            high, low = split_two(value)
            dh[0, rs, :] = high
            dl[0, rs, :] = low
            d3[rs, :] = (value - high.astype(F32) - low.astype(F32)).astype(BF16)
            return carry

        lax.fori_loop(0, 8, second, 0)
        factors = []
        for q in range(STEPS):
            twice = 2.0 * sigma * sigma
            factors.append(twice / (twice - 1.0))
            sigma = twice - 1.0
        return scale, factors

    def chain_step(q, factor):
        def body(n, carry):
            cs = pl.ds(pl.multiple_of(n * 256, 256), 256)
            high, low = dh[q], dl[q]
            square = dot(high, dh[q, :, cs]) + dot(high, dl[q, :, cs]) + dot(low, dh[q, :, cs])
            if q < EXACT_STEPS:
                square += (
                    dot(low, dl[q, :, cs]) + dot(high, d3[:, cs]) + dot(d3[...], dh[q, :, cs])
                )
            value = factor * (2.0 * dmat[:, cs] - square)
            dmat[:, cs] = value
            high, low = split_two(value)
            dh[q + 1, :, cs] = high
            dl[q + 1, :, cs] = low
            return carry

        lax.fori_loop(0, 2, body, 0)
        if q + 1 < EXACT_STEPS:
            def third(n, carry):
                rs = pl.ds(pl.multiple_of(n * 64, 64), 64)
                d3[rs, :] = (
                    dmat[rs, :] - dh[q + 1, rs, :].astype(F32) - dl[q + 1, rs, :].astype(F32)
                ).astype(BF16)
                return carry

            lax.fori_loop(0, 8, third, 0)

    def apply_step(q, factor, value):
        high, low = split_two(value)
        both = jnp.concatenate([high.astype(F32), low.astype(F32)], axis=0).astype(BF16)
        wide = dot(both, dh[q])
        narrow = dot(both, dl[q])
        return factor * (2.0 * value - (wide[0:8] + wide[8:16] + narrow[0:8]))

    def solve(rows, scale, factors):
        value = rows * scale
        for q in range(STEPS):
            value = apply_step(q, factors[q], value)
        return value

    to_sib = remote(own8, sib8, send_sems.at[0], r_sib.at[0], sibling)
    to_sib.start()
    out.used = 1
    out.pending.append((to_sib, None))
    to_sib.wait_recv()
    slot = lax.rem(ia, 2) * 2 + zlo
    contributes = core == half

    @pl.when(jnp.logical_and(contributes, core == 0))
    def _():
        g1[core, v, u, slot, 0:4, :] = own8[0:4, :]
        g1[core, v, u, slot, 4:8, :] = sib8[0:4, :]
        g1[core, v, u, slot, 8:12, :] = own8[4:8, :]
        g1[core, v, u, slot, 12:16, :] = sib8[4:8, :]

    @pl.when(jnp.logical_and(contributes, core == 1))
    def _():
        g1[core, v, u, slot, 0:4, :] = sib8[0:4, :]
        g1[core, v, u, slot, 4:8, :] = own8[0:4, :]
        g1[core, v, u, slot, 8:12, :] = sib8[4:8, :]
        g1[core, v, u, slot, 12:16, :] = own8[4:8, :]

    gather_all(g1, slot, 4, contributes, 0)

    def fill_c(n, carry):
        pia, rest = n // 8, lax.rem(n, 8)
        px, pzlo = rest // 2, lax.rem(rest, 2)
        ph = pia // 2
        pu = px * (1 - ph) + y * ph
        pv = y * (1 - ph) + px * ph
        ps = lax.rem(pia, 2) * 2 + pzlo
        cblk[pl.ds(pl.multiple_of(n * 8, 8), 8), :] = g1[ph, pv, pu, ps, 8:16, :]
        return carry

    lax.fori_loop(0, 32, fill_c, 0)

    def fill_b(n, carry):
        pia, py = n // 2, lax.rem(n, 2) * 2
        ph = pia // 2
        ps = lax.rem(pia, 2) * 2 + zlo

        def piece(yy):
            pu = x * (1 - ph) + yy * ph
            pv = yy * (1 - ph) + x * ph
            return g1[ph, pv, pu, ps, 0:8, :]

        one, two = piece(py), piece(py + 1)

        @pl.when(core == 0)
        def _():
            pvec[0:4, :] = one[0:4]
            pvec[4:8, :] = two[0:4]

        @pl.when(core == 1)
        def _():
            pvec[0:4, :] = one[4:8]
            pvec[4:8, :] = two[4:8]

        bblk[pl.ds(pl.multiple_of(n * 8, 8), 8), :] = pvec[...].astype(BF16).astype(F32)
        return carry

    lax.fori_loop(0, 8, fill_b, 0)

    load_t.wait()

    def contract(g, carry):
        half_c = cblk[...].astype(BF16)
        weight = bblk[...]
        parts = []
        for s in range(2):
            piece = t_ref[pl.ds(g * 8 + s * 4, 4)].reshape(256, 256)
            value = dot(piece, half_c).astype(BF16).reshape(4, 64, RANK)
            mixed[pl.ds(g * 8 + s * 4, 4)] = value
            parts.append(jnp.sum(value.astype(F32) * weight[None], axis=1))
        pa[g] = jnp.concatenate(parts, axis=0)
        return carry

    lax.fori_loop(0, 16, contract, 0)

    not_half = core != half
    out.send(pa, ra1, r_a.at[0], sibling, not_half)

    def load_g1(offset):
        def body(n, carry):
            ph = n // 16
            pv = lax.rem(n // 4, 4)
            pu = lax.rem(n, 4)
            rows = g1[ph, pv, pu, :, offset:offset + 8, :].reshape(32, RANK)
            high, low = split_two(rows)
            rs = pl.ds(pl.multiple_of(n * 32, 32), 32)
            mh[rs, :] = high
            ml[rs, :] = low
            return carry

        lax.fori_loop(0, 32, body, 0)

    load_g1(0)
    gram(gram_b, 1024)
    a_owner = jnp.logical_and(core == half, lax.rem(x, 2) == zlo)

    @pl.when(core == half)
    def _():
        recv(ra1, r_a.at[0]).wait_recv()
        pa[...] += ra1[...]

    for m in range(2):
        px = 1 - zlo + 2 * m
        out.send(
            pa.at[pl.ds(px * 4, 4)], ra2.at[m], r_a.at[1 + m],
            dev(x, y, ia * 2 + 1 - zlo, core), core == half,
        )
    load_g1(8)
    gram(gram_c, 1024)

    @pl.when(core == half)
    def _():
        for m in range(2):
            recv(ra2.at[m], r_a.at[1 + m]).wait_recv()
            px = zlo + 2 * m
            pa[pl.ds(px * 4, 4)] += ra2[m]

    for d in (1, 2, 3):
        px = lax.rem(x + d, 4)
        out.send(
            pa.at[pl.ds(px * 4, 4)], ra3.at[d - 1], r_a.at[2 + d], at_x(d),
            jnp.logical_and(core == half, lax.rem(px, 2) == zlo),
        )
    scale, factors = start_chain(gram_b, gram_c)
    chain_step(0, factors[0])

    @pl.when(a_owner)
    def _():
        for d in (1, 2, 3):
            recv(ra3.at[d - 1], r_a.at[2 + d]).wait_recv()
        pa[pl.ds(x * 4, 4)] += ra3[0] + ra3[1] + ra3[2]

    for d in (1, 2, 3):
        out.send(
            pa.at[x * 4 + lax.rem(y + d, 4)], ra4.at[d - 1], r_a.at[5 + d], at_y(d), a_owner
        )
    for q in range(1, STEPS - 1):
        chain_step(q, factors[q])

    aslot = lax.rem(ia, 2)

    @pl.when(a_owner)
    def _():
        for d in (1, 2, 3):
            recv(ra4.at[d - 1], r_a.at[5 + d]).wait_recv()
        rows = pa[x * 4 + y] + ra4[0] + ra4[1] + ra4[2]
        ga[core, v, u, aslot] = solve(rows, scale, factors)

    gather_all(ga, aslot, 2, a_owner, 1)

    def scale_rows(buf, count, rows):
        def squares(n, total):
            value = buf[n // 16, lax.rem(n // 4, 4), lax.rem(n, 4)].reshape(rows, RANK)
            return total + jnp.sum(value * value, axis=0, keepdims=True)

        total = lax.fori_loop(0, 32, squares, jnp.zeros((1, RANK), F32))
        spread = jnp.sqrt(total / count + EPS)

        def normal(n, carry):
            value = buf[n // 16, lax.rem(n // 4, 4), lax.rem(n, 4)].reshape(rows, RANK) / spread
            high, low = split_two(value)
            rs = pl.ds(pl.multiple_of(n * rows, rows), rows)
            mh[rs, :] = high
            ml[rs, :] = low
            return carry

        lax.fori_loop(0, 32, normal, 0)
        return spread

    spread_a = scale_rows(ga, 512, 16)

    def fill_a(n, carry):
        px, py = n // 4, lax.rem(n, 4)
        pu = px * (1 - half) + py * half
        pv = py * (1 - half) + px * half
        ablk[pl.ds(pl.multiple_of(n * 8, 8), 8), :] = ga[half, pv, pu, aslot] / spread_a
        return carry

    lax.fori_loop(0, 16, fill_a, 0)
    own_a = ablk[pl.ds(pl.multiple_of(ja * 8, 8), 8), :]
    for s in range(4):
        @pl.when(ka == s)
        def _():
            a_out[0, 0] = own_a[2 * s:2 * s + 2]

    def second_mode(g, total):
        rows = ablk[pl.ds(pl.multiple_of(g * 8, 8), 8), :].astype(BF16).astype(F32)
        for s in range(8):
            total = total + mixed[g * 8 + s].astype(F32) * rows[s:s + 1, :]
        return total

    part_b = lax.fori_loop(0, 16, second_mode, jnp.zeros((64, RANK), F32))
    for o in range(8):
        pb[o % 4, o // 4] = part_b[o * 8:o * 8 + 8]
    for d in (1, 2, 3):
        out.send(pb.at[lax.rem(y + d, 4)], rb1.at[d - 1], r_b.at[d - 1], at_y(d))
    gram(gram_a, 512)
    for d in (1, 2, 3):
        recv(rb1.at[d - 1], r_b.at[d - 1]).wait_recv()
    sb[...] = pb[y] + rb1[0] + rb1[1] + rb1[2]
    for d in (1, 2, 3):
        pia = lax.rem(ia + d, 4)
        out.send(
            sb.at[lax.rem(pia, 2)], rb2.at[d - 1], r_b.at[2 + d],
            dev(x, y, pia * 2 + zlo, core), pia // 2 == core,
        )
    scale, factors = start_chain(gram_a, gram_c)
    for q in range(STEPS - 1):
        chain_step(q, factors[q])

    @pl.when(core == half)
    def _():
        for d in (1, 2, 3):
            recv(rb2.at[d - 1], r_b.at[2 + d]).wait_recv()
        rows = sb[lax.rem(ia, 2)] + rb2[0] + rb2[1] + rb2[2]
        gb[core, v, u, slot] = solve(rows, scale, factors)

    gather_all(gb, slot, 4, contributes, 2)
    spread_b = scale_rows(gb, 1024, 32)

    def fill_b2(n, carry):
        py = lax.rem(n, 4)
        pu = x * sel0 + py * core
        pv = py * sel0 + x * core
        b2blk[pl.ds(pl.multiple_of(n * 8, 8), 8), :] = gb[core, pv, pu, (n // 4) * 2 + zlo] / spread_b
        return carry

    lax.fori_loop(0, 8, fill_b2, 0)
    own_b = b2blk[pl.ds(pl.multiple_of((ia * 2 + ka // 2) * 8, 8), 8), :]
    for s in range(2):
        @pl.when(lax.rem(ka, 2) == s)
        def _():
            b_out[0, 0] = own_b[4 * s:4 * s + 4]

    pc[...] = jnp.zeros_like(pc)

    def third_mode(g, carry):
        rows = ablk[pl.ds(pl.multiple_of(g * 8, 8), 8), :].astype(BF16)
        half_b2 = b2blk[...].astype(BF16)
        for s in range(2):
            piece = t_ref[pl.ds(g * 8 + s * 4, 4)].reshape(256, 256)
            weight = jnp.concatenate(
                [half_b2 * rows[s * 4 + n:s * 4 + n + 1, :] for n in range(4)], axis=0
            )
            pc[...] += dot_rows(piece, weight).reshape(4, 4, 2, 8, RANK)
        return carry

    lax.fori_loop(0, 16, third_mode, 0)
    for d in (1, 2, 3):
        out.send(pc.at[:, lax.rem(x + d, 4)], rc1.at[d - 1], r_c.at[d - 1], at_x(d))
    gram(gram_b2, 1024)
    for d in (1, 2, 3):
        recv(rc1.at[d - 1], r_c.at[d - 1]).wait_recv()
    sc[...] = pc[:, x] + rc1[0] + rc1[1] + rc1[2]
    for d in range(1, 8):
        pz = lax.rem(z + d, 8)
        out.send(sc.at[pz // 2, lax.rem(pz, 2)], rc2.at[d - 1], r_c.at[2 + d], at_z(d))
    scale, factors = start_chain(gram_a, gram_b2)
    for q in range(STEPS - 1):
        chain_step(q, factors[q])
        if q == 2:
            for d in range(1, 8):
                recv(rc2.at[d - 1], r_c.at[2 + d]).wait_recv()
            total = sc[ia, zlo]
            for d in range(7):
                total = total + rc2[d]
            tc[...] = total
            out.send(tc, rc3, r_c.at[10], sibling)
    recv(rc3, r_c.at[10]).wait_recv()
    raw = solve(tc[...] + rc3[...], scale, factors)

    sq1[...] = raw * raw
    for d in (1, 2, 3):
        out.send(sq1, rq1.at[d - 1], r_q.at[d - 1], at_x(d))
    for d in (1, 2, 3):
        recv(rq1.at[d - 1], r_q.at[d - 1]).wait_recv()
    sq2[...] = sq1[...] + rq1[0] + rq1[1] + rq1[2]
    for d in (1, 2, 3):
        out.send(sq2, rq2.at[d - 1], r_q.at[2 + d], at_y(d))
    for d in (1, 2, 3):
        recv(rq2.at[d - 1], r_q.at[2 + d]).wait_recv()
    sq3[...] = sq2[...] + rq2[0] + rq2[1] + rq2[2]
    for d in range(1, 8):
        out.send(sq3, rq3.at[d - 1], r_q.at[5 + d], at_z(d))
    for d in range(1, 8):
        recv(rq3.at[d - 1], r_q.at[5 + d]).wait_recv()
    total = sq3[...]
    for d in range(7):
        total = total + rq3[d]
    spread = jnp.sqrt(jnp.sum(total, axis=0, keepdims=True) / 1024 + EPS)
    final = raw / spread
    for s in range(2):
        @pl.when(core == s)
        def _():
            c_out[0, 0] = final[4 * s:4 * s + 4]

    out.finish()


def shards(tensor, factor_b, factor_c):
    vmem = pltpu.VMEM
    dma = pltpu.SemaphoreType.DMA
    scratch = [
        vmem((128, 64, 256), BF16),
        vmem((128, 64, RANK), BF16),
        vmem((8, RANK), F32),
        vmem((8, RANK), F32),
        vmem((2, 4, 4, 4, 16, RANK), F32),
        vmem((2, 4, 4, 2, 8, RANK), F32),
        vmem((2, 4, 4, 4, 8, RANK), F32),
        vmem((16, 8, RANK), F32),
        vmem((4, 2, 8, RANK), F32),
        vmem((4, 4, 2, 8, RANK), F32),
        vmem((16, 8, RANK), F32),
        vmem((2, 4, 8, RANK), F32),
        vmem((3, 4, 8, RANK), F32),
        vmem((3, 8, RANK), F32),
        vmem((3, 2, 8, RANK), F32),
        vmem((2, 8, RANK), F32),
        vmem((3, 8, RANK), F32),
        vmem((3, 4, 2, 8, RANK), F32),
        vmem((4, 2, 8, RANK), F32),
        vmem((7, 8, RANK), F32),
        vmem((8, RANK), F32),
        vmem((8, RANK), F32),
        vmem((3, 8, RANK), F32),
        vmem((3, 8, RANK), F32),
        vmem((7, 8, RANK), F32),
        vmem((8, RANK), F32),
        vmem((8, RANK), F32),
        vmem((8, RANK), F32),
        vmem((1024, RANK), BF16),
        vmem((1024, RANK), BF16),
        vmem((RANK, RANK), F32),
        vmem((RANK, RANK), F32),
        vmem((RANK, RANK), F32),
        vmem((RANK, RANK), F32),
        vmem((RANK, RANK), F32),
        vmem((STEPS, RANK, RANK), BF16),
        vmem((STEPS, RANK, RANK), BF16),
        vmem((RANK, RANK), BF16),
        vmem((64, RANK), F32),
        vmem((256, RANK), F32),
        vmem((128, RANK), F32),
        vmem((64, RANK), F32),
        vmem((8, RANK), F32),
        dma((112,)),
        dma((1,)),
        dma((3, 4)),
        dma((3, 3)),
        dma((3, 3)),
        dma((3, 4)),
        dma((9,)),
        dma((6,)),
        dma((11,)),
        dma((13,)),
        dma,
    ]
    return pl.pallas_call(
        kernel,
        out_shape=(
            jax.ShapeDtypeStruct((1, 1, 2, RANK), F32),
            jax.ShapeDtypeStruct((1, 1, 4, RANK), F32),
            jax.ShapeDtypeStruct((1, 1, 4, RANK), F32),
        ),
        in_specs=[
            pl.BlockSpec(memory_space=pl.ANY),
            pl.BlockSpec(memory_space=pltpu.VMEM),
            pl.BlockSpec(memory_space=pltpu.VMEM),
        ],
        out_specs=[pl.BlockSpec(memory_space=pltpu.VMEM)] * 3,
        scratch_shapes=scratch,
        compiler_params=pltpu.CompilerParams(
            collective_id=0, has_side_effects=True, vmem_limit_bytes=58 * 1024 * 1024
        ),
        name="sweep",
    )(tensor, factor_b, factor_c)


def solution(mesh):
    in_specs = (
        P("ia", "ja", "ka"),
        P("ja", ("ia", "ka"), None, None),
        P("ka", ("ia", "ja"), None, None),
    )
    out_specs = (
        P("ia", ("ja", "ka"), None, None),
        P("ja", ("ia", "ka"), None, None),
        P("ka", ("ia", "ja"), None, None),
    )
    return jax.shard_map(shards, mesh=mesh, in_specs=in_specs, out_specs=out_specs, check_vma=False)
```

```python
import functools

import jax
import jax.numpy as jnp
from jax import lax
from jax.experimental import pallas as pl
from jax.experimental.pallas import tpu as pltpu
from jax.sharding import PartitionSpec as P

RIDGE = 0.1
EPS = 1e-06
F32 = jnp.float32
BF16 = jnp.bfloat16
RANK = 512
STEPS = 9
EXACT_STEPS = 1


def dot(left, right):
    return jnp.dot(left, right, preferred_element_type=F32)


def dot_rows(left, right):
    return lax.dot_general(left, right, (((0,), (0,)), ((), ())), preferred_element_type=F32)


def split_two(value):
    high = value.astype(BF16)
    low = (value - high.astype(F32)).astype(BF16)
    return high, low


def remote(src, dst, send_sem, recv_sem, device):
    return pltpu.make_async_remote_copy(
        src_ref=src,
        dst_ref=dst,
        send_sem=send_sem,
        recv_sem=recv_sem,
        device_id=device,
        device_id_type=pl.DeviceIdType.MESH,
    )


class Sender:
    def __init__(self, sems):
        self.sems = sems
        self.used = 0
        self.pending = []

    def send(self, src, dst, recv_sem, device, cond=None):
        sem = self.sems.at[self.used]
        self.used += 1
        copy = remote(src, dst, sem, recv_sem, device)
        if cond is None:
            copy.start()
        else:
            pl.when(cond)(copy.start)
        self.pending.append((copy, cond))

    def finish(self):
        for copy, cond in self.pending:
            if cond is None:
                copy.wait_send()
            else:
                pl.when(cond)(copy.wait_send)


def kernel(
    t_hbm, fb_ref, fc_ref, a_out, b_out, c_out,
    t_ref, tt, mixed, arep, own8, sib8, g_b, g_c, ga, gb,
    pa, pb, pc, ra1, ra2, ra3, ra4, rb1, sb, rb2, rc0, rc1, sc, rc2, tc, rc3,
    rq1, rq2, rq3, sq1, sq2, sq3,
    mh, ml, gram_b, gram_c, gram_a, gram_b2, dmat, dh, dl, d3, yvec,
    bblk, cblk, ablk, b2blk, pvec,
    send_sems, r_sib, r_p0, r_p1, r_p2, r_p3, r_a, r_b, r_c, r_q, t_sem,
):
    ia = lax.axis_index("ia")
    ja = lax.axis_index("ja")
    ka = lax.axis_index("ka")
    core = lax.rem(ja, 2)
    zlo = lax.rem(ja // 2, 2)
    x = ja // 4
    y = ka
    z = ia * 2 + zlo
    half = ia // 2
    sel0 = 1 - core

    def dev(px, py, pz, pcore):
        return (pz // 2, px * 4 + lax.rem(pz, 2) * 2 + pcore, py)

    sibling = dev(x, y, z, 1 - core)

    def at_x(d):
        return dev(lax.rem(x + d, 4), y, z, core)

    def at_y(d):
        return dev(x, lax.rem(y + d, 4), z, core)

    def at_z(d):
        return dev(x, y, lax.rem(z + d, 8), core)

    load_t = pltpu.make_async_copy(t_hbm, t_ref, t_sem)
    load_t.start()
    out = Sender(send_sems)

    barrier = pltpu.get_barrier_semaphore()
    partners = [sibling]
    partners += [at_x(d) for d in (1, 2, 3)]
    partners += [at_y(d) for d in (1, 2, 3)]
    partners += [at_z(d) for d in range(1, 8)]
    for partner in partners:
        pl.semaphore_signal(
            barrier, inc=1, device_id=partner, device_id_type=pl.DeviceIdType.MESH
        )

    own8[0:4, :] = fb_ref[0, 0]
    own8[4:8, :] = fc_ref[0, 0]
    pl.semaphore_wait(barrier, len(partners))

    def recv(ref, sem):
        return remote(ref, ref, send_sems.at[0], sem, sibling)

    class Gather:
        def __init__(self, buf, stage, slots, slot, contributes, u_is_x):
            self.buf, self.stage, self.slots, self.slot = buf, stage, slots, slot
            self.contributes = contributes
            self.u_is_x = u_is_x
            self.u = x * u_is_x + y * (1 - u_is_x)
            self.v = y * u_is_x + x * (1 - u_is_x)
            self.p0 = [r_p0.at[stage, n] for n in range(slots)]
            self.p1 = [r_p1.at[stage, n] for n in range(4)]
            self.p2 = [r_p2.at[stage, n] for n in range(6)]
            self.p3 = [r_p3.at[stage, n] for n in range(4)]

        def near(self, du, dv):
            pu, pv = lax.rem(self.u + du + 4, 4), lax.rem(self.v + dv + 4, 4)
            keep = self.u_is_x
            return dev(pu * keep + pv * (1 - keep), pv * keep + pu * (1 - keep), z, core)

        def move(self, ref, sem, device):
            out.send(ref, ref, sem, device)

        def chunk(self, du, first=None):
            pu = lax.rem(self.u + du + 4, 4)
            if first is None:
                return self.buf.at[core, self.v, pu]
            size = self.slots // 2
            return self.buf.at[core, self.v, pu, pl.ds(first * size, size)]

        def slab(self, dv, first=None):
            pv = lax.rem(self.v + dv + 4, 4)
            if first is None:
                return self.buf.at[core, pv]
            return self.buf.at[core, pv, pl.ds(first * 2, 2)]

        def p0_send(self):
            ref = self.buf.at[core, self.v, self.u, self.slot]
            for d in (4, 3, 5, 2, 6, 1, 7):
                out.send(ref, ref, r_p0.at[self.stage, self.slot], at_z(d), self.contributes)

        def p0_wait(self):
            for s in range(self.slots):
                other = jnp.logical_not(jnp.logical_and(self.contributes, self.slot == s))
                copy = recv(self.buf.at[core, self.v, self.u, s], self.p0[s])
                pl.when(other)(copy.wait_recv)

        def p1_send(self):
            self.move(self.chunk(0), self.p1[0], self.near(1, 0))
            self.move(self.chunk(0), self.p1[1], self.near(-1, 0))

        def p1_forward(self):
            recv(self.chunk(-1), self.p1[0]).wait_recv()
            self.move(self.chunk(-1, 0), self.p1[2], self.near(1, 0))
            recv(self.chunk(1), self.p1[1]).wait_recv()
            self.move(self.chunk(1, 1), self.p1[3], self.near(-1, 0))

        def p1_finish(self):
            recv(self.chunk(-2, 0), self.p1[2]).wait_recv()
            recv(self.chunk(2, 1), self.p1[3]).wait_recv()

        def p2_send(self):
            self.move(self.slab(0, 0), self.p2[0], self.near(0, 1))
            self.move(self.slab(0, 1), self.p2[2], self.near(0, -1))
            self.move(self.slab(0, 1), self.p2[1], self.near(0, 1))
            self.move(self.slab(0, 0), self.p2[3], self.near(0, -1))

        def p3_send(self, dv, n):
            self.move(self.slab(dv), self.p3[n], sibling)

        def p2_forward(self):
            recv(self.slab(-1, 0), self.p2[0]).wait_recv()
            self.move(self.slab(-1, 0), self.p2[4], self.near(0, 1))
            recv(self.slab(1, 1), self.p2[2]).wait_recv()
            self.move(self.slab(1, 1), self.p2[5], self.near(0, -1))

        def p2_mid(self):
            recv(self.slab(-1, 1), self.p2[1]).wait_recv()
            self.p3_send(-1, 1)
            recv(self.slab(1, 0), self.p2[3]).wait_recv()
            self.p3_send(1, 2)

        def p2_finish(self):
            recv(self.slab(2, 0), self.p2[4]).wait_recv()
            recv(self.slab(2, 1), self.p2[5]).wait_recv()
            self.p3_send(2, 3)

        def p3_wait(self, n):
            recv(self.buf.at[1 - core, n], self.p3[n]).wait_recv()

        def rows(self, n):
            step = (0, -1, 1, 2)[n]
            other = self.v if self.stage < 2 else self.u
            mine = self.buf[core, lax.rem(self.v + step + 4, 4)]
            theirs = self.buf[1 - core, lax.rem(other + step + 4, 4)]
            count = 4 * self.slots * 8
            return [mine.reshape(count, RANK), theirs.reshape(count, RANK)]

    def add_gram(out_ref, parts, first):
        size = parts[0].shape[0]
        for n, part in enumerate(parts):
            high, low = split_two(part)
            mh[n * size:(n + 1) * size, :] = high
            ml[n * size:(n + 1) * size, :] = low
        high, low = mh[...], ml[...]
        value = dot_rows(high, high) + dot_rows(high, low) + dot_rows(low, high)
        out_ref[...] = value if first else out_ref[...] + value

    def diagonal(n, value):
        row = lax.broadcasted_iota(jnp.int32, (64, RANK), 0) + n * 64
        col = lax.broadcasted_iota(jnp.int32, (64, RANK), 1)
        return jnp.where(row == col, value, 0.0)

    def normal_gram(ref, count):
        def squares(n, total):
            rs = pl.ds(pl.multiple_of(n * 64, 64), 64)
            return total + jnp.sum(diagonal(n, ref[rs, :]), axis=0, keepdims=True)

        total = lax.fori_loop(0, 8, squares, jnp.zeros((1, RANK), F32))
        inverse = 1.0 / jnp.sqrt(total / count + EPS)

        def body(n, carry):
            rs = pl.ds(pl.multiple_of(n * 64, 64), 64)
            value = ref[rs, :]
            mine = jnp.sum(diagonal(n, value), axis=1, keepdims=True)
            ref[rs, :] = value * (1.0 / jnp.sqrt(mine / count + EPS)) * inverse
            return carry

        lax.fori_loop(0, 8, body, 0)
        return inverse

    def start_chain(one, two):
        def first(n, carry):
            trace, frob = carry
            rs = pl.ds(pl.multiple_of(n * 64, 64), 64)
            value = one[rs, :] * two[rs, :]
            dmat[rs, :] = value
            trace += jnp.sum(diagonal(n, value), axis=0, keepdims=True)
            frob += jnp.sum(value * value, axis=0, keepdims=True)
            return trace, frob

        zero = jnp.zeros((1, RANK), F32)
        trace, frob = lax.fori_loop(0, 8, first, (zero, zero))
        ridge = RIDGE * jnp.sum(trace, axis=1, keepdims=True) / RANK
        top = ridge + jnp.sqrt(jnp.sum(frob, axis=1, keepdims=True))
        scale = 2.0 / (top + ridge)
        sigma = (top + ridge) / (top - ridge)

        def second(n, carry):
            rs = pl.ds(pl.multiple_of(n * 64, 64), 64)
            value = (dmat[rs, :] + diagonal(n, ridge)) * scale
            dmat[rs, :] = value
            high, low = split_two(value)
            dh[0, rs, :] = high
            dl[0, rs, :] = low
            d3[rs, :] = (value - high.astype(F32) - low.astype(F32)).astype(BF16)
            return carry

        lax.fori_loop(0, 8, second, 0)
        factors = []
        for q in range(STEPS):
            twice = 2.0 * sigma * sigma
            factors.append(twice / (twice - 1.0))
            sigma = twice - 1.0
        return scale, factors

    def set_rows(q, value):
        yvec[...] = value
        high, low = split_two(value)
        dh[q, 512:528, :] = jnp.concatenate(
            [high.astype(F32), low.astype(F32)], axis=0
        ).astype(BF16)

    def chain_step(q, factor, with_rows):
        tall = 528 if with_rows else 512
        for n in range(2):
            cs = slice(n * 256, n * 256 + 256)
            high, low = dh[q, 0:tall, :], dl[q]
            right_high, right_low = dh[q, 0:512, cs], dl[q, :, cs]
            one = dot(high, right_high)
            two = dot(high, right_low)
            square = one[0:512] + two[0:512] + dot(low, right_high)
            if q < EXACT_STEPS:
                square += (
                    dot(low, right_low)
                    + dot(dh[q, 0:512, :], d3[:, cs])
                    + dot(d3[...], right_high)
                )
            value = factor * (2.0 * dmat[:, cs] - square)
            dmat[:, cs] = value
            high, low = split_two(value)
            dh[q + 1, 0:512, cs] = high
            dl[q + 1, :, cs] = low
            if with_rows:
                value = one[512:520] + one[520:528] + two[512:520]
                value = factor * (2.0 * yvec[:, cs] - value)
                yvec[:, cs] = value
                high, low = split_two(value)
                dh[q + 1, 512:528, cs] = jnp.concatenate(
                    [high.astype(F32), low.astype(F32)], axis=0
                ).astype(BF16)

    def apply_step(q, factor, value):
        high, low = split_two(value)
        both = jnp.concatenate([high.astype(F32), low.astype(F32)], axis=0).astype(BF16)
        wide = dot(both, dh[q, 0:512, :])
        narrow = dot(both, dl[q])
        return factor * (2.0 * value - (wide[0:8] + wide[8:16] + narrow[0:8]))

    def join(q, rows, scale, factors):
        value = rows * scale
        for n in range(q):
            value = apply_step(n, factors[n], value)
        set_rows(q, value)

    def last_step(factors):
        return apply_step(STEPS - 1, factors[STEPS - 1], yvec[...])

    yvec[...] = jnp.zeros_like(yvec)
    to_sib = remote(own8, sib8, send_sems.at[0], r_sib.at[0], sibling)
    to_sib.start()
    out.used = 1
    out.pending.append((to_sib, None))
    to_sib.wait_recv()
    slot = lax.rem(ia, 2) * 2 + zlo
    contributes = core == half
    all_b = Gather(g_b, 0, 4, slot, contributes, 0)
    all_c = Gather(g_c, 1, 4, slot, contributes, 1)

    for c in range(2):
        @pl.when(jnp.logical_and(contributes, core == c))
        def _():
            for gather, at in ((all_b, 0), (all_c, 4)):
                mine = own8[at:at + 4, :]
                theirs = sib8[at:at + 4, :]
                first, second = (mine, theirs) if c == 0 else (theirs, mine)
                gather.buf[core, gather.v, gather.u, slot, 0:4, :] = first
                gather.buf[core, gather.v, gather.u, slot, 4:8, :] = second

    both = (all_b, all_c)
    for gather in both:
        gather.p0_send()
    for gather in both:
        gather.p0_wait()
        gather.p1_send()
    for gather in both:
        gather.p1_forward()
    for gather in both:
        gather.p1_finish()
        gather.p2_send()
        gather.p3_send(0, 0)

    def fill_c(n, carry):
        pia, rest = n // 8, lax.rem(n, 8)
        px, pzlo = rest // 2, lax.rem(rest, 2)
        ps = lax.rem(pia, 2) * 2 + pzlo
        cblk[pl.ds(pl.multiple_of(n * 8, 8), 8), :] = g_c[pia // 2, y, px, ps]
        return carry

    def fill_b(n, carry):
        pia, py = n // 2, lax.rem(n, 2) * 2
        ps = lax.rem(pia, 2) * 2 + zlo
        one, two = g_b[pia // 2, x, py, ps], g_b[pia // 2, x, py + 1, ps]

        @pl.when(core == 0)
        def _():
            pvec[0:4, :] = one[0:4]
            pvec[4:8, :] = two[0:4]

        @pl.when(core == 1)
        def _():
            pvec[0:4, :] = one[4:8]
            pvec[4:8, :] = two[4:8]

        bblk[pl.ds(pl.multiple_of(n * 8, 8), 8), :] = pvec[...].astype(BF16).astype(F32)
        return carry

    for gather in both:
        gather.p3_wait(0)
    lax.fori_loop(0, 32, fill_c, 0)
    lax.fori_loop(0, 8, fill_b, 0)
    add_gram(gram_b, all_b.rows(0), True)
    for gather in both:
        gather.p2_forward()

    load_t.wait()

    def contract(g, carry):
        half_c = cblk[...].astype(BF16)
        weight = bblk[...]
        parts = []
        for s in range(2):
            piece = t_ref[pl.ds(g * 8 + s * 4, 4)].reshape(256, 256)
            value = dot(piece, half_c).reshape(4, 64, RANK)
            mixed[pl.ds(g * 8 + s * 4, 4)] = value.astype(BF16)
            parts.append(jnp.sum(value * weight[None], axis=1))
        pa[g] = jnp.concatenate(parts, axis=0)
        return carry

    lax.fori_loop(0, 8, contract, 0)
    for gather in both:
        gather.p2_mid()
    lax.fori_loop(8, 16, contract, 0)

    out.send(pa, ra1, r_a.at[0], sibling, core != half)
    for gather in both:
        gather.p2_finish()
    add_gram(gram_c, all_c.rows(0), True)
    for n in (1, 2):
        all_b.p3_wait(n)
        add_gram(gram_b, all_b.rows(n), False)
    a_owner = jnp.logical_and(core == half, lax.rem(x, 2) == zlo)

    @pl.when(core == half)
    def _():
        recv(ra1, r_a.at[0]).wait_recv()
        pa[...] += ra1[...]

    for m in range(2):
        px = 1 - zlo + 2 * m
        out.send(
            pa.at[pl.ds(px * 4, 4)], ra2.at[m], r_a.at[1 + m],
            dev(x, y, ia * 2 + 1 - zlo, core), core == half,
        )
    for n in (1, 2):
        all_c.p3_wait(n)
        add_gram(gram_c, all_c.rows(n), False)

    @pl.when(core == half)
    def _():
        for m in range(2):
            recv(ra2.at[m], r_a.at[1 + m]).wait_recv()
            px = zlo + 2 * m
            pa[pl.ds(px * 4, 4)] += ra2[m]

    for d in (1, 2, 3):
        px = lax.rem(x + d, 4)
        out.send(
            pa.at[pl.ds(px * 4, 4)], ra3.at[d - 1], r_a.at[2 + d], at_x(d),
            jnp.logical_and(core == half, lax.rem(px, 2) == zlo),
        )
    all_b.p3_wait(3)
    add_gram(gram_b, all_b.rows(3), False)
    all_c.p3_wait(3)
    add_gram(gram_c, all_c.rows(3), False)

    @pl.when(a_owner)
    def _():
        for d in (1, 2, 3):
            recv(ra3.at[d - 1], r_a.at[2 + d]).wait_recv()
        pa[pl.ds(x * 4, 4)] += ra3[0] + ra3[1] + ra3[2]

    for d in (1, 2, 3):
        out.send(
            pa.at[x * 4 + lax.rem(y + d, 4)], ra4.at[d - 1], r_a.at[5 + d], at_y(d), a_owner
        )
    scale, factors = start_chain(gram_b, gram_c)
    chain_step(0, factors[0], False)

    @pl.when(a_owner)
    def _():
        for d in (1, 2, 3):
            recv(ra4.at[d - 1], r_a.at[5 + d]).wait_recv()
        rows = pa[x * 4 + y] + ra4[0] + ra4[1] + ra4[2]
        join(1, rows, scale, factors)

    for q in range(1, STEPS - 1):
        chain_step(q, factors[q], True)
    aslot = lax.rem(ia, 2)
    all_a = Gather(ga, 2, 2, aslot, a_owner, sel0)

    @pl.when(a_owner)
    def _():
        ga[core, all_a.v, all_a.u, aslot] = last_step(factors)

    def turn(g, carry):
        tt[g] = t_ref[pl.ds(g * 16, 16)].reshape(1024, 256).T
        return carry

    all_a.p0_send()
    lax.fori_loop(0, 4, turn, 0)
    all_a.p0_wait()
    all_a.p1_send()
    lax.fori_loop(4, 6, turn, 0)
    all_a.p1_forward()
    all_a.p1_finish()
    all_a.p2_send()
    all_a.p3_send(0, 0)
    lax.fori_loop(6, 8, turn, 0)
    all_a.p2_forward()
    all_a.p2_mid()
    all_a.p2_finish()
    all_a.p3_wait(0)
    all_a.p3_wait(1)
    add_gram(gram_a, all_a.rows(0) + all_a.rows(1), True)
    all_a.p3_wait(2)
    all_a.p3_wait(3)
    add_gram(gram_a, all_a.rows(2) + all_a.rows(3), False)
    inverse_a = normal_gram(gram_a, 512)

    def fill_a(n, carry):
        px, py = n // 4, lax.rem(n, 4)
        pu = px * (1 - half) + py * half
        pv = py * (1 - half) + px * half
        ablk[pl.ds(pl.multiple_of(n * 8, 8), 8), :] = ga[half, pv, pu, aslot] * inverse_a
        return carry

    lax.fori_loop(0, 16, fill_a, 0)

    def second_mode(g, total):
        rows = ablk[pl.ds(pl.multiple_of(g * 8, 8), 8), :].astype(BF16).astype(F32)
        for s in range(8):
            total = total + mixed[g * 8 + s].astype(F32) * rows[s:s + 1, :]
        return total

    part_b = lax.fori_loop(0, 16, second_mode, jnp.zeros((64, RANK), F32))
    for o in range(8):
        pb[o % 4, o // 4] = part_b[o * 8:o * 8 + 8]
    for d in (1, 2, 3):
        out.send(pb.at[lax.rem(y + d, 4)], rb1.at[d - 1], r_b.at[d - 1], at_y(d))
    scale, factors = start_chain(gram_a, gram_c)
    chain_step(0, factors[0], False)
    for d in (1, 2, 3):
        recv(rb1.at[d - 1], r_b.at[d - 1]).wait_recv()
    sb[...] = pb[y] + rb1[0] + rb1[1] + rb1[2]
    for d in (1, 2, 3):
        pia = lax.rem(ia + d, 4)
        out.send(
            sb.at[lax.rem(pia, 2)], rb2.at[d - 1], r_b.at[2 + d],
            dev(x, y, pia * 2 + zlo, core), pia // 2 == core,
        )
    own_a = ablk[pl.ds(pl.multiple_of(ja * 8, 8), 8), :]
    for s in range(4):
        @pl.when(ka == s)
        def _():
            a_out[0, 0] = own_a[2 * s:2 * s + 2]

    for q in (1, 2):
        chain_step(q, factors[q], False)

    @pl.when(core == half)
    def _():
        for d in (1, 2, 3):
            recv(rb2.at[d - 1], r_b.at[2 + d]).wait_recv()
        join(3, sb[lax.rem(ia, 2)] + rb2[0] + rb2[1] + rb2[2], scale, factors)

    for q in range(3, STEPS - 1):
        chain_step(q, factors[q], True)
    all_b2 = Gather(gb, 3, 4, slot, contributes, sel0)

    @pl.when(core == half)
    def _():
        gb[core, all_b2.v, all_b2.u, slot] = last_step(factors)

    def repeat_a(g, carry):
        rows = ablk[pl.ds(pl.multiple_of(g * 8, 8), 8), :].astype(BF16).astype(F32)
        for s in range(8):
            arep[g * 8 + s] = jnp.broadcast_to(rows[s:s + 1, :], (16, RANK)).astype(BF16)
        return carry

    all_b2.p0_send()
    lax.fori_loop(0, 16, repeat_a, 0)
    all_b2.p0_wait()
    all_b2.p1_send()
    all_b2.p1_forward()
    all_b2.p1_finish()
    all_b2.p2_send()
    all_b2.p3_send(0, 0)
    all_b2.p2_forward()
    all_b2.p3_wait(0)
    add_gram(gram_b2, all_b2.rows(0), True)
    all_b2.p2_mid()
    all_b2.p2_finish()
    for n in (1, 2, 3):
        all_b2.p3_wait(n)
        add_gram(gram_b2, all_b2.rows(n), False)
    inverse_b = normal_gram(gram_b2, 1024)

    def fill_b2(n, carry):
        py = lax.rem(n, 4)
        pu = x * sel0 + py * core
        pv = py * sel0 + x * core
        rows = gb[core, pv, pu, (n // 4) * 2 + zlo] * inverse_b
        b2blk[pl.ds(pl.multiple_of(n * 8, 8), 8), :] = rows
        return carry

    lax.fori_loop(0, 8, fill_b2, 0)

    pc[...] = jnp.zeros_like(pc)

    def third_mode(g, carry):
        half_b2 = b2blk[...].astype(BF16).reshape(4, 16, RANK)
        weight = jnp.concatenate(
            [(half_b2 * arep[g * 16 + n][None]).reshape(64, RANK) for n in range(16)], axis=0
        )
        pc[...] += dot(tt[g], weight).reshape(4, 4, 2, 8, RANK)
        return carry

    lax.fori_loop(0, 8, third_mode, 0)
    out.send(pc.at[pl.ds(2 * (1 - core), 2)], rc0, r_c.at[0], sibling)
    scale, factors = start_chain(gram_a, gram_b2)
    recv(rc0, r_c.at[0]).wait_recv()
    pc[pl.ds(2 * core, 2)] += rc0[...]
    for d in (1, 2, 3):
        out.send(
            pc.at[pl.ds(2 * core, 2), lax.rem(x + d, 4)], rc1.at[d - 1], r_c.at[d], at_x(d)
        )
    for q in (0, 1):
        chain_step(q, factors[q], False)
    own_b = b2blk[pl.ds(pl.multiple_of((ia * 2 + ka // 2) * 8, 8), 8), :]
    for s in range(2):
        @pl.when(lax.rem(ka, 2) == s)
        def _():
            b_out[0, 0] = own_b[4 * s:4 * s + 4]

    for d in (1, 2, 3):
        recv(rc1.at[d - 1], r_c.at[d]).wait_recv()
    sc[...] = pc[pl.ds(2 * core, 2), x] + rc1[0] + rc1[1] + rc1[2]
    for d in range(1, 8):
        pz = lax.rem(z + d, 8)
        out.send(
            sc.at[lax.rem(pz // 2, 2), lax.rem(pz, 2)], rc2.at[d - 1], r_c.at[3 + d], at_z(d),
            pz // 4 == core,
        )
    chain_step(2, factors[2], False)

    @pl.when(core == half)
    def _():
        for d in range(1, 8):
            recv(rc2.at[d - 1], r_c.at[3 + d]).wait_recv()
        total = sc[lax.rem(ia, 2), zlo]
        for d in range(7):
            total = total + rc2[d]
        tc[...] = total

    out.send(tc, rc3, r_c.at[11], sibling, core == half)
    chain_step(3, factors[3], False)

    @pl.when(core != half)
    def _():
        recv(rc3, r_c.at[11]).wait_recv()
        tc[...] = rc3[...]

    join(4, tc[...], scale, factors)
    for q in range(4, STEPS - 1):
        chain_step(q, factors[q], True)
    raw = last_step(factors)

    sq1[...] = raw * raw
    for d in (1, 2, 3):
        out.send(sq1, rq1.at[d - 1], r_q.at[d - 1], at_x(d))
    for d in (1, 2, 3):
        recv(rq1.at[d - 1], r_q.at[d - 1]).wait_recv()
    sq2[...] = sq1[...] + rq1[0] + rq1[1] + rq1[2]
    for d in (1, 2, 3):
        out.send(sq2, rq2.at[d - 1], r_q.at[2 + d], at_y(d))
    for d in (1, 2, 3):
        recv(rq2.at[d - 1], r_q.at[2 + d]).wait_recv()
    sq3[...] = sq2[...] + rq2[0] + rq2[1] + rq2[2]
    for d in range(1, 8):
        out.send(sq3, rq3.at[d - 1], r_q.at[5 + d], at_z(d))
    for d in range(1, 8):
        recv(rq3.at[d - 1], r_q.at[5 + d]).wait_recv()
    total = sq3[...]
    for d in range(7):
        total = total + rq3[d]
    spread = jnp.sqrt(jnp.sum(total, axis=0, keepdims=True) / 1024 + EPS)
    final = raw / spread
    for s in range(2):
        @pl.when(core == s)
        def _():
            c_out[0, 0] = final[4 * s:4 * s + 4]

    out.finish()


def hand_over(a_ref, b_ref, c_ref, a_out, b_out, c_out):
    a_out[...] = a_ref[...]
    b_out[...] = b_ref[...]
    c_out[...] = c_ref[...]


def shards(tensor, factor_b, factor_c):
    vmem = pltpu.VMEM
    dma = pltpu.SemaphoreType.DMA
    scratch = [
        vmem((128, 64, 256), BF16),
        vmem((8, 256, 1024), BF16),
        vmem((128, 64, RANK), BF16),
        vmem((128, 16, RANK), BF16),
        vmem((8, RANK), F32),
        vmem((8, RANK), F32),
        vmem((2, 4, 4, 4, 8, RANK), F32),
        vmem((2, 4, 4, 4, 8, RANK), F32),
        vmem((2, 4, 4, 2, 8, RANK), F32),
        vmem((2, 4, 4, 4, 8, RANK), F32),
        vmem((16, 8, RANK), F32),
        vmem((4, 2, 8, RANK), F32),
        vmem((4, 4, 2, 8, RANK), F32),
        vmem((16, 8, RANK), F32),
        vmem((2, 4, 8, RANK), F32),
        vmem((3, 4, 8, RANK), F32),
        vmem((3, 8, RANK), F32),
        vmem((3, 2, 8, RANK), F32),
        vmem((2, 8, RANK), F32),
        vmem((3, 8, RANK), F32),
        vmem((2, 4, 2, 8, RANK), F32),
        vmem((3, 2, 2, 8, RANK), F32),
        vmem((2, 2, 8, RANK), F32),
        vmem((7, 8, RANK), F32),
        vmem((8, RANK), F32),
        vmem((8, RANK), F32),
        vmem((3, 8, RANK), F32),
        vmem((3, 8, RANK), F32),
        vmem((7, 8, RANK), F32),
        vmem((8, RANK), F32),
        vmem((8, RANK), F32),
        vmem((8, RANK), F32),
        vmem((256, RANK), BF16),
        vmem((256, RANK), BF16),
        vmem((RANK, RANK), F32),
        vmem((RANK, RANK), F32),
        vmem((RANK, RANK), F32),
        vmem((RANK, RANK), F32),
        vmem((RANK, RANK), F32),
        vmem((STEPS, RANK + 16, RANK), BF16),
        vmem((STEPS, RANK, RANK), BF16),
        vmem((RANK, RANK), BF16),
        vmem((8, RANK), F32),
        vmem((64, RANK), F32),
        vmem((256, RANK), F32),
        vmem((128, RANK), F32),
        vmem((64, RANK), F32),
        vmem((8, RANK), F32),
        dma((144,)),
        dma((1,)),
        dma((4, 4)),
        dma((4, 4)),
        dma((4, 6)),
        dma((4, 4)),
        dma((9,)),
        dma((6,)),
        dma((12,)),
        dma((13,)),
        dma,
    ]
    results = pl.pallas_call(
        kernel,
        out_shape=(
            jax.ShapeDtypeStruct((1, 1, 2, RANK), F32),
            jax.ShapeDtypeStruct((1, 1, 4, RANK), F32),
            jax.ShapeDtypeStruct((1, 1, 4, RANK), F32),
        ),
        in_specs=[
            pl.BlockSpec(memory_space=pl.ANY),
            pl.BlockSpec(memory_space=pltpu.VMEM),
            pl.BlockSpec(memory_space=pltpu.VMEM),
        ],
        out_specs=[pl.BlockSpec(memory_space=pltpu.VMEM)] * 3,
        scratch_shapes=scratch,
        compiler_params=pltpu.CompilerParams(
            collective_id=0, has_side_effects=True, vmem_limit_bytes=58 * 1024 * 1024
        ),
        name="sweep",
    )(tensor, factor_b, factor_c)
    return pl.pallas_call(
        hand_over,
        out_shape=tuple(jax.ShapeDtypeStruct(r.shape, F32) for r in results),
        name="hand_over",
    )(*results)


def solution(mesh):
    in_specs = (
        P("ia", "ja", "ka"),
        P("ja", ("ia", "ka"), None, None),
        P("ka", ("ia", "ja"), None, None),
    )
    out_specs = (
        P("ia", ("ja", "ka"), None, None),
        P("ja", ("ia", "ka"), None, None),
        P("ka", ("ia", "ja"), None, None),
    )
    return jax.shard_map(shards, mesh=mesh, in_specs=in_specs, out_specs=out_specs, check_vma=False)
```

```python
import functools

import jax
import jax.numpy as jnp
from jax import lax
from jax.experimental import pallas as pl
from jax.experimental.pallas import tpu as pltpu
from jax.sharding import PartitionSpec as P

RIDGE = 0.1
EPS = 1e-06
F32 = jnp.float32
BF16 = jnp.bfloat16
RANK = 512
STEPS = 9
EXACT_STEPS = 1


def dot(left, right):
    return jnp.dot(left, right, preferred_element_type=F32)


def dot_rows(left, right):
    return lax.dot_general(left, right, (((0,), (0,)), ((), ())), preferred_element_type=F32)


def split_two(value):
    high = value.astype(BF16)
    low = (value - high.astype(F32)).astype(BF16)
    return high, low


def remote(src, dst, send_sem, recv_sem, device):
    return pltpu.make_async_remote_copy(
        src_ref=src,
        dst_ref=dst,
        send_sem=send_sem,
        recv_sem=recv_sem,
        device_id=device,
        device_id_type=pl.DeviceIdType.MESH,
    )


class Sender:
    def __init__(self, sems):
        self.sems = sems
        self.used = 0
        self.pending = []

    def send(self, src, dst, recv_sem, device, cond=None):
        sem = self.sems.at[self.used]
        self.used += 1
        copy = remote(src, dst, sem, recv_sem, device)
        if cond is None:
            copy.start()
        else:
            pl.when(cond)(copy.start)
        self.pending.append((copy, cond))

    def finish(self):
        for copy, cond in self.pending:
            if cond is None:
                copy.wait_send()
            else:
                pl.when(cond)(copy.wait_send)


def kernel(
    t_hbm, fb_ref, fc_ref, a_out, b_out, c_out,
    t_ref, tt, mixed, arep, own8, sib8, g_b, g_c, ga, gb,
    pa, pb, pc, ra1, ra2, ra3, ra4, rb1, sb, rb2, rc0, rc1, sc, rc2, tc, rc3,
    rq1, rq2, rq3, sq1, sq2, sq3,
    mh, ml, gram_b, gram_c, gram_a, gram_b2, dmat, dh, dl, d3, yvec, xmat, xh, xl, raw_a, raw_b,
    bblk, cblk, ablk, b2blk, pvec,
    send_sems, r_sib, r_p0, r_p1, r_p2, r_p3, r_a, r_b, r_c, r_q, t_sem,
):
    ia = lax.axis_index("ia")
    ja = lax.axis_index("ja")
    ka = lax.axis_index("ka")
    core = lax.rem(ja, 2)
    zlo = lax.rem(ja // 2, 2)
    x = ja // 4
    y = ka
    z = ia * 2 + zlo
    half = ia // 2
    sel0 = 1 - core

    def dev(px, py, pz, pcore):
        return (pz // 2, px * 4 + lax.rem(pz, 2) * 2 + pcore, py)

    sibling = dev(x, y, z, 1 - core)

    def at_x(d):
        return dev(lax.rem(x + d, 4), y, z, core)

    def at_y(d):
        return dev(x, lax.rem(y + d, 4), z, core)

    def at_z(d):
        return dev(x, y, lax.rem(z + d, 8), core)

    load_t = pltpu.make_async_copy(t_hbm, t_ref, t_sem)
    load_t.start()
    out = Sender(send_sems)

    barrier = pltpu.get_barrier_semaphore()
    partners = [sibling]
    partners += [at_x(d) for d in (1, 2, 3)]
    partners += [at_y(d) for d in (1, 2, 3)]
    partners += [at_z(d) for d in range(1, 8)]
    for partner in partners:
        pl.semaphore_signal(
            barrier, inc=1, device_id=partner, device_id_type=pl.DeviceIdType.MESH
        )

    own8[0:4, :] = fb_ref[0, 0]
    own8[4:8, :] = fc_ref[0, 0]
    pl.semaphore_wait(barrier, len(partners))

    def recv(ref, sem):
        return remote(ref, ref, send_sems.at[0], sem, sibling)

    class Gather:
        def __init__(self, buf, stage, slots, slot, contributes, u_is_x):
            self.buf, self.stage, self.slots, self.slot = buf, stage, slots, slot
            self.contributes = contributes
            self.u_is_x = u_is_x
            self.u = x * u_is_x + y * (1 - u_is_x)
            self.v = y * u_is_x + x * (1 - u_is_x)
            self.p0 = [r_p0.at[stage, n] for n in range(slots)]
            self.p1 = [r_p1.at[stage, n] for n in range(3)]
            self.p2 = [r_p2.at[stage, n] for n in range(6)]
            self.p3 = [r_p3.at[stage, n] for n in range(4)]

        def near(self, du, dv):
            pu, pv = lax.rem(self.u + du + 4, 4), lax.rem(self.v + dv + 4, 4)
            keep = self.u_is_x
            return dev(pu * keep + pv * (1 - keep), pv * keep + pu * (1 - keep), z, core)

        def move(self, ref, sem, device):
            out.send(ref, ref, sem, device)

        def chunk(self, du):
            return self.buf.at[core, self.v, lax.rem(self.u + du + 4, 4)]

        def slab(self, dv, first=None):
            pv = lax.rem(self.v + dv + 4, 4)
            if first is None:
                return self.buf.at[core, pv]
            return self.buf.at[core, pv, pl.ds(first * 2, 2)]

        def p0_send(self):
            ref = self.buf.at[core, self.v, self.u, self.slot]
            for d in (4, 3, 5, 2, 6, 1, 7):
                out.send(ref, ref, r_p0.at[self.stage, self.slot], at_z(d), self.contributes)

        def p0_wait(self):
            for s in range(self.slots):
                other = jnp.logical_not(jnp.logical_and(self.contributes, self.slot == s))
                copy = recv(self.buf.at[core, self.v, self.u, s], self.p0[s])
                pl.when(other)(copy.wait_recv)

        def p1_send(self):
            for d in (2, 1, 3):
                self.move(self.chunk(0), self.p1[d - 1], self.near(d, 0))

        def p1_wait(self):
            for d in (1, 3, 2):
                recv(self.chunk(-d), self.p1[d - 1]).wait_recv()

        def p2_send(self):
            self.move(self.slab(0, 0), self.p2[0], self.near(0, 1))
            self.move(self.slab(0, 1), self.p2[2], self.near(0, -1))
            self.move(self.slab(0, 1), self.p2[1], self.near(0, 1))
            self.move(self.slab(0, 0), self.p2[3], self.near(0, -1))

        def p3_send(self, dv, n):
            self.move(self.slab(dv), self.p3[n], sibling)

        def p2_forward(self):
            recv(self.slab(-1, 0), self.p2[0]).wait_recv()
            self.move(self.slab(-1, 0), self.p2[4], self.near(0, 1))
            recv(self.slab(1, 1), self.p2[2]).wait_recv()
            self.move(self.slab(1, 1), self.p2[5], self.near(0, -1))

        def p2_mid(self):
            recv(self.slab(-1, 1), self.p2[1]).wait_recv()
            self.p3_send(-1, 1)
            recv(self.slab(1, 0), self.p2[3]).wait_recv()
            self.p3_send(1, 2)

        def p2_finish(self):
            recv(self.slab(2, 0), self.p2[4]).wait_recv()
            recv(self.slab(2, 1), self.p2[5]).wait_recv()
            self.p3_send(2, 3)

        def p3_wait(self, n):
            recv(self.buf.at[1 - core, n], self.p3[n]).wait_recv()

        def rows(self, n):
            step = (0, -1, 1, 2)[n]
            other = self.v if self.stage < 2 else self.u
            mine = self.buf[core, lax.rem(self.v + step + 4, 4)]
            theirs = self.buf[1 - core, lax.rem(other + step + 4, 4)]
            count = 4 * self.slots * 8
            return [mine.reshape(count, RANK), theirs.reshape(count, RANK)]

    def add_gram(out_ref, parts, first):
        size = parts[0].shape[0]
        for n, part in enumerate(parts):
            high, low = split_two(part)
            mh[n * size:(n + 1) * size, :] = high
            ml[n * size:(n + 1) * size, :] = low
        high, low = mh[...], ml[...]
        value = dot_rows(high, high) + dot_rows(high, low) + dot_rows(low, high)
        out_ref[...] = value if first else out_ref[...] + value

    def diagonal(n, value):
        row = lax.broadcasted_iota(jnp.int32, (64, RANK), 0) + n * 64
        col = lax.broadcasted_iota(jnp.int32, (64, RANK), 1)
        return jnp.where(row == col, value, 0.0)

    def normal_gram(ref, count):
        def squares(n, total):
            rs = pl.ds(pl.multiple_of(n * 64, 64), 64)
            return total + jnp.sum(diagonal(n, ref[rs, :]), axis=0, keepdims=True)

        total = lax.fori_loop(0, 8, squares, jnp.zeros((1, RANK), F32))
        inverse = 1.0 / jnp.sqrt(total / count + EPS)

        def body(n, carry):
            rs = pl.ds(pl.multiple_of(n * 64, 64), 64)
            value = ref[rs, :]
            mine = jnp.sum(diagonal(n, value), axis=1, keepdims=True)
            ref[rs, :] = value * (1.0 / jnp.sqrt(mine / count + EPS)) * inverse
            return carry

        lax.fori_loop(0, 8, body, 0)
        return inverse

    def start_chain(one, two):
        def first(n, carry):
            trace, frob = carry
            rs = pl.ds(pl.multiple_of(n * 64, 64), 64)
            value = one[rs, :] * two[rs, :]
            dmat[rs, :] = value
            trace += jnp.sum(diagonal(n, value), axis=0, keepdims=True)
            frob += jnp.sum(value * value, axis=0, keepdims=True)
            return trace, frob

        zero = jnp.zeros((1, RANK), F32)
        trace, frob = lax.fori_loop(0, 8, first, (zero, zero))
        ridge = RIDGE * jnp.sum(trace, axis=1, keepdims=True) / RANK
        top = ridge + jnp.sqrt(jnp.sum(frob, axis=1, keepdims=True))
        scale = 2.0 / (top + ridge)
        sigma = (top + ridge) / (top - ridge)

        def second(n, carry):
            rs = pl.ds(pl.multiple_of(n * 64, 64), 64)
            value = (dmat[rs, :] + diagonal(n, ridge)) * scale
            dmat[rs, :] = value
            high, low = split_two(value)
            dh[0, rs, :] = high
            dl[0, rs, :] = low
            d3[rs, :] = (value - high.astype(F32) - low.astype(F32)).astype(BF16)
            return carry

        lax.fori_loop(0, 8, second, 0)
        factors = []
        for q in range(STEPS):
            twice = 2.0 * sigma * sigma
            factors.append(twice / (twice - 1.0))
            sigma = twice - 1.0
        return scale, factors

    def set_rows(q, value):
        yvec[...] = value
        high, low = split_two(value)
        dh[q, 512:528, :] = jnp.concatenate(
            [high.astype(F32), low.astype(F32)], axis=0
        ).astype(BF16)

    def chain_step(q, factor, with_rows):
        tall = 528 if with_rows else 512
        for n in range(2):
            cs = slice(n * 256, n * 256 + 256)
            high, low = dh[q, 0:tall, :], dl[q]
            right_high, right_low = dh[q, 0:512, cs], dl[q, :, cs]
            one = dot(high, right_high)
            two = dot(high, right_low)
            square = one[0:512] + two[0:512] + dot(low, right_high)
            if q < EXACT_STEPS:
                square += (
                    dot(low, right_low)
                    + dot(dh[q, 0:512, :], d3[:, cs])
                    + dot(d3[...], right_high)
                )
            value = factor * (2.0 * dmat[:, cs] - square)
            dmat[:, cs] = value
            high, low = split_two(value)
            dh[q + 1, 0:512, cs] = high
            dl[q + 1, :, cs] = low
            if with_rows:
                value = one[512:520] + one[520:528] + two[512:520]
                value = factor * (2.0 * yvec[:, cs] - value)
                yvec[:, cs] = value
                high, low = split_two(value)
                dh[q + 1, 512:528, cs] = jnp.concatenate(
                    [high.astype(F32), low.astype(F32)], axis=0
                ).astype(BF16)

    def start_inverse(scale, factor):
        def body(n, carry):
            rs = pl.ds(pl.multiple_of(n * 64, 64), 64)
            value = (diagonal(n, 2.0) - dmat[rs, :]) * (scale * factor)
            xmat[rs, :] = value
            high, low = split_two(value)
            xh[1, rs, :] = high
            xl[1, rs, :] = low
            return carry

        lax.fori_loop(0, 8, body, 0)

    def inverse_step(q, factor):
        now, later = q % 2, (q + 1) % 2
        for n in range(2):
            cs = slice(n * 256, n * 256 + 256)
            right_high, right_low = dh[q, 0:512, cs], dl[q, :, cs]
            value = dot(xh[now], right_high) + dot(xh[now], right_low) + dot(xl[now], right_high)
            value = factor * (2.0 * xmat[:, cs] - value)
            xmat[:, cs] = value
            high, low = split_two(value)
            xh[later, :, cs] = high
            xl[later, :, cs] = low

    def times_inverse(rows):
        high, low = split_two(rows)
        last = STEPS % 2
        return dot(high, xh[last]) + dot(high, xl[last]) + dot(low, xh[last])

    def both_steps(q, factors):
        inverse_step(q, factors[q])
        if q < STEPS - 1:
            chain_step(q, factors[q], False)

    def apply_step(q, factor, value):
        high, low = split_two(value)
        both = jnp.concatenate([high.astype(F32), low.astype(F32)], axis=0).astype(BF16)
        wide = dot(both, dh[q, 0:512, :])
        narrow = dot(both, dl[q])
        return factor * (2.0 * value - (wide[0:8] + wide[8:16] + narrow[0:8]))

    def join(q, rows, scale, factors):
        value = rows * scale
        for n in range(q):
            value = apply_step(n, factors[n], value)
        set_rows(q, value)

    def last_step(factors):
        return apply_step(STEPS - 1, factors[STEPS - 1], yvec[...])

    yvec[...] = jnp.zeros_like(yvec)
    to_sib = remote(own8, sib8, send_sems.at[0], r_sib.at[0], sibling)
    to_sib.start()
    out.used = 1
    out.pending.append((to_sib, None))
    to_sib.wait_recv()
    slot = lax.rem(ia, 2) * 2 + zlo
    contributes = core == half
    all_b = Gather(g_b, 0, 4, slot, contributes, 0)
    all_c = Gather(g_c, 1, 4, slot, contributes, 1)

    for c in range(2):
        @pl.when(jnp.logical_and(contributes, core == c))
        def _():
            for gather, at in ((all_b, 0), (all_c, 4)):
                mine = own8[at:at + 4, :]
                theirs = sib8[at:at + 4, :]
                first, second = (mine, theirs) if c == 0 else (theirs, mine)
                gather.buf[core, gather.v, gather.u, slot, 0:4, :] = first
                gather.buf[core, gather.v, gather.u, slot, 4:8, :] = second

    both = (all_b, all_c)

    def turn(g, carry):
        tt[g] = t_ref[pl.ds(g * 16, 16)].reshape(1024, 256).T
        return carry

    for gather in both:
        gather.p0_send()
    load_t.wait()
    lax.fori_loop(0, 4, turn, 0)
    for gather in both:
        gather.p0_wait()
        gather.p1_send()
    lax.fori_loop(4, 8, turn, 0)
    for gather in both:
        gather.p1_wait()
        gather.p2_send()
        gather.p3_send(0, 0)

    def fill_c(n, carry):
        pia, rest = n // 8, lax.rem(n, 8)
        px, pzlo = rest // 2, lax.rem(rest, 2)
        ps = lax.rem(pia, 2) * 2 + pzlo
        cblk[pl.ds(pl.multiple_of(n * 8, 8), 8), :] = g_c[pia // 2, y, px, ps]
        return carry

    def fill_b(n, carry):
        pia, py = n // 2, lax.rem(n, 2) * 2
        ps = lax.rem(pia, 2) * 2 + zlo
        one, two = g_b[pia // 2, x, py, ps], g_b[pia // 2, x, py + 1, ps]

        @pl.when(core == 0)
        def _():
            pvec[0:4, :] = one[0:4]
            pvec[4:8, :] = two[0:4]

        @pl.when(core == 1)
        def _():
            pvec[0:4, :] = one[4:8]
            pvec[4:8, :] = two[4:8]

        bblk[pl.ds(pl.multiple_of(n * 8, 8), 8), :] = pvec[...].astype(BF16).astype(F32)
        return carry

    for gather in both:
        gather.p3_wait(0)
    lax.fori_loop(0, 32, fill_c, 0)
    lax.fori_loop(0, 8, fill_b, 0)

    def contract(g, carry):
        half_c = cblk[...].astype(BF16)
        weight = bblk[...]
        parts = []
        for s in range(2):
            piece = t_ref[pl.ds(g * 8 + s * 4, 4)].reshape(256, 256)
            value = dot(piece, half_c).reshape(4, 64, RANK)
            mixed[pl.ds(g * 8 + s * 4, 4)] = value.astype(BF16)
            parts.append(jnp.sum(value * weight[None], axis=1))
        pa[g] = jnp.concatenate(parts, axis=0)
        return carry

    lax.fori_loop(0, 4, contract, 0)
    for gather in both:
        gather.p2_forward()
    lax.fori_loop(4, 10, contract, 0)
    for gather in both:
        gather.p2_mid()
    lax.fori_loop(10, 16, contract, 0)

    out.send(pa, ra1, r_a.at[0], sibling, core != half)
    a_owner = jnp.logical_and(core == half, lax.rem(x, 2) == zlo)
    add_gram(gram_b, all_b.rows(0), True)
    add_gram(gram_c, all_c.rows(0), True)
    for gather in both:
        gather.p2_finish()

    @pl.when(core == half)
    def _():
        recv(ra1, r_a.at[0]).wait_recv()
        pa[...] += ra1[...]

    for m in range(2):
        px = 1 - zlo + 2 * m
        out.send(
            pa.at[pl.ds(px * 4, 4)], ra2.at[m], r_a.at[1 + m],
            dev(x, y, ia * 2 + 1 - zlo, core), core == half,
        )
    all_b.p3_wait(1)
    add_gram(gram_b, all_b.rows(1), False)
    all_c.p3_wait(1)
    add_gram(gram_c, all_c.rows(1), False)

    @pl.when(core == half)
    def _():
        for m in range(2):
            recv(ra2.at[m], r_a.at[1 + m]).wait_recv()
            px = zlo + 2 * m
            pa[pl.ds(px * 4, 4)] += ra2[m]

    for d in (1, 2, 3):
        px = lax.rem(x + d, 4)
        out.send(
            pa.at[pl.ds(px * 4, 4)], ra3.at[d - 1], r_a.at[2 + d], at_x(d),
            jnp.logical_and(core == half, lax.rem(px, 2) == zlo),
        )
    all_b.p3_wait(2)
    add_gram(gram_b, all_b.rows(2), False)
    all_c.p3_wait(2)
    add_gram(gram_c, all_c.rows(2), False)

    @pl.when(a_owner)
    def _():
        for d in (1, 2, 3):
            recv(ra3.at[d - 1], r_a.at[2 + d]).wait_recv()
        pa[pl.ds(x * 4, 4)] += ra3[0] + ra3[1] + ra3[2]

    for d in (1, 2, 3):
        out.send(
            pa.at[x * 4 + lax.rem(y + d, 4)], ra4.at[d - 1], r_a.at[5 + d], at_y(d), a_owner
        )
    all_b.p3_wait(3)
    add_gram(gram_b, all_b.rows(3), False)
    all_c.p3_wait(3)
    add_gram(gram_c, all_c.rows(3), False)
    aslot = lax.rem(ia, 2)
    all_a = Gather(ga, 2, 2, aslot, a_owner, sel0)

    @pl.when(a_owner)
    def _():
        for d in (1, 2, 3):
            recv(ra4.at[d - 1], r_a.at[5 + d]).wait_recv()
        ga[core, all_a.v, all_a.u, aslot] = pa[x * 4 + y] + ra4[0] + ra4[1] + ra4[2]

    def invert(one, two, gather):
        scale, factors = start_chain(one, two)
        start_inverse(scale, factors[0])
        chain_step(0, factors[0], False)
        gather.p0_wait()
        gather.p1_send()
        both_steps(1, factors)
        gather.p1_wait()
        gather.p2_send()
        gather.p3_send(0, 0)
        both_steps(2, factors)
        gather.p2_forward()
        both_steps(3, factors)
        gather.p2_mid()
        both_steps(4, factors)
        gather.p2_finish()
        for q in range(5, STEPS):
            both_steps(q, factors)
        for n in range(4):
            gather.p3_wait(n)

    all_a.p0_send()
    invert(gram_b, gram_c, all_a)
    for n in range(2):
        raw_a[n] = times_inverse(ga[n].reshape(256, RANK)).reshape(4, 4, 2, 8, RANK)

    def fill_a(n, carry):
        px, py = n // 4, lax.rem(n, 4)
        pu = px * (1 - half) + py * half
        pv = py * (1 - half) + px * half
        ablk[pl.ds(pl.multiple_of(n * 8, 8), 8), :] = raw_a[half, pv, pu, aslot]
        return carry

    lax.fori_loop(0, 16, fill_a, 0)

    def second_mode(g, total):
        rows = ablk[pl.ds(pl.multiple_of(g * 8, 8), 8), :].astype(BF16).astype(F32)
        for s in range(8):
            total = total + mixed[g * 8 + s].astype(F32) * rows[s:s + 1, :]
        return total

    part_b = lax.fori_loop(0, 16, second_mode, jnp.zeros((64, RANK), F32))
    for o in range(8):
        pb[o % 4, o // 4] = part_b[o * 8:o * 8 + 8]
    for d in (1, 2, 3):
        out.send(pb.at[lax.rem(y + d, 4)], rb1.at[d - 1], r_b.at[d - 1], at_y(d))
    for n in range(2):
        add_gram(gram_a, [raw_a[n].reshape(256, RANK)], n == 0)
    for d in (1, 2, 3):
        recv(rb1.at[d - 1], r_b.at[d - 1]).wait_recv()
    sb[...] = pb[y] + rb1[0] + rb1[1] + rb1[2]
    for d in (1, 2, 3):
        pia = lax.rem(ia + d, 4)
        out.send(
            sb.at[lax.rem(pia, 2)], rb2.at[d - 1], r_b.at[2 + d],
            dev(x, y, pia * 2 + zlo, core), pia // 2 == core,
        )
    inverse_a = normal_gram(gram_a, 512)

    def repeat_a(g, carry):
        rows = ablk[pl.ds(pl.multiple_of(g * 8, 8), 8), :].astype(BF16).astype(F32)
        for s in range(8):
            arep[g * 8 + s] = jnp.broadcast_to(rows[s:s + 1, :], (16, RANK)).astype(BF16)
        return carry

    lax.fori_loop(0, 16, repeat_a, 0)
    own_a = ablk[pl.ds(pl.multiple_of(ja * 8, 8), 8), :] * inverse_a
    for s in range(4):
        @pl.when(ka == s)
        def _():
            a_out[0, 0] = own_a[2 * s:2 * s + 2]

    all_b2 = Gather(gb, 3, 4, slot, contributes, sel0)

    @pl.when(core == half)
    def _():
        for d in (1, 2, 3):
            recv(rb2.at[d - 1], r_b.at[2 + d]).wait_recv()
        rows = sb[lax.rem(ia, 2)] + rb2[0] + rb2[1] + rb2[2]
        gb[core, all_b2.v, all_b2.u, slot] = rows * inverse_a

    all_b2.p0_send()
    invert(gram_a, gram_c, all_b2)

    def fill_b2(n, carry):
        py = lax.rem(n, 4)
        pu = x * sel0 + py * core
        pv = py * sel0 + x * core
        rows = gb[core, pv, pu, (n // 4) * 2 + zlo]
        b2blk[pl.ds(pl.multiple_of(n * 8, 8), 8), :] = rows
        return carry

    lax.fori_loop(0, 8, fill_b2, 0)
    b2blk[...] = times_inverse(b2blk[...])

    pc[...] = jnp.zeros_like(pc)

    def third_mode(g, carry):
        half_b2 = b2blk[...].astype(BF16).reshape(4, 16, RANK)
        weight = jnp.concatenate(
            [(half_b2 * arep[g * 16 + n][None]).reshape(64, RANK) for n in range(16)], axis=0
        )
        pc[...] += dot(tt[g], weight).reshape(4, 4, 2, 8, RANK)
        return carry

    lax.fori_loop(0, 8, third_mode, 0)
    out.send(pc.at[pl.ds(2 * (1 - core), 2)], rc0, r_c.at[0], sibling)

    def all_rows(n, carry):
        h, pair = n // 2, lax.rem(n, 2) * 2
        rows = times_inverse(gb[h, pl.ds(pair, 2)].reshape(256, RANK))
        high, low = split_two(rows)
        mh[...] = high
        ml[...] = low
        high, low = mh[...], ml[...]
        gram_b2[...] += dot_rows(high, high) + dot_rows(high, low) + dot_rows(low, high)
        return carry

    gram_b2[...] = jnp.zeros_like(gram_b2)
    lax.fori_loop(0, 2, all_rows, 0)
    recv(rc0, r_c.at[0]).wait_recv()
    pc[pl.ds(2 * core, 2)] += rc0[...]
    for d in (1, 2, 3):
        out.send(
            pc.at[pl.ds(2 * core, 2), lax.rem(x + d, 4)], rc1.at[d - 1], r_c.at[d], at_x(d)
        )
    lax.fori_loop(2, 4, all_rows, 0)
    inverse_b = normal_gram(gram_b2, 1024)
    own_b = b2blk[pl.ds(pl.multiple_of((ia * 2 + ka // 2) * 8, 8), 8), :] * inverse_b
    for s in range(2):
        @pl.when(lax.rem(ka, 2) == s)
        def _():
            b_out[0, 0] = own_b[4 * s:4 * s + 4]

    scale, factors = start_chain(gram_a, gram_b2)
    chain_step(0, factors[0], False)
    for d in (1, 2, 3):
        recv(rc1.at[d - 1], r_c.at[d]).wait_recv()
    sc[...] = pc[pl.ds(2 * core, 2), x] + rc1[0] + rc1[1] + rc1[2]
    for d in range(1, 8):
        pz = lax.rem(z + d, 8)
        out.send(
            sc.at[lax.rem(pz // 2, 2), lax.rem(pz, 2)], rc2.at[d - 1], r_c.at[3 + d], at_z(d),
            pz // 4 == core,
        )
    for q in (1, 2):
        chain_step(q, factors[q], False)

    @pl.when(core == half)
    def _():
        for d in range(1, 8):
            recv(rc2.at[d - 1], r_c.at[3 + d]).wait_recv()
        total = sc[lax.rem(ia, 2), zlo]
        for d in range(7):
            total = total + rc2[d]
        tc[...] = total

    out.send(tc, rc3, r_c.at[11], sibling, core == half)
    chain_step(3, factors[3], False)

    @pl.when(core != half)
    def _():
        recv(rc3, r_c.at[11]).wait_recv()
        tc[...] = rc3[...]

    join(4, tc[...] * (inverse_a * inverse_b), scale, factors)
    for q in range(4, STEPS - 1):
        chain_step(q, factors[q], True)
    raw = last_step(factors)

    sq1[...] = raw * raw
    for d in (1, 2, 3):
        out.send(sq1, rq1.at[d - 1], r_q.at[d - 1], at_x(d))
    for d in (1, 2, 3):
        recv(rq1.at[d - 1], r_q.at[d - 1]).wait_recv()
    sq2[...] = sq1[...] + rq1[0] + rq1[1] + rq1[2]
    for d in (1, 2, 3):
        out.send(sq2, rq2.at[d - 1], r_q.at[2 + d], at_y(d))
    for d in (1, 2, 3):
        recv(rq2.at[d - 1], r_q.at[2 + d]).wait_recv()
    sq3[...] = sq2[...] + rq2[0] + rq2[1] + rq2[2]
    for d in range(1, 8):
        out.send(sq3, rq3.at[d - 1], r_q.at[5 + d], at_z(d))
    for d in range(1, 8):
        recv(rq3.at[d - 1], r_q.at[5 + d]).wait_recv()
    total = sq3[...]
    for d in range(7):
        total = total + rq3[d]
    spread = jnp.sqrt(jnp.sum(total, axis=0, keepdims=True) / 1024 + EPS)
    final = raw / spread
    for s in range(2):
        @pl.when(core == s)
        def _():
            c_out[0, 0] = final[4 * s:4 * s + 4]

    out.finish()


def hand_over(a_ref, b_ref, c_ref, a_out, b_out, c_out):
    a_out[...] = a_ref[...]
    b_out[...] = b_ref[...]
    c_out[...] = c_ref[...]


def shards(tensor, factor_b, factor_c):
    vmem = pltpu.VMEM
    dma = pltpu.SemaphoreType.DMA
    scratch = [
        vmem((128, 64, 256), BF16),
        vmem((8, 256, 1024), BF16),
        vmem((128, 64, RANK), BF16),
        vmem((128, 16, RANK), BF16),
        vmem((8, RANK), F32),
        vmem((8, RANK), F32),
        vmem((2, 4, 4, 4, 8, RANK), F32),
        vmem((2, 4, 4, 4, 8, RANK), F32),
        vmem((2, 4, 4, 2, 8, RANK), F32),
        vmem((2, 4, 4, 4, 8, RANK), F32),
        vmem((16, 8, RANK), F32),
        vmem((4, 2, 8, RANK), F32),
        vmem((4, 4, 2, 8, RANK), F32),
        vmem((16, 8, RANK), F32),
        vmem((2, 4, 8, RANK), F32),
        vmem((3, 4, 8, RANK), F32),
        vmem((3, 8, RANK), F32),
        vmem((3, 2, 8, RANK), F32),
        vmem((2, 8, RANK), F32),
        vmem((3, 8, RANK), F32),
        vmem((2, 4, 2, 8, RANK), F32),
        vmem((3, 2, 2, 8, RANK), F32),
        vmem((2, 2, 8, RANK), F32),
        vmem((7, 8, RANK), F32),
        vmem((8, RANK), F32),
        vmem((8, RANK), F32),
        vmem((3, 8, RANK), F32),
        vmem((3, 8, RANK), F32),
        vmem((7, 8, RANK), F32),
        vmem((8, RANK), F32),
        vmem((8, RANK), F32),
        vmem((8, RANK), F32),
        vmem((256, RANK), BF16),
        vmem((256, RANK), BF16),
        vmem((RANK, RANK), F32),
        vmem((RANK, RANK), F32),
        vmem((RANK, RANK), F32),
        vmem((RANK, RANK), F32),
        vmem((RANK, RANK), F32),
        vmem((STEPS, RANK + 16, RANK), BF16),
        vmem((STEPS, RANK, RANK), BF16),
        vmem((RANK, RANK), BF16),
        vmem((8, RANK), F32),
        vmem((RANK, RANK), F32),
        vmem((2, RANK, RANK), BF16),
        vmem((2, RANK, RANK), BF16),
        vmem((2, 4, 4, 2, 8, RANK), F32),
        vmem((2, 4, 4, 4, 8, RANK), F32),
        vmem((64, RANK), F32),
        vmem((256, RANK), F32),
        vmem((128, RANK), F32),
        vmem((64, RANK), F32),
        vmem((8, RANK), F32),
        dma((144,)),
        dma((1,)),
        dma((4, 4)),
        dma((4, 3)),
        dma((4, 6)),
        dma((4, 4)),
        dma((9,)),
        dma((6,)),
        dma((12,)),
        dma((13,)),
        dma,
    ]
    results = pl.pallas_call(
        kernel,
        out_shape=(
            jax.ShapeDtypeStruct((1, 1, 2, RANK), F32),
            jax.ShapeDtypeStruct((1, 1, 4, RANK), F32),
            jax.ShapeDtypeStruct((1, 1, 4, RANK), F32),
        ),
        in_specs=[
            pl.BlockSpec(memory_space=pl.ANY),
            pl.BlockSpec(memory_space=pltpu.VMEM),
            pl.BlockSpec(memory_space=pltpu.VMEM),
        ],
        out_specs=[pl.BlockSpec(memory_space=pltpu.VMEM)] * 3,
        scratch_shapes=scratch,
        compiler_params=pltpu.CompilerParams(
            collective_id=0, has_side_effects=True, vmem_limit_bytes=58 * 1024 * 1024
        ),
        name="sweep",
    )(tensor, factor_b, factor_c)
    return pl.pallas_call(
        hand_over,
        out_shape=tuple(jax.ShapeDtypeStruct(r.shape, F32) for r in results),
        name="hand_over",
    )(*results)


def solution(mesh):
    in_specs = (
        P("ia", "ja", "ka"),
        P("ja", ("ia", "ka"), None, None),
        P("ka", ("ia", "ja"), None, None),
    )
    out_specs = (
        P("ia", ("ja", "ka"), None, None),
        P("ja", ("ia", "ka"), None, None),
        P("ka", ("ia", "ja"), None, None),
    )
    return jax.shard_map(shards, mesh=mesh, in_specs=in_specs, out_specs=out_specs, check_vma=False)
```

```python
import functools

import jax
import jax.numpy as jnp
from jax import lax
from jax.experimental import pallas as pl
from jax.experimental.pallas import tpu as pltpu
from jax.sharding import PartitionSpec as P

RIDGE = 0.1
EPS = 1e-06
F32 = jnp.float32
BF16 = jnp.bfloat16
RANK = 512
STEPS = 9
EXACT_STEPS = 1


def dot(left, right):
    return jnp.dot(left, right, preferred_element_type=F32)


def dot_rows(left, right):
    return lax.dot_general(left, right, (((0,), (0,)), ((), ())), preferred_element_type=F32)


def split_two(value):
    high = value.astype(BF16)
    low = (value - high.astype(F32)).astype(BF16)
    return high, low


def remote(src, dst, send_sem, recv_sem, device):
    return pltpu.make_async_remote_copy(
        src_ref=src,
        dst_ref=dst,
        send_sem=send_sem,
        recv_sem=recv_sem,
        device_id=device,
        device_id_type=pl.DeviceIdType.MESH,
    )


class Sender:
    def __init__(self, sems):
        self.sems = sems
        self.used = 0
        self.pending = []

    def send(self, src, dst, recv_sem, device, cond=None):
        sem = self.sems.at[self.used]
        self.used += 1
        copy = remote(src, dst, sem, recv_sem, device)
        if cond is None:
            copy.start()
        else:
            pl.when(cond)(copy.start)
        self.pending.append((copy, cond))

    def finish(self):
        for copy, cond in self.pending:
            if cond is None:
                copy.wait_send()
            else:
                pl.when(cond)(copy.wait_send)


def kernel(
    t_hbm, fb_ref, fc_ref, a_out, b_out, c_out,
    t_ref, tt, mixed, arep, own8, sib8, g_b, g_c, ga, gb,
    pa, pb, pc, ra1, ra2, rb1, rc0, rc1, sc, rc2, tc,
    rq1, rq3, sq1, sq3,
    mh, ml, gram_b, gram_c, gram_a, gram_b2, dmat, dh, dl, d3, yvec, xmat, xh, xl, raw_a, raw_b,
    bblk, cblk, ablk, b2blk, pvec,
    send_sems, r_sib, r_p0, r_p1, r_p2, r_p3, r_a, r_b, r_c, r_q, t_sem,
):
    ia = lax.axis_index("ia")
    ja = lax.axis_index("ja")
    ka = lax.axis_index("ka")
    core = lax.rem(ja, 2)
    zlo = lax.rem(ja // 2, 2)
    x = ja // 4
    y = ka
    z = ia * 2 + zlo
    half = ia // 2
    sel0 = 1 - core

    def dev(px, py, pz, pcore):
        return (pz // 2, px * 4 + lax.rem(pz, 2) * 2 + pcore, py)

    sibling = dev(x, y, z, 1 - core)

    def at_x(d):
        return dev(lax.rem(x + d, 4), y, z, core)

    def at_xy(n):
        return dev(lax.rem(x + n // 4, 4), lax.rem(y + n % 4, 4), z, core)

    def at_iy(n):
        return dev(x, lax.rem(y + n % 4, 4), lax.rem(ia + n // 4, 4) * 2 + zlo, core)

    def at_z(d):
        return dev(x, y, lax.rem(z + d, 8), core)

    load_t = pltpu.make_async_copy(t_hbm, t_ref, t_sem)
    load_t.start()
    out = Sender(send_sems)

    barrier = pltpu.get_barrier_semaphore()
    partners = [sibling]
    partners += [at_xy(n) for n in range(1, 16)]
    partners += [at_z(d) for d in range(1, 8)]
    partners += [dev(x, y, lax.rem(z + d, 8), 1 - core) for d in range(1, 8)]
    partners += [at_iy(n) for n in range(1, 16) if n // 4 and n % 4]
    for partner in partners:
        pl.semaphore_signal(
            barrier, inc=1, device_id=partner, device_id_type=pl.DeviceIdType.MESH
        )

    own8[0:4, :] = fb_ref[0, 0]
    own8[4:8, :] = fc_ref[0, 0]
    pl.semaphore_wait(barrier, len(partners))

    def recv(ref, sem):
        return remote(ref, ref, send_sems.at[0], sem, sibling)

    class Gather:
        def __init__(self, buf, stage, slots, slot, contributes, u_is_x):
            self.buf, self.stage, self.slots, self.slot = buf, stage, slots, slot
            self.contributes = contributes
            self.u_is_x = u_is_x
            self.u = x * u_is_x + y * (1 - u_is_x)
            self.v = y * u_is_x + x * (1 - u_is_x)
            self.p0 = [r_p0.at[stage, n] for n in range(slots)]
            self.p1 = [r_p1.at[stage, n] for n in range(3)]
            self.p2 = [r_p2.at[stage, n] for n in range(6)]
            self.p3 = [r_p3.at[stage, n] for n in range(4)]

        def near(self, du, dv):
            pu, pv = lax.rem(self.u + du + 4, 4), lax.rem(self.v + dv + 4, 4)
            keep = self.u_is_x
            return dev(pu * keep + pv * (1 - keep), pv * keep + pu * (1 - keep), z, core)

        def move(self, ref, sem, device):
            out.send(ref, ref, sem, device)

        def chunk(self, du):
            return self.buf.at[core, self.v, lax.rem(self.u + du + 4, 4)]

        def slab(self, dv, first=None):
            pv = lax.rem(self.v + dv + 4, 4)
            if first is None:
                return self.buf.at[core, pv]
            return self.buf.at[core, pv, pl.ds(first * 2, 2)]

        def p0_send(self):
            ref = self.buf.at[core, self.v, self.u, self.slot]
            for d in (4, 3, 5, 2, 6, 1, 7):
                out.send(ref, ref, r_p0.at[self.stage, self.slot], at_z(d), self.contributes)

        def p0_wait(self):
            for s in range(self.slots):
                other = jnp.logical_not(jnp.logical_and(self.contributes, self.slot == s))
                copy = recv(self.buf.at[core, self.v, self.u, s], self.p0[s])
                pl.when(other)(copy.wait_recv)

        def p1_send(self):
            for d in (2, 1, 3):
                self.move(self.chunk(0), self.p1[d - 1], self.near(d, 0))

        def p1_wait(self):
            for d in (1, 3, 2):
                recv(self.chunk(-d), self.p1[d - 1]).wait_recv()

        def p2_send(self):
            self.move(self.slab(0, 0), self.p2[0], self.near(0, 1))
            self.move(self.slab(0, 1), self.p2[2], self.near(0, -1))
            self.move(self.slab(0, 1), self.p2[1], self.near(0, 1))
            self.move(self.slab(0, 0), self.p2[3], self.near(0, -1))

        def p3_send(self, dv, n):
            self.move(self.slab(dv), self.p3[n], sibling)

        def p2_forward(self):
            recv(self.slab(-1, 0), self.p2[0]).wait_recv()
            self.move(self.slab(-1, 0), self.p2[4], self.near(0, 1))
            recv(self.slab(1, 1), self.p2[2]).wait_recv()
            self.move(self.slab(1, 1), self.p2[5], self.near(0, -1))

        def p2_mid(self):
            recv(self.slab(-1, 1), self.p2[1]).wait_recv()
            self.p3_send(-1, 1)
            recv(self.slab(1, 0), self.p2[3]).wait_recv()
            self.p3_send(1, 2)

        def p2_finish(self):
            recv(self.slab(2, 0), self.p2[4]).wait_recv()
            recv(self.slab(2, 1), self.p2[5]).wait_recv()
            self.p3_send(2, 3)

        def p3_wait(self, n):
            recv(self.buf.at[1 - core, n], self.p3[n]).wait_recv()

        def rows(self, n):
            step = (0, -1, 1, 2)[n]
            other = self.v if self.stage < 2 else self.u
            mine = self.buf[core, lax.rem(self.v + step + 4, 4)]
            theirs = self.buf[1 - core, lax.rem(other + step + 4, 4)]
            count = 4 * self.slots * 8
            return [mine.reshape(count, RANK), theirs.reshape(count, RANK)]

    def add_gram(out_ref, parts, first):
        size = parts[0].shape[0]
        for n, part in enumerate(parts):
            high, low = split_two(part)
            mh[n * size:(n + 1) * size, :] = high
            ml[n * size:(n + 1) * size, :] = low
        high, low = mh[...], ml[...]
        value = dot_rows(high, high) + dot_rows(high, low) + dot_rows(low, high)
        out_ref[...] = value if first else out_ref[...] + value

    def diagonal(n, value):
        row = lax.broadcasted_iota(jnp.int32, (64, RANK), 0) + n * 64
        col = lax.broadcasted_iota(jnp.int32, (64, RANK), 1)
        return jnp.where(row == col, value, 0.0)

    def normal_gram(ref, count):
        def squares(n, total):
            rs = pl.ds(pl.multiple_of(n * 64, 64), 64)
            return total + jnp.sum(diagonal(n, ref[rs, :]), axis=0, keepdims=True)

        total = lax.fori_loop(0, 8, squares, jnp.zeros((1, RANK), F32))
        inverse = 1.0 / jnp.sqrt(total / count + EPS)

        def body(n, carry):
            rs = pl.ds(pl.multiple_of(n * 64, 64), 64)
            value = ref[rs, :]
            mine = jnp.sum(diagonal(n, value), axis=1, keepdims=True)
            ref[rs, :] = value * (1.0 / jnp.sqrt(mine / count + EPS)) * inverse
            return carry

        lax.fori_loop(0, 8, body, 0)
        return inverse

    def start_chain(one, two):
        def first(n, carry):
            trace, frob = carry
            rs = pl.ds(pl.multiple_of(n * 64, 64), 64)
            value = one[rs, :] * two[rs, :]
            dmat[rs, :] = value
            trace += jnp.sum(diagonal(n, value), axis=0, keepdims=True)
            frob += jnp.sum(value * value, axis=0, keepdims=True)
            return trace, frob

        zero = jnp.zeros((1, RANK), F32)
        trace, frob = lax.fori_loop(0, 8, first, (zero, zero))
        ridge = RIDGE * jnp.sum(trace, axis=1, keepdims=True) / RANK
        top = ridge + jnp.sqrt(jnp.sum(frob, axis=1, keepdims=True))
        scale = 2.0 / (top + ridge)
        sigma = (top + ridge) / (top - ridge)

        def second(n, carry):
            rs = pl.ds(pl.multiple_of(n * 64, 64), 64)
            value = (dmat[rs, :] + diagonal(n, ridge)) * scale
            dmat[rs, :] = value
            high, low = split_two(value)
            dh[0, rs, :] = high
            dl[0, rs, :] = low
            d3[rs, :] = (value - high.astype(F32) - low.astype(F32)).astype(BF16)
            return carry

        lax.fori_loop(0, 8, second, 0)
        factors = []
        for q in range(STEPS):
            twice = 2.0 * sigma * sigma
            factors.append(twice / (twice - 1.0))
            sigma = twice - 1.0
        return scale, factors

    def set_rows(q, value):
        yvec[...] = value
        high, low = split_two(value)
        dh[q, 512:528, :] = jnp.concatenate(
            [high.astype(F32), low.astype(F32)], axis=0
        ).astype(BF16)

    def chain_step(q, factor, with_rows):
        tall = 528 if with_rows else 512
        for n in range(2):
            cs = slice(n * 256, n * 256 + 256)
            high, low = dh[q, 0:tall, :], dl[q]
            right_high, right_low = dh[q, 0:512, cs], dl[q, :, cs]
            one = dot(high, right_high)
            two = dot(high, right_low)
            square = one[0:512] + two[0:512] + dot(low, right_high)
            if q < EXACT_STEPS:
                square += (
                    dot(low, right_low)
                    + dot(dh[q, 0:512, :], d3[:, cs])
                    + dot(d3[...], right_high)
                )
            value = factor * (2.0 * dmat[:, cs] - square)
            dmat[:, cs] = value
            if q + 1 < STEPS - 1:
                high, low = split_two(value)
                dh[q + 1, 0:512, cs] = high
                dl[q + 1, :, cs] = low
            else:
                row = lax.broadcasted_iota(jnp.int32, (RANK, 256), 0)
                col = lax.broadcasted_iota(jnp.int32, (RANK, 256), 1) + n * 256
                dh[q + 1, 0:512, cs] = (jnp.where(row == col, 1.0, 0.0) - value).astype(BF16)
            if with_rows:
                value = one[512:520] + one[520:528] + two[512:520]
                value = factor * (2.0 * yvec[:, cs] - value)
                yvec[:, cs] = value
                high, low = split_two(value)
                dh[q + 1, 512:528, cs] = jnp.concatenate(
                    [high.astype(F32), low.astype(F32)], axis=0
                ).astype(BF16)

    def start_inverse(scale, factor):
        def body(n, carry):
            rs = pl.ds(pl.multiple_of(n * 64, 64), 64)
            value = (diagonal(n, 2.0) - dmat[rs, :]) * (scale * factor)
            xmat[rs, :] = value
            high, low = split_two(value)
            xh[1, rs, :] = high
            xl[1, rs, :] = low
            return carry

        lax.fori_loop(0, 8, body, 0)

    def inverse_step(q, factor):
        now, later = q % 2, (q + 1) % 2
        for n in range(2):
            cs = slice(n * 256, n * 256 + 256)
            right_high, right_low = dh[q, 0:512, cs], dl[q, :, cs]
            value = dot(xh[now], right_high)
            if q < STEPS - 1:
                value += dot(xh[now], right_low) + dot(xl[now], right_high)
                value = factor * (2.0 * xmat[:, cs] - value)
            else:
                value = factor * (xmat[:, cs] + value)
            xmat[:, cs] = value
            high, low = split_two(value)
            xh[later, :, cs] = high
            xl[later, :, cs] = low

    def times_inverse(rows):
        high, low = split_two(rows)
        last = STEPS % 2
        return dot(high, xh[last]) + dot(high, xl[last]) + dot(low, xh[last])

    def both_steps(q, factors):
        inverse_step(q, factors[q])
        if q < STEPS - 1:
            chain_step(q, factors[q], False)

    def apply_step(q, factor, value):
        high, low = split_two(value)
        both = jnp.concatenate([high.astype(F32), low.astype(F32)], axis=0).astype(BF16)
        wide = dot(both, dh[q, 0:512, :])
        narrow = dot(both, dl[q])
        return factor * (2.0 * value - (wide[0:8] + wide[8:16] + narrow[0:8]))

    def join(q, rows, scale, factors):
        value = rows * scale
        for n in range(q):
            value = apply_step(n, factors[n], value)
        set_rows(q, value)

    def last_step(factors):
        value = yvec[...]
        high, low = split_two(value)
        both = jnp.concatenate([high.astype(F32), low.astype(F32)], axis=0).astype(BF16)
        wide = dot(both, dh[STEPS - 1, 0:512, :])
        return factors[STEPS - 1] * (value + wide[0:8] + wide[8:16])

    yvec[...] = jnp.zeros_like(yvec)
    to_sib = remote(own8, sib8, send_sems.at[0], r_sib.at[0], sibling)
    to_sib.start()
    out.used = 1
    out.pending.append((to_sib, None))
    to_sib.wait_recv()
    slot = lax.rem(ia, 2) * 2 + zlo
    contributes = core == half
    all_b = Gather(g_b, 0, 4, slot, contributes, 0)
    all_c = Gather(g_c, 1, 4, slot, contributes, 1)

    for c in range(2):
        @pl.when(jnp.logical_and(contributes, core == c))
        def _():
            for gather, at in ((all_b, 0), (all_c, 4)):
                mine = own8[at:at + 4, :]
                theirs = sib8[at:at + 4, :]
                first, second = (mine, theirs) if c == 0 else (theirs, mine)
                gather.buf[core, gather.v, gather.u, slot, 0:4, :] = first
                gather.buf[core, gather.v, gather.u, slot, 4:8, :] = second

    both = (all_b, all_c)

    def turn(g, carry):
        tt[g] = t_ref[pl.ds(g * 16, 16)].reshape(1024, 256).T
        return carry

    for gather in both:
        gather.p0_send()
    load_t.wait()
    lax.fori_loop(0, 4, turn, 0)
    for gather in both:
        gather.p0_wait()
        gather.p1_send()
    lax.fori_loop(4, 8, turn, 0)
    for gather in both:
        gather.p1_wait()
        gather.p2_send()
        gather.p3_send(0, 0)

    def fill_c(n, carry):
        pia, rest = n // 8, lax.rem(n, 8)
        px, pzlo = rest // 2, lax.rem(rest, 2)
        ps = lax.rem(pia, 2) * 2 + pzlo
        cblk[pl.ds(pl.multiple_of(n * 8, 8), 8), :] = g_c[pia // 2, y, px, ps]
        return carry

    def fill_b(n, carry):
        pia, py = n // 2, lax.rem(n, 2) * 2
        ps = lax.rem(pia, 2) * 2 + zlo
        one, two = g_b[pia // 2, x, py, ps], g_b[pia // 2, x, py + 1, ps]

        @pl.when(core == 0)
        def _():
            pvec[0:4, :] = one[0:4]
            pvec[4:8, :] = two[0:4]

        @pl.when(core == 1)
        def _():
            pvec[0:4, :] = one[4:8]
            pvec[4:8, :] = two[4:8]

        bblk[pl.ds(pl.multiple_of(n * 8, 8), 8), :] = pvec[...].astype(BF16).astype(F32)
        return carry

    for gather in both:
        gather.p3_wait(0)
    lax.fori_loop(0, 32, fill_c, 0)
    lax.fori_loop(0, 8, fill_b, 0)

    def contract(g, carry):
        half_c = cblk[...].astype(BF16)
        weight = bblk[...]
        parts = []
        for s in range(2):
            piece = t_ref[pl.ds(g * 8 + s * 4, 4)].reshape(256, 256)
            value = dot(piece, half_c).reshape(4, 64, RANK)
            mixed[pl.ds(g * 8 + s * 4, 4)] = value.astype(BF16)
            parts.append(jnp.sum(value * weight[None], axis=1))
        px = g // 4
        pa[lax.rem(px, 2), px // 2, lax.rem(g, 4)] = jnp.concatenate(parts, axis=0)
        return carry

    lax.fori_loop(0, 4, contract, 0)
    for gather in both:
        gather.p2_forward()
    lax.fori_loop(4, 10, contract, 0)
    for gather in both:
        gather.p2_mid()
    lax.fori_loop(10, 16, contract, 0)

    beside = 1 - zlo
    out.send(pa.at[zlo], ra1.at[0], r_a.at[0], sibling, core != half)
    out.send(
        pa.at[beside], ra1.at[1], r_a.at[1], dev(x, y, ia * 2 + beside, core), core == half
    )
    out.send(
        pa.at[beside], ra1.at[2], r_a.at[2], dev(x, y, ia * 2 + beside, 1 - core), core != half
    )
    a_owner = jnp.logical_and(core == half, lax.rem(x, 2) == zlo)
    add_gram(gram_b, all_b.rows(0), True)
    add_gram(gram_c, all_c.rows(0), True)
    for gather in both:
        gather.p2_finish()

    all_b.p3_wait(1)
    add_gram(gram_b, all_b.rows(1), False)
    all_c.p3_wait(1)
    add_gram(gram_c, all_c.rows(1), False)

    @pl.when(core == half)
    def _():
        for m in range(3):
            recv(ra1.at[m], r_a.at[m]).wait_recv()
        pa[zlo] += ra1[0] + ra1[1] + ra1[2]

    for n in range(1, 16):
        px, py = lax.rem(x + n // 4, 4), lax.rem(y + n % 4, 4)
        out.send(
            pa.at[zlo, px // 2, py], ra2.at[n - 1], r_a.at[2 + n], at_xy(n),
            jnp.logical_and(core == half, lax.rem(px, 2) == zlo),
        )
    all_b.p3_wait(2)
    add_gram(gram_b, all_b.rows(2), False)
    all_c.p3_wait(2)
    add_gram(gram_c, all_c.rows(2), False)

    all_b.p3_wait(3)
    add_gram(gram_b, all_b.rows(3), False)
    all_c.p3_wait(3)
    add_gram(gram_c, all_c.rows(3), False)
    aslot = lax.rem(ia, 2)
    all_a = Gather(ga, 2, 2, aslot, a_owner, sel0)

    @pl.when(a_owner)
    def _():
        total = pa[zlo, x // 2, y]
        for n in range(1, 16):
            recv(ra2.at[n - 1], r_a.at[2 + n]).wait_recv()
            total = total + ra2[n - 1]
        ga[core, all_a.v, all_a.u, aslot] = total

    def invert(one, two, gather):
        scale, factors = start_chain(one, two)
        start_inverse(scale, factors[0])
        chain_step(0, factors[0], False)
        gather.p0_wait()
        gather.p1_send()
        both_steps(1, factors)
        both_steps(2, factors)
        gather.p1_wait()
        gather.p2_send()
        gather.p3_send(0, 0)
        both_steps(3, factors)
        both_steps(4, factors)
        gather.p2_forward()
        both_steps(5, factors)
        gather.p2_mid()
        both_steps(6, factors)
        gather.p2_finish()
        both_steps(7, factors)
        both_steps(8, factors)
        for n in range(4):
            gather.p3_wait(n)

    all_a.p0_send()
    invert(gram_b, gram_c, all_a)
    for n in range(2):
        raw_a[n] = times_inverse(ga[n].reshape(256, RANK)).reshape(4, 4, 2, 8, RANK)

    def fill_a(n, carry):
        px, py = n // 4, lax.rem(n, 4)
        pu = px * (1 - half) + py * half
        pv = py * (1 - half) + px * half
        ablk[pl.ds(pl.multiple_of(n * 8, 8), 8), :] = raw_a[half, pv, pu, aslot]
        return carry

    lax.fori_loop(0, 16, fill_a, 0)

    def second_mode(g, total):
        rows = ablk[pl.ds(pl.multiple_of(g * 8, 8), 8), :].astype(BF16).astype(F32)
        for s in range(8):
            total = total + mixed[g * 8 + s].astype(F32) * rows[s:s + 1, :]
        return total

    part_b = lax.fori_loop(0, 16, second_mode, jnp.zeros((64, RANK), F32))
    pb[...] = part_b.reshape(8, 8, RANK)
    for n in range(1, 16):
        pia, py = lax.rem(ia + n // 4, 4), lax.rem(y + n % 4, 4)
        out.send(
            pb.at[lax.rem(pia, 2) * 4 + py], rb1.at[n - 1], r_b.at[n - 1], at_iy(n),
            pia // 2 == core,
        )
    for n in range(2):
        add_gram(gram_a, [raw_a[n].reshape(256, RANK)], n == 0)
    inverse_a = normal_gram(gram_a, 512)

    all_b2 = Gather(gb, 3, 4, slot, contributes, sel0)

    @pl.when(core == half)
    def _():
        rows = pb[lax.rem(ia, 2) * 4 + y]
        for n in range(1, 16):
            recv(rb1.at[n - 1], r_b.at[n - 1]).wait_recv()
            rows = rows + rb1[n - 1]
        gb[core, all_b2.v, all_b2.u, slot] = rows * inverse_a

    all_b2.p0_send()

    def repeat_a(g, carry):
        rows = ablk[pl.ds(pl.multiple_of(g * 8, 8), 8), :].astype(BF16).astype(F32)
        for s in range(8):
            arep[g * 8 + s] = jnp.broadcast_to(rows[s:s + 1, :], (16, RANK)).astype(BF16)
        return carry

    lax.fori_loop(0, 16, repeat_a, 0)
    own_a = ablk[pl.ds(pl.multiple_of(ja * 8, 8), 8), :] * inverse_a
    for s in range(4):
        @pl.when(ka == s)
        def _():
            a_out[0, 0] = own_a[2 * s:2 * s + 2]

    invert(gram_a, gram_c, all_b2)

    def fill_b2(n, carry):
        py = lax.rem(n, 4)
        pu = x * sel0 + py * core
        pv = py * sel0 + x * core
        rows = gb[core, pv, pu, (n // 4) * 2 + zlo]
        b2blk[pl.ds(pl.multiple_of(n * 8, 8), 8), :] = rows
        return carry

    lax.fori_loop(0, 8, fill_b2, 0)
    b2blk[...] = times_inverse(b2blk[...])

    pc[...] = jnp.zeros_like(pc)

    def third_mode(g, carry):
        half_b2 = b2blk[...].astype(BF16).reshape(4, 16, RANK)
        weight = jnp.concatenate(
            [(half_b2 * arep[g * 16 + n][None]).reshape(64, RANK) for n in range(16)], axis=0
        )
        pc[...] += dot(tt[g], weight).reshape(4, 4, 2, 8, RANK)
        return carry

    lax.fori_loop(0, 8, third_mode, 0)
    out.send(pc.at[pl.ds(2 * (1 - core), 2)], rc0, r_c.at[0], sibling)

    def all_rows(n, carry):
        h, pair = n // 2, lax.rem(n, 2) * 2
        rows = times_inverse(gb[h, pl.ds(pair, 2)].reshape(256, RANK))
        high, low = split_two(rows)
        mh[...] = high
        ml[...] = low
        high, low = mh[...], ml[...]
        gram_b2[...] += dot_rows(high, high) + dot_rows(high, low) + dot_rows(low, high)
        return carry

    gram_b2[...] = jnp.zeros_like(gram_b2)
    lax.fori_loop(0, 2, all_rows, 0)
    recv(rc0, r_c.at[0]).wait_recv()
    pc[pl.ds(2 * core, 2)] += rc0[...]
    for d in (1, 2, 3):
        out.send(
            pc.at[pl.ds(2 * core, 2), lax.rem(x + d, 4)], rc1.at[d - 1], r_c.at[d], at_x(d)
        )
    lax.fori_loop(2, 4, all_rows, 0)
    inverse_b = normal_gram(gram_b2, 1024)
    own_b = b2blk[pl.ds(pl.multiple_of((ia * 2 + ka // 2) * 8, 8), 8), :] * inverse_b
    for s in range(2):
        @pl.when(lax.rem(ka, 2) == s)
        def _():
            b_out[0, 0] = own_b[4 * s:4 * s + 4]

    scale, factors = start_chain(gram_a, gram_b2)
    chain_step(0, factors[0], False)
    for d in (1, 2, 3):
        recv(rc1.at[d - 1], r_c.at[d]).wait_recv()
    sc[...] = pc[pl.ds(2 * core, 2), x] + rc1[0] + rc1[1] + rc1[2]
    for d in range(8):
        pz = lax.rem(z + d, 8)
        for other in range(2):
            if d == 0 and not other:
                continue
            out.send(
                sc.at[lax.rem(pz // 2, 2), lax.rem(pz, 2)], rc2.at[d], r_c.at[4 + d],
                dev(x, y, pz, core * (1 - other) + (1 - core) * other), pz // 4 == core,
            )
    for q in (1, 2):
        chain_step(q, factors[q], False)
    for d in range(1, 8):
        recv(rc2.at[d], r_c.at[4 + d]).wait_recv()

    @pl.when(core == half)
    def _():
        tc[...] = sc[lax.rem(ia, 2), zlo]

    @pl.when(core != half)
    def _():
        recv(rc2.at[0], r_c.at[4]).wait_recv()
        tc[...] = rc2[0]

    total = tc[...]
    for d in range(1, 8):
        total = total + rc2[d]
    join(3, total * (inverse_a * inverse_b), scale, factors)
    for q in range(3, STEPS - 1):
        chain_step(q, factors[q], True)
    raw = last_step(factors)

    sq1[...] = raw * raw
    for n in range(1, 16):
        out.send(sq1, rq1.at[n - 1], r_q.at[n - 1], at_xy(n))
    total = sq1[...]
    for n in range(1, 16):
        recv(rq1.at[n - 1], r_q.at[n - 1]).wait_recv()
        total = total + rq1[n - 1]
    sq3[...] = total
    for d in range(1, 8):
        out.send(sq3, rq3.at[d - 1], r_q.at[14 + d], at_z(d))
    for d in range(1, 8):
        recv(rq3.at[d - 1], r_q.at[14 + d]).wait_recv()
    total = sq3[...]
    for d in range(7):
        total = total + rq3[d]
    spread = jnp.sqrt(jnp.sum(total, axis=0, keepdims=True) / 1024 + EPS)
    final = raw / spread
    for s in range(2):
        @pl.when(core == s)
        def _():
            c_out[0, 0] = final[4 * s:4 * s + 4]

    out.finish()


def hand_over(a_ref, b_ref, c_ref, a_out, b_out, c_out):
    a_out[...] = a_ref[...]
    b_out[...] = b_ref[...]
    c_out[...] = c_ref[...]


def shards(tensor, factor_b, factor_c):
    vmem = pltpu.VMEM
    dma = pltpu.SemaphoreType.DMA
    scratch = [
        vmem((128, 64, 256), BF16),
        vmem((8, 256, 1024), BF16),
        vmem((128, 64, RANK), BF16),
        vmem((128, 16, RANK), BF16),
        vmem((8, RANK), F32),
        vmem((8, RANK), F32),
        vmem((2, 4, 4, 4, 8, RANK), F32),
        vmem((2, 4, 4, 4, 8, RANK), F32),
        vmem((2, 4, 4, 2, 8, RANK), F32),
        vmem((2, 4, 4, 4, 8, RANK), F32),
        vmem((2, 2, 4, 8, RANK), F32),
        vmem((8, 8, RANK), F32),
        vmem((4, 4, 2, 8, RANK), F32),
        vmem((3, 2, 4, 8, RANK), F32),
        vmem((15, 8, RANK), F32),
        vmem((15, 8, RANK), F32),
        vmem((2, 4, 2, 8, RANK), F32),
        vmem((3, 2, 2, 8, RANK), F32),
        vmem((2, 2, 8, RANK), F32),
        vmem((8, 8, RANK), F32),
        vmem((8, RANK), F32),
        vmem((15, 8, RANK), F32),
        vmem((7, 8, RANK), F32),
        vmem((8, RANK), F32),
        vmem((8, RANK), F32),
        vmem((256, RANK), BF16),
        vmem((256, RANK), BF16),
        vmem((RANK, RANK), F32),
        vmem((RANK, RANK), F32),
        vmem((RANK, RANK), F32),
        vmem((RANK, RANK), F32),
        vmem((RANK, RANK), F32),
        vmem((STEPS, RANK + 16, RANK), BF16),
        vmem((STEPS, RANK, RANK), BF16),
        vmem((RANK, RANK), BF16),
        vmem((8, RANK), F32),
        vmem((RANK, RANK), F32),
        vmem((2, RANK, RANK), BF16),
        vmem((2, RANK, RANK), BF16),
        vmem((2, 4, 4, 2, 8, RANK), F32),
        vmem((2, 4, 4, 4, 8, RANK), F32),
        vmem((64, RANK), F32),
        vmem((256, RANK), F32),
        vmem((128, RANK), F32),
        vmem((64, RANK), F32),
        vmem((8, RANK), F32),
        dma((192,)),
        dma((1,)),
        dma((4, 4)),
        dma((4, 3)),
        dma((4, 6)),
        dma((4, 4)),
        dma((18,)),
        dma((15,)),
        dma((12,)),
        dma((22,)),
        dma,
    ]
    results = pl.pallas_call(
        kernel,
        out_shape=(
            jax.ShapeDtypeStruct((1, 1, 2, RANK), F32),
            jax.ShapeDtypeStruct((1, 1, 4, RANK), F32),
            jax.ShapeDtypeStruct((1, 1, 4, RANK), F32),
        ),
        in_specs=[
            pl.BlockSpec(memory_space=pl.ANY),
            pl.BlockSpec(memory_space=pltpu.VMEM),
            pl.BlockSpec(memory_space=pltpu.VMEM),
        ],
        out_specs=[pl.BlockSpec(memory_space=pltpu.VMEM)] * 3,
        scratch_shapes=scratch,
        compiler_params=pltpu.CompilerParams(
            collective_id=0, has_side_effects=True, vmem_limit_bytes=58 * 1024 * 1024
        ),
        name="sweep",
    )(tensor, factor_b, factor_c)
    return pl.pallas_call(
        hand_over,
        out_shape=tuple(jax.ShapeDtypeStruct(r.shape, F32) for r in results),
        name="hand_over",
    )(*results)


def solution(mesh):
    in_specs = (
        P("ia", "ja", "ka"),
        P("ja", ("ia", "ka"), None, None),
        P("ka", ("ia", "ja"), None, None),
    )
    out_specs = (
        P("ia", ("ja", "ka"), None, None),
        P("ja", ("ia", "ka"), None, None),
        P("ka", ("ia", "ja"), None, None),
    )
    return jax.shard_map(shards, mesh=mesh, in_specs=in_specs, out_specs=out_specs, check_vma=False)
```

```python
import functools

import jax
import jax.numpy as jnp
from jax import lax
from jax.experimental import pallas as pl
from jax.experimental.pallas import tpu as pltpu
from jax.sharding import PartitionSpec as P

RIDGE = 0.1
EPS = 1e-06
F32 = jnp.float32
BF16 = jnp.bfloat16
RANK = 512
STEPS = 9


def dot(left, right):
    return jnp.dot(left, right, preferred_element_type=F32)


def dot_rows(left, right):
    return lax.dot_general(left, right, (((0,), (0,)), ((), ())), preferred_element_type=F32)


def split_two(value):
    high = value.astype(BF16)
    low = (value - high.astype(F32)).astype(BF16)
    return high, low


def remote(src, dst, send_sem, recv_sem, device):
    return pltpu.make_async_remote_copy(
        src_ref=src,
        dst_ref=dst,
        send_sem=send_sem,
        recv_sem=recv_sem,
        device_id=device,
        device_id_type=pl.DeviceIdType.MESH,
    )


class Sender:
    def __init__(self, sems):
        self.sems = sems
        self.used = 0
        self.pending = []

    def send(self, src, dst, recv_sem, device, cond=None):
        sem = self.sems.at[self.used]
        self.used += 1
        copy = remote(src, dst, sem, recv_sem, device)
        if cond is None:
            copy.start()
        else:
            pl.when(cond)(copy.start)
        self.pending.append((copy, cond))

    def finish(self):
        for copy, cond in self.pending:
            if cond is None:
                copy.wait_send()
            else:
                pl.when(cond)(copy.wait_send)


def kernel(
    t_hbm, fb_ref, fc_ref, a_out, b_out, c_out,
    t_ref, tt, mixed, arep, own8, sib8, g_b, g_c, ga, gb,
    pa, pb, pc, ra1, ra2, rb1, rc0, rc1, sc, rc2, tc,
    rq1, rq3, sq1, sq3,
    mh, ml, gram_b, gram_c, gram_a, gram_b2, dmat, dh, dl, low_b, low_c, yvec, xmat, xh, xl, raw_a, raw_b,
    bblk, cblk, ablk, b2blk, pvec,
    send_sems, r_sib, r_p0, r_p1, r_p2, r_p3, r_a, r_b, r_c, r_q, t_sem,
):
    ia = lax.axis_index("ia")
    ja = lax.axis_index("ja")
    ka = lax.axis_index("ka")
    core = lax.rem(ja, 2)
    zlo = lax.rem(ja // 2, 2)
    x = ja // 4
    y = ka
    z = ia * 2 + zlo
    half = ia // 2
    sel0 = 1 - core

    def dev(px, py, pz, pcore):
        return (pz // 2, px * 4 + lax.rem(pz, 2) * 2 + pcore, py)

    sibling = dev(x, y, z, 1 - core)

    def at_x(d):
        return dev(lax.rem(x + d, 4), y, z, core)

    def at_xy(n):
        return dev(lax.rem(x + n // 4, 4), lax.rem(y + n % 4, 4), z, core)

    def at_iy(n):
        return dev(x, lax.rem(y + n % 4, 4), lax.rem(ia + n // 4, 4) * 2 + zlo, core)

    def at_z(d):
        return dev(x, y, lax.rem(z + d, 8), core)

    load_t = pltpu.make_async_copy(t_hbm, t_ref, t_sem)
    load_t.start()
    out = Sender(send_sems)

    barrier = pltpu.get_barrier_semaphore()
    partners = [sibling]
    partners += [at_xy(n) for n in range(1, 16)]
    partners += [at_z(d) for d in range(1, 8)]
    partners += [dev(x, y, lax.rem(z + d, 8), 1 - core) for d in range(1, 8)]
    partners += [at_iy(n) for n in range(1, 16) if n // 4 and n % 4]
    for partner in partners:
        pl.semaphore_signal(
            barrier, inc=1, device_id=partner, device_id_type=pl.DeviceIdType.MESH
        )

    own8[0:4, :] = fb_ref[0, 0]
    own8[4:8, :] = fc_ref[0, 0]
    pl.semaphore_wait(barrier, len(partners))

    def recv(ref, sem):
        return remote(ref, ref, send_sems.at[0], sem, sibling)

    class Gather:
        def __init__(self, buf, stage, slots, slot, contributes, u_is_x):
            self.buf, self.stage, self.slots, self.slot = buf, stage, slots, slot
            self.contributes = contributes
            self.u_is_x = u_is_x
            self.u = x * u_is_x + y * (1 - u_is_x)
            self.v = y * u_is_x + x * (1 - u_is_x)
            self.p0 = [r_p0.at[stage, n] for n in range(slots)]
            self.p1 = [r_p1.at[stage, n] for n in range(3)]
            self.p2 = [r_p2.at[stage, n] for n in range(6)]
            self.p3 = [r_p3.at[stage, n] for n in range(4)]

        def near(self, du, dv):
            pu, pv = lax.rem(self.u + du + 4, 4), lax.rem(self.v + dv + 4, 4)
            keep = self.u_is_x
            return dev(pu * keep + pv * (1 - keep), pv * keep + pu * (1 - keep), z, core)

        def move(self, ref, sem, device):
            out.send(ref, ref, sem, device)

        def chunk(self, du):
            return self.buf.at[core, self.v, lax.rem(self.u + du + 4, 4)]

        def slab(self, dv, first=None):
            pv = lax.rem(self.v + dv + 4, 4)
            if first is None:
                return self.buf.at[core, pv]
            return self.buf.at[core, pv, pl.ds(first * 2, 2)]

        def p0_send(self):
            ref = self.buf.at[core, self.v, self.u, self.slot]
            for d in (4, 3, 5, 2, 6, 1, 7):
                out.send(ref, ref, r_p0.at[self.stage, self.slot], at_z(d), self.contributes)

        def p0_wait(self):
            for s in range(self.slots):
                other = jnp.logical_not(jnp.logical_and(self.contributes, self.slot == s))
                copy = recv(self.buf.at[core, self.v, self.u, s], self.p0[s])
                pl.when(other)(copy.wait_recv)

        def p1_send(self):
            for d in (2, 1, 3):
                self.move(self.chunk(0), self.p1[d - 1], self.near(d, 0))

        def p1_wait(self):
            for d in (1, 3, 2):
                recv(self.chunk(-d), self.p1[d - 1]).wait_recv()

        def p2_send(self):
            self.move(self.slab(0, 0), self.p2[0], self.near(0, 1))
            self.move(self.slab(0, 1), self.p2[2], self.near(0, -1))
            self.move(self.slab(0, 1), self.p2[1], self.near(0, 1))
            self.move(self.slab(0, 0), self.p2[3], self.near(0, -1))

        def p3_send(self, dv, n):
            self.move(self.slab(dv), self.p3[n], sibling)

        def p2_forward(self):
            recv(self.slab(-1, 0), self.p2[0]).wait_recv()
            self.move(self.slab(-1, 0), self.p2[4], self.near(0, 1))
            recv(self.slab(1, 1), self.p2[2]).wait_recv()
            self.move(self.slab(1, 1), self.p2[5], self.near(0, -1))

        def p2_mid(self):
            recv(self.slab(-1, 1), self.p2[1]).wait_recv()
            self.p3_send(-1, 1)
            recv(self.slab(1, 0), self.p2[3]).wait_recv()
            self.p3_send(1, 2)

        def p2_finish(self):
            recv(self.slab(2, 0), self.p2[4]).wait_recv()
            recv(self.slab(2, 1), self.p2[5]).wait_recv()
            self.p3_send(2, 3)

        def p3_wait(self, n):
            recv(self.buf.at[1 - core, n], self.p3[n]).wait_recv()

        def rows(self, n):
            step = (0, -1, 1, 2)[n]
            other = self.v if self.stage < 2 else self.u
            mine = self.buf[core, lax.rem(self.v + step + 4, 4)]
            theirs = self.buf[1 - core, lax.rem(other + step + 4, 4)]
            count = 4 * self.slots * 8
            return [mine.reshape(count, RANK), theirs.reshape(count, RANK)]

    def close_gram(out_ref, low_ref):
        value = low_ref[...]
        out_ref[...] += value + value.T

    def add_gram(out_ref, parts, first, low_ref=None):
        size = parts[0].shape[0]
        for n, part in enumerate(parts):
            high, low = split_two(part)
            mh[n * size:(n + 1) * size, :] = high
            ml[n * size:(n + 1) * size, :] = low
        high, low = mh[...], ml[...]
        value = dot_rows(high, high)
        cross = dot_rows(high, low)
        if low_ref is None:
            value += cross + dot_rows(low, high)
        else:
            low_ref[...] = cross if first else low_ref[...] + cross
        out_ref[...] = value if first else out_ref[...] + value

    def diagonal(n, value):
        row = lax.broadcasted_iota(jnp.int32, (64, RANK), 0) + n * 64
        col = lax.broadcasted_iota(jnp.int32, (64, RANK), 1)
        return jnp.where(row == col, value, 0.0)

    def normal_gram(ref, count):
        def squares(n, total):
            rs = pl.ds(pl.multiple_of(n * 64, 64), 64)
            return total + jnp.sum(diagonal(n, ref[rs, :]), axis=0, keepdims=True)

        total = lax.fori_loop(0, 8, squares, jnp.zeros((1, RANK), F32))
        inverse = 1.0 / jnp.sqrt(total / count + EPS)

        def body(n, carry):
            rs = pl.ds(pl.multiple_of(n * 64, 64), 64)
            value = ref[rs, :]
            mine = jnp.sum(diagonal(n, value), axis=1, keepdims=True)
            ref[rs, :] = value * (1.0 / jnp.sqrt(mine / count + EPS)) * inverse
            return carry

        lax.fori_loop(0, 8, body, 0)
        return inverse

    def start_chain(one, two):
        def first(n, carry):
            trace, frob = carry
            rs = pl.ds(pl.multiple_of(n * 64, 64), 64)
            value = one[rs, :] * two[rs, :]
            dmat[rs, :] = value
            trace += jnp.sum(diagonal(n, value), axis=0, keepdims=True)
            frob += jnp.sum(value * value, axis=0, keepdims=True)
            return trace, frob

        zero = jnp.zeros((1, RANK), F32)
        trace, frob = lax.fori_loop(0, 8, first, (zero, zero))
        ridge = RIDGE * jnp.sum(trace, axis=1, keepdims=True) / RANK
        top = ridge + jnp.sqrt(jnp.sum(frob, axis=1, keepdims=True))
        scale = 2.0 / (top + ridge)
        sigma = (top + ridge) / (top - ridge)

        def second(n, carry):
            rs = pl.ds(pl.multiple_of(n * 64, 64), 64)
            value = (dmat[rs, :] + diagonal(n, ridge)) * scale
            dmat[rs, :] = value
            high, low = split_two(value)
            dh[0, rs, :] = high
            dl[0, rs, :] = low
            return carry

        lax.fori_loop(0, 8, second, 0)
        factors = []
        for q in range(STEPS):
            twice = 2.0 * sigma * sigma
            factors.append(twice / (twice - 1.0))
            sigma = twice - 1.0
        return scale, factors

    def set_rows(q, value):
        yvec[...] = value
        high, low = split_two(value)
        dh[q, 512:528, :] = jnp.concatenate(
            [high.astype(F32), low.astype(F32)], axis=0
        ).astype(BF16)

    def chain_step(q, factor, with_rows):
        tall = 528 if with_rows else 512
        for n in range(2):
            cs = slice(n * 256, n * 256 + 256)
            high, low = dh[q, 0:tall, :], dl[q]
            right_high, right_low = dh[q, 0:512, cs], dl[q, :, cs]
            one = dot(high, right_high)
            two = dot(high, right_low)
            square = one[0:512] + two[0:512] + dot(low, right_high)
            value = factor * (2.0 * dmat[:, cs] - square)
            dmat[:, cs] = value
            if q + 1 < STEPS - 1:
                high, low = split_two(value)
                dh[q + 1, 0:512, cs] = high
                dl[q + 1, :, cs] = low
            else:
                row = lax.broadcasted_iota(jnp.int32, (RANK, 256), 0)
                col = lax.broadcasted_iota(jnp.int32, (RANK, 256), 1) + n * 256
                dh[q + 1, 0:512, cs] = (jnp.where(row == col, 1.0, 0.0) - value).astype(BF16)
            if with_rows:
                value = one[512:520] + one[520:528] + two[512:520]
                value = factor * (2.0 * yvec[:, cs] - value)
                yvec[:, cs] = value
                high, low = split_two(value)
                dh[q + 1, 512:528, cs] = jnp.concatenate(
                    [high.astype(F32), low.astype(F32)], axis=0
                ).astype(BF16)

    def start_inverse(scale, factor):
        def body(n, carry):
            rs = pl.ds(pl.multiple_of(n * 64, 64), 64)
            value = (diagonal(n, 2.0) - dmat[rs, :]) * (scale * factor)
            xmat[rs, :] = value
            high, low = split_two(value)
            xh[1, rs, :] = high
            xl[1, rs, :] = low
            return carry

        lax.fori_loop(0, 8, body, 0)

    def inverse_step(q, factor):
        now, later = q % 2, (q + 1) % 2
        for n in range(2):
            cs = slice(n * 256, n * 256 + 256)
            right_high, right_low = dh[q, 0:512, cs], dl[q, :, cs]
            value = dot(xh[now], right_high)
            if q < STEPS - 1:
                value += dot(xh[now], right_low) + dot(xl[now], right_high)
                value = factor * (2.0 * xmat[:, cs] - value)
            else:
                value = factor * (xmat[:, cs] + value)
            xmat[:, cs] = value
            high, low = split_two(value)
            xh[later, :, cs] = high
            xl[later, :, cs] = low

    def times_inverse(rows):
        high, low = split_two(rows)
        last = STEPS % 2
        return dot(high, xh[last]) + dot(high, xl[last]) + dot(low, xh[last])

    def both_steps(q, factors):
        inverse_step(q, factors[q])
        if q < STEPS - 1:
            chain_step(q, factors[q], False)

    def apply_step(q, factor, value):
        high, low = split_two(value)
        both = jnp.concatenate([high.astype(F32), low.astype(F32)], axis=0).astype(BF16)
        wide = dot(both, dh[q, 0:512, :])
        narrow = dot(both, dl[q])
        return factor * (2.0 * value - (wide[0:8] + wide[8:16] + narrow[0:8]))

    def join(q, rows, scale, factors):
        value = rows * scale
        for n in range(q):
            value = apply_step(n, factors[n], value)
        set_rows(q, value)

    def last_step(factors):
        value = yvec[...]
        high, low = split_two(value)
        both = jnp.concatenate([high.astype(F32), low.astype(F32)], axis=0).astype(BF16)
        wide = dot(both, dh[STEPS - 1, 0:512, :])
        return factors[STEPS - 1] * (value + wide[0:8] + wide[8:16])

    yvec[...] = jnp.zeros_like(yvec)
    to_sib = remote(own8, sib8, send_sems.at[0], r_sib.at[0], sibling)
    to_sib.start()
    out.used = 1
    out.pending.append((to_sib, None))
    to_sib.wait_recv()
    slot = lax.rem(ia, 2) * 2 + zlo
    contributes = core == half
    all_b = Gather(g_b, 0, 4, slot, contributes, 0)
    all_c = Gather(g_c, 1, 4, slot, contributes, 1)

    for c in range(2):
        @pl.when(jnp.logical_and(contributes, core == c))
        def _():
            for gather, at in ((all_b, 0), (all_c, 4)):
                mine = own8[at:at + 4, :]
                theirs = sib8[at:at + 4, :]
                first, second = (mine, theirs) if c == 0 else (theirs, mine)
                gather.buf[core, gather.v, gather.u, slot, 0:4, :] = first
                gather.buf[core, gather.v, gather.u, slot, 4:8, :] = second

    both = (all_b, all_c)

    def turn(g, carry):
        tt[g] = t_ref[pl.ds(g * 16, 16)].reshape(1024, 256).T
        return carry

    for gather in both:
        gather.p0_send()
    load_t.wait()
    lax.fori_loop(0, 4, turn, 0)
    for gather in both:
        gather.p0_wait()
        gather.p1_send()
    lax.fori_loop(4, 8, turn, 0)
    for gather in both:
        gather.p1_wait()
        gather.p2_send()
        gather.p3_send(0, 0)

    def fill_c(n, carry):
        pia, rest = n // 8, lax.rem(n, 8)
        px, pzlo = rest // 2, lax.rem(rest, 2)
        ps = lax.rem(pia, 2) * 2 + pzlo
        cblk[pl.ds(pl.multiple_of(n * 8, 8), 8), :] = g_c[pia // 2, y, px, ps]
        return carry

    def fill_b(n, carry):
        pia, py = n // 2, lax.rem(n, 2) * 2
        ps = lax.rem(pia, 2) * 2 + zlo
        one, two = g_b[pia // 2, x, py, ps], g_b[pia // 2, x, py + 1, ps]

        @pl.when(core == 0)
        def _():
            pvec[0:4, :] = one[0:4]
            pvec[4:8, :] = two[0:4]

        @pl.when(core == 1)
        def _():
            pvec[0:4, :] = one[4:8]
            pvec[4:8, :] = two[4:8]

        bblk[pl.ds(pl.multiple_of(n * 8, 8), 8), :] = pvec[...].astype(BF16).astype(F32)
        return carry

    for gather in both:
        gather.p3_wait(0)
    lax.fori_loop(0, 32, fill_c, 0)
    lax.fori_loop(0, 8, fill_b, 0)

    def contract(g, carry):
        half_c = cblk[...].astype(BF16)
        weight = bblk[...]
        parts = []
        for s in range(2):
            piece = t_ref[pl.ds(g * 8 + s * 4, 4)].reshape(256, 256)
            value = dot(piece, half_c).reshape(4, 64, RANK)
            mixed[pl.ds(g * 8 + s * 4, 4)] = value.astype(BF16)
            parts.append(jnp.sum(value * weight[None], axis=1))
        px = g // 4
        pa[lax.rem(px, 2), px // 2, lax.rem(g, 4)] = jnp.concatenate(parts, axis=0)
        return carry

    lax.fori_loop(0, 4, contract, 0)
    for gather in both:
        gather.p2_forward()
    lax.fori_loop(4, 10, contract, 0)
    for gather in both:
        gather.p2_mid()
    lax.fori_loop(10, 16, contract, 0)

    beside = 1 - zlo
    out.send(pa.at[zlo], ra1.at[0], r_a.at[0], sibling, core != half)
    out.send(
        pa.at[beside], ra1.at[1], r_a.at[1], dev(x, y, ia * 2 + beside, core), core == half
    )
    out.send(
        pa.at[beside], ra1.at[2], r_a.at[2], dev(x, y, ia * 2 + beside, 1 - core), core != half
    )
    a_owner = jnp.logical_and(core == half, lax.rem(x, 2) == zlo)
    add_gram(gram_b, all_b.rows(0), True, low_b)
    add_gram(gram_c, all_c.rows(0), True, low_c)
    for gather in both:
        gather.p2_finish()

    all_b.p3_wait(1)
    add_gram(gram_b, all_b.rows(1), False, low_b)
    all_c.p3_wait(1)
    add_gram(gram_c, all_c.rows(1), False, low_c)

    @pl.when(core == half)
    def _():
        for m in range(3):
            recv(ra1.at[m], r_a.at[m]).wait_recv()
        pa[zlo] += ra1[0] + ra1[1] + ra1[2]

    for n in range(1, 16):
        px, py = lax.rem(x + n // 4, 4), lax.rem(y + n % 4, 4)
        out.send(
            pa.at[zlo, px // 2, py], ra2.at[n - 1], r_a.at[2 + n], at_xy(n),
            jnp.logical_and(core == half, lax.rem(px, 2) == zlo),
        )
    all_b.p3_wait(2)
    add_gram(gram_b, all_b.rows(2), False, low_b)
    all_c.p3_wait(2)
    add_gram(gram_c, all_c.rows(2), False, low_c)

    all_b.p3_wait(3)
    add_gram(gram_b, all_b.rows(3), False, low_b)
    all_c.p3_wait(3)
    add_gram(gram_c, all_c.rows(3), False, low_c)
    aslot = lax.rem(ia, 2)
    all_a = Gather(ga, 2, 2, aslot, a_owner, sel0)

    def invert(one, two, gather, begin):
        scale, factors = start_chain(one, two)
        start_inverse(scale, factors[0])
        begin()
        chain_step(0, factors[0], False)
        both_steps(1, factors)
        gather.p0_wait()
        gather.p1_send()
        both_steps(2, factors)
        both_steps(3, factors)
        gather.p1_wait()
        gather.p2_send()
        gather.p3_send(0, 0)
        both_steps(4, factors)
        both_steps(5, factors)
        gather.p2_forward()
        both_steps(6, factors)
        gather.p2_mid()
        gather.p2_finish()
        both_steps(7, factors)
        both_steps(8, factors)
        for n in range(4):
            gather.p3_wait(n)

    def begin_a():
        @pl.when(a_owner)
        def _():
            total = pa[zlo, x // 2, y]
            for n in range(1, 16):
                recv(ra2.at[n - 1], r_a.at[2 + n]).wait_recv()
                total = total + ra2[n - 1]
            ga[core, all_a.v, all_a.u, aslot] = total

        all_a.p0_send()

    close_gram(gram_b, low_b)
    close_gram(gram_c, low_c)
    invert(gram_b, gram_c, all_a, begin_a)
    for n in range(2):
        raw_a[n] = times_inverse(ga[n].reshape(256, RANK)).reshape(4, 4, 2, 8, RANK)

    def fill_a(n, carry):
        px, py = n // 4, lax.rem(n, 4)
        pu = px * (1 - half) + py * half
        pv = py * (1 - half) + px * half
        ablk[pl.ds(pl.multiple_of(n * 8, 8), 8), :] = raw_a[half, pv, pu, aslot]
        return carry

    lax.fori_loop(0, 16, fill_a, 0)

    def second_mode(g, total):
        rows = ablk[pl.ds(pl.multiple_of(g * 8, 8), 8), :].astype(BF16).astype(F32)
        for s in range(8):
            total = total + mixed[g * 8 + s].astype(F32) * rows[s:s + 1, :]
        return total

    part_b = lax.fori_loop(0, 16, second_mode, jnp.zeros((64, RANK), F32))
    pb[...] = part_b.reshape(8, 8, RANK)
    for n in range(1, 16):
        pia, py = lax.rem(ia + n // 4, 4), lax.rem(y + n % 4, 4)
        out.send(
            pb.at[lax.rem(pia, 2) * 4 + py], rb1.at[n - 1], r_b.at[n - 1], at_iy(n),
            pia // 2 == core,
        )
    for n in range(2):
        add_gram(gram_a, [raw_a[n].reshape(256, RANK)], n == 0)
    inverse_a = normal_gram(gram_a, 512)

    def repeat_a(g, carry):
        rows = ablk[pl.ds(pl.multiple_of(g * 8, 8), 8), :].astype(BF16).astype(F32)
        for s in range(8):
            arep[g * 8 + s] = jnp.broadcast_to(rows[s:s + 1, :], (16, RANK)).astype(BF16)
        return carry

    lax.fori_loop(0, 16, repeat_a, 0)
    all_b2 = Gather(gb, 3, 4, slot, contributes, sel0)

    @pl.when(core == half)
    def _():
        rows = pb[lax.rem(ia, 2) * 4 + y]
        for n in range(1, 16):
            recv(rb1.at[n - 1], r_b.at[n - 1]).wait_recv()
            rows = rows + rb1[n - 1]
        gb[core, all_b2.v, all_b2.u, slot] = rows * inverse_a

    all_b2.p0_send()

    own_a = ablk[pl.ds(pl.multiple_of(ja * 8, 8), 8), :] * inverse_a
    for s in range(4):
        @pl.when(ka == s)
        def _():
            a_out[0, 0] = own_a[2 * s:2 * s + 2]

    invert(gram_a, gram_c, all_b2, lambda: None)

    def fill_b2(n, carry):
        py = lax.rem(n, 4)
        pu = x * sel0 + py * core
        pv = py * sel0 + x * core
        rows = gb[core, pv, pu, (n // 4) * 2 + zlo]
        b2blk[pl.ds(pl.multiple_of(n * 8, 8), 8), :] = rows
        return carry

    lax.fori_loop(0, 8, fill_b2, 0)
    b2blk[...] = times_inverse(b2blk[...])

    pc[...] = jnp.zeros_like(pc)

    def third_mode(g, carry):
        half_b2 = b2blk[...].astype(BF16).reshape(4, 16, RANK)
        weight = jnp.concatenate(
            [(half_b2 * arep[g * 16 + n][None]).reshape(64, RANK) for n in range(16)], axis=0
        )
        pc[...] += dot(tt[g], weight).reshape(4, 4, 2, 8, RANK)
        return carry

    lax.fori_loop(0, 8, third_mode, 0)
    out.send(pc.at[pl.ds(2 * (1 - core), 2)], rc0, r_c.at[0], sibling)

    def all_rows(n, carry):
        h, pair = n // 2, lax.rem(n, 2) * 2
        rows = times_inverse(gb[h, pl.ds(pair, 2)].reshape(256, RANK))
        high, low = split_two(rows)
        mh[...] = high
        ml[...] = low
        high, low = mh[...], ml[...]
        gram_b2[...] += dot_rows(high, high)
        low_b[...] += dot_rows(high, low)
        return carry

    gram_b2[...] = jnp.zeros_like(gram_b2)
    low_b[...] = jnp.zeros_like(low_b)
    lax.fori_loop(0, 2, all_rows, 0)
    recv(rc0, r_c.at[0]).wait_recv()
    pc[pl.ds(2 * core, 2)] += rc0[...]
    for d in (1, 2, 3):
        out.send(
            pc.at[pl.ds(2 * core, 2), lax.rem(x + d, 4)], rc1.at[d - 1], r_c.at[d], at_x(d)
        )
    lax.fori_loop(2, 4, all_rows, 0)
    close_gram(gram_b2, low_b)
    inverse_b = normal_gram(gram_b2, 1024)
    own_b = b2blk[pl.ds(pl.multiple_of((ia * 2 + ka // 2) * 8, 8), 8), :] * inverse_b
    for s in range(2):
        @pl.when(lax.rem(ka, 2) == s)
        def _():
            b_out[0, 0] = own_b[4 * s:4 * s + 4]

    scale, factors = start_chain(gram_a, gram_b2)
    chain_step(0, factors[0], False)
    for d in (1, 2, 3):
        recv(rc1.at[d - 1], r_c.at[d]).wait_recv()
    sc[...] = pc[pl.ds(2 * core, 2), x] + rc1[0] + rc1[1] + rc1[2]
    for d in range(8):
        pz = lax.rem(z + d, 8)
        for other in range(2):
            if d == 0 and not other:
                continue
            out.send(
                sc.at[lax.rem(pz // 2, 2), lax.rem(pz, 2)], rc2.at[d], r_c.at[4 + d],
                dev(x, y, pz, core * (1 - other) + (1 - core) * other), pz // 4 == core,
            )
    for q in (1, 2):
        chain_step(q, factors[q], False)
    for d in range(1, 8):
        recv(rc2.at[d], r_c.at[4 + d]).wait_recv()

    @pl.when(core == half)
    def _():
        tc[...] = sc[lax.rem(ia, 2), zlo]

    @pl.when(core != half)
    def _():
        recv(rc2.at[0], r_c.at[4]).wait_recv()
        tc[...] = rc2[0]

    total = tc[...]
    for d in range(1, 8):
        total = total + rc2[d]
    join(3, total * (inverse_a * inverse_b), scale, factors)
    for q in range(3, STEPS - 1):
        chain_step(q, factors[q], True)
    raw = last_step(factors)

    sq1[...] = raw * raw
    for n in range(1, 16):
        out.send(sq1, rq1.at[n - 1], r_q.at[n - 1], at_xy(n))
    total = sq1[...]
    for n in range(1, 16):
        recv(rq1.at[n - 1], r_q.at[n - 1]).wait_recv()
        total = total + rq1[n - 1]
    sq3[...] = total
    for d in range(1, 8):
        out.send(sq3, rq3.at[d - 1], r_q.at[14 + d], at_z(d))
    for d in range(1, 8):
        recv(rq3.at[d - 1], r_q.at[14 + d]).wait_recv()
    total = sq3[...]
    for d in range(7):
        total = total + rq3[d]
    spread = jnp.sqrt(jnp.sum(total, axis=0, keepdims=True) / 1024 + EPS)
    final = raw / spread
    for s in range(2):
        @pl.when(core == s)
        def _():
            c_out[0, 0] = final[4 * s:4 * s + 4]

    out.finish()


def hand_over(a_ref, b_ref, c_ref, a_out, b_out, c_out):
    a_out[...] = a_ref[...]
    b_out[...] = b_ref[...]
    c_out[...] = c_ref[...]


def shards(tensor, factor_b, factor_c):
    vmem = pltpu.VMEM
    dma = pltpu.SemaphoreType.DMA
    scratch = [
        vmem((128, 64, 256), BF16),
        vmem((8, 256, 1024), BF16),
        vmem((128, 64, RANK), BF16),
        vmem((128, 16, RANK), BF16),
        vmem((8, RANK), F32),
        vmem((8, RANK), F32),
        vmem((2, 4, 4, 4, 8, RANK), F32),
        vmem((2, 4, 4, 4, 8, RANK), F32),
        vmem((2, 4, 4, 2, 8, RANK), F32),
        vmem((2, 4, 4, 4, 8, RANK), F32),
        vmem((2, 2, 4, 8, RANK), F32),
        vmem((8, 8, RANK), F32),
        vmem((4, 4, 2, 8, RANK), F32),
        vmem((3, 2, 4, 8, RANK), F32),
        vmem((15, 8, RANK), F32),
        vmem((15, 8, RANK), F32),
        vmem((2, 4, 2, 8, RANK), F32),
        vmem((3, 2, 2, 8, RANK), F32),
        vmem((2, 2, 8, RANK), F32),
        vmem((8, 8, RANK), F32),
        vmem((8, RANK), F32),
        vmem((15, 8, RANK), F32),
        vmem((7, 8, RANK), F32),
        vmem((8, RANK), F32),
        vmem((8, RANK), F32),
        vmem((256, RANK), BF16),
        vmem((256, RANK), BF16),
        vmem((RANK, RANK), F32),
        vmem((RANK, RANK), F32),
        vmem((RANK, RANK), F32),
        vmem((RANK, RANK), F32),
        vmem((RANK, RANK), F32),
        vmem((STEPS, RANK + 16, RANK), BF16),
        vmem((STEPS, RANK, RANK), BF16),
        vmem((RANK, RANK), F32),
        vmem((RANK, RANK), F32),
        vmem((8, RANK), F32),
        vmem((RANK, RANK), F32),
        vmem((2, RANK, RANK), BF16),
        vmem((2, RANK, RANK), BF16),
        vmem((2, 4, 4, 2, 8, RANK), F32),
        vmem((2, 4, 4, 4, 8, RANK), F32),
        vmem((64, RANK), F32),
        vmem((256, RANK), F32),
        vmem((128, RANK), F32),
        vmem((64, RANK), F32),
        vmem((8, RANK), F32),
        dma((192,)),
        dma((1,)),
        dma((4, 4)),
        dma((4, 3)),
        dma((4, 6)),
        dma((4, 4)),
        dma((18,)),
        dma((15,)),
        dma((12,)),
        dma((22,)),
        dma,
    ]
    results = pl.pallas_call(
        kernel,
        out_shape=(
            jax.ShapeDtypeStruct((1, 1, 2, RANK), F32),
            jax.ShapeDtypeStruct((1, 1, 4, RANK), F32),
            jax.ShapeDtypeStruct((1, 1, 4, RANK), F32),
        ),
        in_specs=[
            pl.BlockSpec(memory_space=pl.ANY),
            pl.BlockSpec(memory_space=pltpu.VMEM),
            pl.BlockSpec(memory_space=pltpu.VMEM),
        ],
        out_specs=[pl.BlockSpec(memory_space=pltpu.VMEM)] * 3,
        scratch_shapes=scratch,
        compiler_params=pltpu.CompilerParams(
            collective_id=0, has_side_effects=True, vmem_limit_bytes=58 * 1024 * 1024
        ),
        name="sweep",
    )(tensor, factor_b, factor_c)
    return pl.pallas_call(
        hand_over,
        out_shape=tuple(jax.ShapeDtypeStruct(r.shape, F32) for r in results),
        name="hand_over",
    )(*results)


def solution(mesh):
    in_specs = (
        P("ia", "ja", "ka"),
        P("ja", ("ia", "ka"), None, None),
        P("ka", ("ia", "ja"), None, None),
    )
    out_specs = (
        P("ia", ("ja", "ka"), None, None),
        P("ja", ("ia", "ka"), None, None),
        P("ka", ("ia", "ja"), None, None),
    )
    return jax.shard_map(shards, mesh=mesh, in_specs=in_specs, out_specs=out_specs, check_vma=False)
```

```python
import functools

import jax
import jax.numpy as jnp
from jax import lax
from jax.experimental import pallas as pl
from jax.experimental.pallas import tpu as pltpu
from jax.sharding import PartitionSpec as P

RIDGE = 0.1
EPS = 1e-06
F32 = jnp.float32
BF16 = jnp.bfloat16
RANK = 512
STEPS = 9


def dot(left, right):
    return jnp.dot(left, right, preferred_element_type=F32)


def dot_rows(left, right):
    return lax.dot_general(left, right, (((0,), (0,)), ((), ())), preferred_element_type=F32)


def split_two(value):
    high = value.astype(BF16)
    low = (value - high.astype(F32)).astype(BF16)
    return high, low


def remote(src, dst, send_sem, recv_sem, device):
    return pltpu.make_async_remote_copy(
        src_ref=src,
        dst_ref=dst,
        send_sem=send_sem,
        recv_sem=recv_sem,
        device_id=device,
        device_id_type=pl.DeviceIdType.MESH,
    )


class Sender:
    def __init__(self, sems):
        self.sems = sems
        self.used = 0
        self.pending = []

    def send(self, src, dst, recv_sem, device, cond=None):
        sem = self.sems.at[self.used]
        self.used += 1
        copy = remote(src, dst, sem, recv_sem, device)
        if cond is None:
            copy.start()
        else:
            pl.when(cond)(copy.start)
        self.pending.append((copy, cond))

    def finish(self):
        for copy, cond in self.pending:
            if cond is None:
                copy.wait_send()
            else:
                pl.when(cond)(copy.wait_send)


def kernel(
    t_hbm, fb_ref, fc_ref, a_out, b_out, c_out,
    t_ref, tt, mixed, arep, own8, sib8, g_b, g_c, ga, gb,
    pa, pb, pc, ra1, ra2, rb1, rc0, rc1, sc, rc2, tc,
    rq1, rq3, sq1, sq3,
    mh, ml, gram_b, gram_c, gram_a, gram_b2, dmat, dh, dl, low_b, low_c, yvec, xmat, xh, xl, raw_a, raw_b,
    bblk, cblk, ablk, b2blk, pvec,
    send_sems, r_sib, r_p0, r_p1, r_p2, r_p3, r_a, r_b, r_c, r_q, t_sem,
):
    ia = lax.axis_index("ia")
    ja = lax.axis_index("ja")
    ka = lax.axis_index("ka")
    core = lax.rem(ja, 2)
    zlo = lax.rem(ja // 2, 2)
    x = ja // 4
    y = ka
    z = ia * 2 + zlo
    half = ia // 2
    sel0 = 1 - core

    def dev(px, py, pz, pcore):
        return (pz // 2, px * 4 + lax.rem(pz, 2) * 2 + pcore, py)

    sibling = dev(x, y, z, 1 - core)

    def at_x(d):
        return dev(lax.rem(x + d, 4), y, z, core)

    def at_xy(n):
        return dev(lax.rem(x + n // 4, 4), lax.rem(y + n % 4, 4), z, core)

    def at_iy(n):
        return dev(x, lax.rem(y + n % 4, 4), lax.rem(ia + n // 4, 4) * 2 + zlo, core)

    def at_z(d):
        return dev(x, y, lax.rem(z + d, 8), core)

    load_t = pltpu.make_async_copy(t_hbm, t_ref, t_sem)
    load_t.start()
    out = Sender(send_sems)

    barrier = pltpu.get_barrier_semaphore()
    partners = [sibling]
    partners += [at_xy(n) for n in range(1, 16)]
    partners += [at_z(d) for d in range(1, 8)]
    partners += [dev(x, y, lax.rem(z + d, 8), 1 - core) for d in range(1, 8)]
    partners += [at_iy(n) for n in range(1, 16) if n // 4 and n % 4]
    for partner in partners:
        pl.semaphore_signal(
            barrier, inc=1, device_id=partner, device_id_type=pl.DeviceIdType.MESH
        )

    own8[0:4, :] = fb_ref[0, 0]
    own8[4:8, :] = fc_ref[0, 0]
    pl.semaphore_wait(barrier, len(partners))

    def recv(ref, sem):
        return remote(ref, ref, send_sems.at[0], sem, sibling)

    class Gather:
        def __init__(self, buf, stage, slots, slot, contributes, u_is_x):
            self.buf, self.stage, self.slots, self.slot = buf, stage, slots, slot
            self.contributes = contributes
            self.u_is_x = u_is_x
            self.u = x * u_is_x + y * (1 - u_is_x)
            self.v = y * u_is_x + x * (1 - u_is_x)
            self.p0 = [r_p0.at[stage, n] for n in range(slots)]
            self.p1 = [r_p1.at[stage, n] for n in range(3)]
            self.p2 = [r_p2.at[stage, n] for n in range(6)]
            self.p3 = [r_p3.at[stage, n] for n in range(4)]

        def near(self, du, dv):
            pu, pv = lax.rem(self.u + du + 4, 4), lax.rem(self.v + dv + 4, 4)
            keep = self.u_is_x
            return dev(pu * keep + pv * (1 - keep), pv * keep + pu * (1 - keep), z, core)

        def move(self, ref, sem, device):
            out.send(ref, ref, sem, device)

        def chunk(self, du):
            return self.buf.at[core, self.v, lax.rem(self.u + du + 4, 4)]

        def slab(self, dv, first=None):
            pv = lax.rem(self.v + dv + 4, 4)
            if first is None:
                return self.buf.at[core, pv]
            return self.buf.at[core, pv, pl.ds(first * 2, 2)]

        def p0_send(self):
            ref = self.buf.at[core, self.v, self.u, self.slot]
            for d in (4, 3, 5, 2, 6, 1, 7):
                out.send(ref, ref, r_p0.at[self.stage, self.slot], at_z(d), self.contributes)

        def p0_wait(self):
            for s in range(self.slots):
                other = jnp.logical_not(jnp.logical_and(self.contributes, self.slot == s))
                copy = recv(self.buf.at[core, self.v, self.u, s], self.p0[s])
                pl.when(other)(copy.wait_recv)

        def p1_send(self):
            for d in (2, 1, 3):
                self.move(self.chunk(0), self.p1[d - 1], self.near(d, 0))

        def p1_wait(self):
            for d in (1, 3, 2):
                recv(self.chunk(-d), self.p1[d - 1]).wait_recv()

        def p2_send(self):
            self.move(self.slab(0, 0), self.p2[0], self.near(0, 1))
            self.move(self.slab(0, 1), self.p2[2], self.near(0, -1))
            self.move(self.slab(0, 1), self.p2[1], self.near(0, 1))
            self.move(self.slab(0, 0), self.p2[3], self.near(0, -1))

        def p3_send(self, dv, n):
            self.move(self.slab(dv), self.p3[n], sibling)

        def p2_forward(self):
            recv(self.slab(-1, 0), self.p2[0]).wait_recv()
            self.move(self.slab(-1, 0), self.p2[4], self.near(0, 1))
            recv(self.slab(1, 1), self.p2[2]).wait_recv()
            self.move(self.slab(1, 1), self.p2[5], self.near(0, -1))

        def p2_mid(self):
            recv(self.slab(-1, 1), self.p2[1]).wait_recv()
            self.p3_send(-1, 1)
            recv(self.slab(1, 0), self.p2[3]).wait_recv()
            self.p3_send(1, 2)

        def p2_finish(self):
            recv(self.slab(2, 0), self.p2[4]).wait_recv()
            recv(self.slab(2, 1), self.p2[5]).wait_recv()
            self.p3_send(2, 3)

        def p3_wait(self, n):
            recv(self.buf.at[1 - core, n], self.p3[n]).wait_recv()

        def rows(self, n):
            step = (0, -1, 1, 2)[n]
            other = self.v if self.stage < 2 else self.u
            mine = self.buf[core, lax.rem(self.v + step + 4, 4)]
            theirs = self.buf[1 - core, lax.rem(other + step + 4, 4)]
            count = 4 * self.slots * 8
            return [mine.reshape(count, RANK), theirs.reshape(count, RANK)]

    def close_gram(out_ref, low_ref):
        value = low_ref[...]
        out_ref[...] += value + value.T

    def add_gram(out_ref, parts, first, low_ref=None):
        size = parts[0].shape[0]
        for n, part in enumerate(parts):
            high, low = split_two(part)
            mh[n * size:(n + 1) * size, :] = high
            ml[n * size:(n + 1) * size, :] = low
        high, low = mh[...], ml[...]
        value = dot_rows(high, high)
        cross = dot_rows(high, low)
        if low_ref is None:
            value += cross + dot_rows(low, high)
        else:
            low_ref[...] = cross if first else low_ref[...] + cross
        out_ref[...] = value if first else out_ref[...] + value

    def diagonal(n, value):
        row = lax.broadcasted_iota(jnp.int32, (64, RANK), 0) + n * 64
        col = lax.broadcasted_iota(jnp.int32, (64, RANK), 1)
        return jnp.where(row == col, value, 0.0)

    def normal_gram(ref, count):
        def squares(n, total):
            rs = pl.ds(pl.multiple_of(n * 64, 64), 64)
            return total + jnp.sum(diagonal(n, ref[rs, :]), axis=0, keepdims=True)

        total = lax.fori_loop(0, 8, squares, jnp.zeros((1, RANK), F32))
        inverse = 1.0 / jnp.sqrt(total / count + EPS)

        def body(n, carry):
            rs = pl.ds(pl.multiple_of(n * 64, 64), 64)
            value = ref[rs, :]
            mine = jnp.sum(diagonal(n, value), axis=1, keepdims=True)
            ref[rs, :] = value * (1.0 / jnp.sqrt(mine / count + EPS)) * inverse
            return carry

        lax.fori_loop(0, 8, body, 0)
        return inverse

    def start_chain(one, two):
        def first(n, carry):
            trace, frob = carry
            rs = pl.ds(pl.multiple_of(n * 64, 64), 64)
            value = one[rs, :] * two[rs, :]
            dmat[rs, :] = value
            trace += jnp.sum(diagonal(n, value), axis=0, keepdims=True)
            frob += jnp.sum(value * value, axis=0, keepdims=True)
            return trace, frob

        zero = jnp.zeros((1, RANK), F32)
        trace, frob = lax.fori_loop(0, 8, first, (zero, zero))
        ridge = RIDGE * jnp.sum(trace, axis=1, keepdims=True) / RANK
        top = ridge + jnp.sqrt(jnp.sum(frob, axis=1, keepdims=True))
        scale = 2.0 / (top + ridge)
        sigma = (top + ridge) / (top - ridge)

        def second(n, carry):
            rs = pl.ds(pl.multiple_of(n * 64, 64), 64)
            value = (dmat[rs, :] + diagonal(n, ridge)) * scale
            dmat[rs, :] = value
            high, low = split_two(value)
            dh[0, rs, :] = high
            dl[0, rs, :] = low
            return carry

        lax.fori_loop(0, 8, second, 0)
        factors = []
        for q in range(STEPS):
            twice = 2.0 * sigma * sigma
            factors.append(twice / (twice - 1.0))
            sigma = twice - 1.0
        return scale, factors

    def set_rows(q, value):
        yvec[...] = value
        high, low = split_two(value)
        dh[q, 512:528, :] = jnp.concatenate(
            [high.astype(F32), low.astype(F32)], axis=0
        ).astype(BF16)

    def chain_step(q, factor, with_rows):
        tall = 528 if with_rows else 512
        for n in range(2):
            cs = slice(n * 256, n * 256 + 256)
            high, low = dh[q, 0:tall, :], dl[q]
            right_high, right_low = dh[q, 0:512, cs], dl[q, :, cs]
            one = dot(high, right_high)
            two = dot(high, right_low)
            square = one[0:512] + two[0:512] + dot(low, right_high)
            value = factor * (2.0 * dmat[:, cs] - square)
            dmat[:, cs] = value
            if q + 1 < STEPS - 1:
                high, low = split_two(value)
                dh[q + 1, 0:512, cs] = high
                dl[q + 1, :, cs] = low
            else:
                row = lax.broadcasted_iota(jnp.int32, (RANK, 256), 0)
                col = lax.broadcasted_iota(jnp.int32, (RANK, 256), 1) + n * 256
                dh[q + 1, 0:512, cs] = (jnp.where(row == col, 1.0, 0.0) - value).astype(BF16)
            if with_rows:
                value = one[512:520] + one[520:528] + two[512:520]
                value = factor * (2.0 * yvec[:, cs] - value)
                yvec[:, cs] = value
                high, low = split_two(value)
                dh[q + 1, 512:528, cs] = jnp.concatenate(
                    [high.astype(F32), low.astype(F32)], axis=0
                ).astype(BF16)

    def start_inverse(scale, factor):
        def body(n, carry):
            rs = pl.ds(pl.multiple_of(n * 64, 64), 64)
            value = (diagonal(n, 2.0) - dmat[rs, :]) * (scale * factor)
            xmat[rs, :] = value
            high, low = split_two(value)
            xh[1, rs, :] = high
            xl[1, rs, :] = low
            return carry

        lax.fori_loop(0, 8, body, 0)

    def inverse_step(q, factor):
        now, later = q % 2, (q + 1) % 2
        for n in range(2):
            cs = slice(n * 256, n * 256 + 256)
            right_high, right_low = dh[q, 0:512, cs], dl[q, :, cs]
            value = dot(xh[now], right_high)
            if q < STEPS - 1:
                value += dot(xh[now], right_low) + dot(xl[now], right_high)
                value = factor * (2.0 * xmat[:, cs] - value)
            else:
                value = factor * (xmat[:, cs] + value)
            xmat[:, cs] = value
            high, low = split_two(value)
            xh[later, :, cs] = high
            xl[later, :, cs] = low

    def times_inverse(rows):
        high, low = split_two(rows)
        last = STEPS % 2
        return dot(high, xh[last]) + dot(high, xl[last]) + dot(low, xh[last])

    def both_steps(q, factors):
        inverse_step(q, factors[q])
        if q < STEPS - 1:
            chain_step(q, factors[q], False)

    def apply_step(q, factor, value):
        high, low = split_two(value)
        both = jnp.concatenate([high.astype(F32), low.astype(F32)], axis=0).astype(BF16)
        wide = dot(both, dh[q, 0:512, :])
        narrow = dot(both, dl[q])
        return factor * (2.0 * value - (wide[0:8] + wide[8:16] + narrow[0:8]))

    def join(q, rows, scale, factors):
        value = rows * scale
        for n in range(q):
            value = apply_step(n, factors[n], value)
        set_rows(q, value)

    def last_step(factors):
        value = yvec[...]
        high, low = split_two(value)
        both = jnp.concatenate([high.astype(F32), low.astype(F32)], axis=0).astype(BF16)
        wide = dot(both, dh[STEPS - 1, 0:512, :])
        return factors[STEPS - 1] * (value + wide[0:8] + wide[8:16])

    yvec[...] = jnp.zeros_like(yvec)
    to_sib = remote(own8, sib8, send_sems.at[0], r_sib.at[0], sibling)
    to_sib.start()
    out.used = 1
    out.pending.append((to_sib, None))
    to_sib.wait_recv()
    slot = lax.rem(ia, 2) * 2 + zlo
    contributes = core == half
    all_b = Gather(g_b, 0, 4, slot, contributes, 0)
    all_c = Gather(g_c, 1, 4, slot, contributes, 1)

    for c in range(2):
        @pl.when(jnp.logical_and(contributes, core == c))
        def _():
            for gather, at in ((all_b, 0), (all_c, 4)):
                mine = own8[at:at + 4, :]
                theirs = sib8[at:at + 4, :]
                first, second = (mine, theirs) if c == 0 else (theirs, mine)
                gather.buf[core, gather.v, gather.u, slot, 0:4, :] = first
                gather.buf[core, gather.v, gather.u, slot, 4:8, :] = second

    both = (all_b, all_c)

    def turn(g, carry):
        tt[g] = t_ref[pl.ds(g * 16, 16)].reshape(1024, 256).T
        return carry

    for gather in both:
        gather.p0_send()
    load_t.wait()
    lax.fori_loop(0, 4, turn, 0)
    for gather in both:
        gather.p0_wait()
        gather.p1_send()
    lax.fori_loop(4, 8, turn, 0)
    for gather in both:
        gather.p1_wait()
        gather.p2_send()
        gather.p3_send(0, 0)

    def fill_c(n, carry):
        pia, rest = n // 8, lax.rem(n, 8)
        px, pzlo = rest // 2, lax.rem(rest, 2)
        ps = lax.rem(pia, 2) * 2 + pzlo
        cblk[pl.ds(pl.multiple_of(n * 8, 8), 8), :] = g_c[pia // 2, y, px, ps]
        return carry

    def fill_b(n, carry):
        pia, py = n // 2, lax.rem(n, 2) * 2
        ps = lax.rem(pia, 2) * 2 + zlo
        one, two = g_b[pia // 2, x, py, ps], g_b[pia // 2, x, py + 1, ps]

        @pl.when(core == 0)
        def _():
            pvec[0:4, :] = one[0:4]
            pvec[4:8, :] = two[0:4]

        @pl.when(core == 1)
        def _():
            pvec[0:4, :] = one[4:8]
            pvec[4:8, :] = two[4:8]

        bblk[pl.ds(pl.multiple_of(n * 8, 8), 8), :] = pvec[...].astype(BF16).astype(F32)
        return carry

    for gather in both:
        gather.p3_wait(0)
    lax.fori_loop(0, 32, fill_c, 0)
    lax.fori_loop(0, 8, fill_b, 0)

    def contract(g, carry):
        half_c = cblk[...].astype(BF16)
        weight = bblk[...]
        parts = []
        for s in range(2):
            piece = t_ref[pl.ds(g * 8 + s * 4, 4)].reshape(256, 256)
            value = dot(piece, half_c).reshape(4, 64, RANK)
            mixed[pl.ds(g * 8 + s * 4, 4)] = value.astype(BF16)
            parts.append(jnp.sum(value * weight[None], axis=1))
        px = g // 4
        pa[lax.rem(px, 2), px // 2, lax.rem(g, 4)] = jnp.concatenate(parts, axis=0)
        return carry

    lax.fori_loop(0, 4, contract, 0)
    for gather in both:
        gather.p2_forward()
    lax.fori_loop(4, 10, contract, 0)
    for gather in both:
        gather.p2_mid()
    lax.fori_loop(10, 16, contract, 0)

    beside = 1 - zlo
    out.send(pa.at[zlo], ra1.at[0], r_a.at[0], sibling, core != half)
    out.send(
        pa.at[beside], ra1.at[1], r_a.at[1], dev(x, y, ia * 2 + beside, core), core == half
    )
    out.send(
        pa.at[beside], ra1.at[2], r_a.at[2], dev(x, y, ia * 2 + beside, 1 - core), core != half
    )
    a_owner = jnp.logical_and(core == half, lax.rem(x, 2) == zlo)
    add_gram(gram_b, all_b.rows(0), True, low_b)
    add_gram(gram_c, all_c.rows(0), True, low_c)
    for gather in both:
        gather.p2_finish()

    all_b.p3_wait(1)
    add_gram(gram_b, all_b.rows(1), False, low_b)
    all_c.p3_wait(1)
    add_gram(gram_c, all_c.rows(1), False, low_c)

    @pl.when(core == half)
    def _():
        for m in range(3):
            recv(ra1.at[m], r_a.at[m]).wait_recv()
        pa[zlo] += ra1[0] + ra1[1] + ra1[2]

    for n in range(1, 16):
        px, py = lax.rem(x + n // 4, 4), lax.rem(y + n % 4, 4)
        out.send(
            pa.at[zlo, px // 2, py], ra2.at[n - 1], r_a.at[2 + n], at_xy(n),
            jnp.logical_and(core == half, lax.rem(px, 2) == zlo),
        )
    all_b.p3_wait(2)
    add_gram(gram_b, all_b.rows(2), False, low_b)
    all_c.p3_wait(2)
    add_gram(gram_c, all_c.rows(2), False, low_c)

    all_b.p3_wait(3)
    add_gram(gram_b, all_b.rows(3), False, low_b)
    all_c.p3_wait(3)
    add_gram(gram_c, all_c.rows(3), False, low_c)
    aslot = lax.rem(ia, 2)
    all_a = Gather(ga, 2, 2, aslot, a_owner, sel0)

    def invert(one, two, gather, begin):
        scale, factors = start_chain(one, two)
        start_inverse(scale, factors[0])
        early = begin()

        def first_axis():
            gather.p0_wait()
            gather.p1_send()

        def second_axis():
            gather.p1_wait()
            gather.p2_send()
            gather.p3_send(0, 0)

        if early:
            first_axis()
        chain_step(0, factors[0], False)
        both_steps(1, factors)
        if not early:
            first_axis()
        both_steps(2, factors)
        if early:
            second_axis()
        both_steps(3, factors)
        if not early:
            second_axis()
        both_steps(4, factors)
        if early:
            gather.p2_forward()
        both_steps(5, factors)
        if early:
            gather.p2_mid()
        else:
            gather.p2_forward()
        both_steps(6, factors)
        if not early:
            gather.p2_mid()
        gather.p2_finish()
        both_steps(7, factors)
        both_steps(8, factors)
        for n in range(4):
            gather.p3_wait(n)

    def begin_a():
        @pl.when(a_owner)
        def _():
            total = pa[zlo, x // 2, y]
            for n in range(1, 16):
                recv(ra2.at[n - 1], r_a.at[2 + n]).wait_recv()
                total = total + ra2[n - 1]
            ga[core, all_a.v, all_a.u, aslot] = total

        all_a.p0_send()
        return False

    close_gram(gram_b, low_b)
    close_gram(gram_c, low_c)
    invert(gram_b, gram_c, all_a, begin_a)
    for n in range(2):
        raw_a[n] = times_inverse(ga[n].reshape(256, RANK)).reshape(4, 4, 2, 8, RANK)

    def fill_a(n, carry):
        px, py = n // 4, lax.rem(n, 4)
        pu = px * (1 - half) + py * half
        pv = py * (1 - half) + px * half
        ablk[pl.ds(pl.multiple_of(n * 8, 8), 8), :] = raw_a[half, pv, pu, aslot]
        return carry

    lax.fori_loop(0, 16, fill_a, 0)

    def second_mode(g, total):
        rows = ablk[pl.ds(pl.multiple_of(g * 8, 8), 8), :].astype(BF16).astype(F32)
        for s in range(8):
            total = total + mixed[g * 8 + s].astype(F32) * rows[s:s + 1, :]
        return total

    part_b = lax.fori_loop(0, 16, second_mode, jnp.zeros((64, RANK), F32))
    pb[...] = part_b.reshape(8, 8, RANK)
    for n in range(1, 16):
        pia, py = lax.rem(ia + n // 4, 4), lax.rem(y + n % 4, 4)
        out.send(
            pb.at[lax.rem(pia, 2) * 4 + py], rb1.at[n - 1], r_b.at[n - 1], at_iy(n),
            pia // 2 == core,
        )
    for n in range(2):
        add_gram(gram_a, [raw_a[n].reshape(256, RANK)], n == 0)

    all_b2 = Gather(gb, 3, 4, slot, contributes, sel0)

    @pl.when(core == half)
    def _():
        rows = pb[lax.rem(ia, 2) * 4 + y]
        for n in range(1, 16):
            recv(rb1.at[n - 1], r_b.at[n - 1]).wait_recv()
            rows = rows + rb1[n - 1]
        gb[core, all_b2.v, all_b2.u, slot] = rows

    all_b2.p0_send()
    inverse_a = normal_gram(gram_a, 512)

    def repeat_a(g, carry):
        rows = ablk[pl.ds(pl.multiple_of(g * 8, 8), 8), :].astype(BF16).astype(F32)
        for s in range(8):
            arep[g * 8 + s] = jnp.broadcast_to(rows[s:s + 1, :], (16, RANK)).astype(BF16)
        return carry

    lax.fori_loop(0, 16, repeat_a, 0)

    own_a = ablk[pl.ds(pl.multiple_of(ja * 8, 8), 8), :] * inverse_a
    for s in range(4):
        @pl.when(ka == s)
        def _():
            a_out[0, 0] = own_a[2 * s:2 * s + 2]

    invert(gram_a, gram_c, all_b2, lambda: True)

    def fill_b2(n, carry):
        py = lax.rem(n, 4)
        pu = x * sel0 + py * core
        pv = py * sel0 + x * core
        rows = gb[core, pv, pu, (n // 4) * 2 + zlo] * inverse_a
        b2blk[pl.ds(pl.multiple_of(n * 8, 8), 8), :] = rows
        return carry

    lax.fori_loop(0, 8, fill_b2, 0)
    b2blk[...] = times_inverse(b2blk[...])

    pc[...] = jnp.zeros_like(pc)

    def third_mode(g, carry):
        half_b2 = b2blk[...].astype(BF16).reshape(4, 16, RANK)
        weight = jnp.concatenate(
            [(half_b2 * arep[g * 16 + n][None]).reshape(64, RANK) for n in range(16)], axis=0
        )
        pc[...] += dot(tt[g], weight).reshape(4, 4, 2, 8, RANK)
        return carry

    lax.fori_loop(0, 8, third_mode, 0)
    out.send(pc.at[pl.ds(2 * (1 - core), 2)], rc0, r_c.at[0], sibling)

    def all_rows(n, carry):
        h, pair = n // 2, lax.rem(n, 2) * 2
        rows = times_inverse(gb[h, pl.ds(pair, 2)].reshape(256, RANK) * inverse_a)
        high, low = split_two(rows)
        mh[...] = high
        ml[...] = low
        high, low = mh[...], ml[...]
        gram_b2[...] += dot_rows(high, high)
        low_b[...] += dot_rows(high, low)
        return carry

    gram_b2[...] = jnp.zeros_like(gram_b2)
    low_b[...] = jnp.zeros_like(low_b)
    lax.fori_loop(0, 3, all_rows, 0)
    recv(rc0, r_c.at[0]).wait_recv()
    pc[pl.ds(2 * core, 2)] += rc0[...]
    for d in (1, 2, 3):
        out.send(
            pc.at[pl.ds(2 * core, 2), lax.rem(x + d, 4)], rc1.at[d - 1], r_c.at[d], at_x(d)
        )
    lax.fori_loop(3, 4, all_rows, 0)
    close_gram(gram_b2, low_b)
    inverse_b = normal_gram(gram_b2, 1024)
    own_b = b2blk[pl.ds(pl.multiple_of((ia * 2 + ka // 2) * 8, 8), 8), :] * inverse_b
    for s in range(2):
        @pl.when(lax.rem(ka, 2) == s)
        def _():
            b_out[0, 0] = own_b[4 * s:4 * s + 4]

    scale, factors = start_chain(gram_a, gram_b2)
    for q in (0, 1):
        chain_step(q, factors[q], False)
    for d in (1, 2, 3):
        recv(rc1.at[d - 1], r_c.at[d]).wait_recv()
    sc[...] = pc[pl.ds(2 * core, 2), x] + rc1[0] + rc1[1] + rc1[2]
    for d in range(8):
        pz = lax.rem(z + d, 8)
        for other in range(2):
            if d == 0 and not other:
                continue
            out.send(
                sc.at[lax.rem(pz // 2, 2), lax.rem(pz, 2)], rc2.at[d], r_c.at[4 + d],
                dev(x, y, pz, core * (1 - other) + (1 - core) * other), pz // 4 == core,
            )
    for q in (2, 3, 4):
        chain_step(q, factors[q], False)
    for d in range(1, 8):
        recv(rc2.at[d], r_c.at[4 + d]).wait_recv()

    @pl.when(core == half)
    def _():
        tc[...] = sc[lax.rem(ia, 2), zlo]

    @pl.when(core != half)
    def _():
        recv(rc2.at[0], r_c.at[4]).wait_recv()
        tc[...] = rc2[0]

    total = tc[...]
    for d in range(1, 8):
        total = total + rc2[d]
    join(5, total * (inverse_a * inverse_b), scale, factors)
    for q in range(5, STEPS - 1):
        chain_step(q, factors[q], True)
    raw = last_step(factors)

    sq1[...] = raw * raw
    for n in range(1, 16):
        out.send(sq1, rq1.at[n - 1], r_q.at[n - 1], at_xy(n))
    total = sq1[...]
    for n in range(1, 16):
        recv(rq1.at[n - 1], r_q.at[n - 1]).wait_recv()
        total = total + rq1[n - 1]
    sq3[...] = total
    for d in range(1, 8):
        out.send(sq3, rq3.at[d - 1], r_q.at[14 + d], at_z(d))
    out.finish()
    for d in range(1, 8):
        recv(rq3.at[d - 1], r_q.at[14 + d]).wait_recv()
    total = sq3[...]
    for d in range(7):
        total = total + rq3[d]
    spread = jnp.sqrt(jnp.sum(total, axis=0, keepdims=True) / 1024 + EPS)
    final = raw / spread
    for s in range(2):
        @pl.when(core == s)
        def _():
            c_out[0, 0] = final[4 * s:4 * s + 4]


def hand_over(a_ref, b_ref, c_ref, a_out, b_out, c_out):
    a_out[...] = a_ref[...]
    b_out[...] = b_ref[...]
    c_out[...] = c_ref[...]


def shards(tensor, factor_b, factor_c):
    vmem = pltpu.VMEM
    dma = pltpu.SemaphoreType.DMA
    scratch = [
        vmem((128, 64, 256), BF16),
        vmem((8, 256, 1024), BF16),
        vmem((128, 64, RANK), BF16),
        vmem((128, 16, RANK), BF16),
        vmem((8, RANK), F32),
        vmem((8, RANK), F32),
        vmem((2, 4, 4, 4, 8, RANK), F32),
        vmem((2, 4, 4, 4, 8, RANK), F32),
        vmem((2, 4, 4, 2, 8, RANK), F32),
        vmem((2, 4, 4, 4, 8, RANK), F32),
        vmem((2, 2, 4, 8, RANK), F32),
        vmem((8, 8, RANK), F32),
        vmem((4, 4, 2, 8, RANK), F32),
        vmem((3, 2, 4, 8, RANK), F32),
        vmem((15, 8, RANK), F32),
        vmem((15, 8, RANK), F32),
        vmem((2, 4, 2, 8, RANK), F32),
        vmem((3, 2, 2, 8, RANK), F32),
        vmem((2, 2, 8, RANK), F32),
        vmem((8, 8, RANK), F32),
        vmem((8, RANK), F32),
        vmem((15, 8, RANK), F32),
        vmem((7, 8, RANK), F32),
        vmem((8, RANK), F32),
        vmem((8, RANK), F32),
        vmem((256, RANK), BF16),
        vmem((256, RANK), BF16),
        vmem((RANK, RANK), F32),
        vmem((RANK, RANK), F32),
        vmem((RANK, RANK), F32),
        vmem((RANK, RANK), F32),
        vmem((RANK, RANK), F32),
        vmem((STEPS, RANK + 16, RANK), BF16),
        vmem((STEPS, RANK, RANK), BF16),
        vmem((RANK, RANK), F32),
        vmem((RANK, RANK), F32),
        vmem((8, RANK), F32),
        vmem((RANK, RANK), F32),
        vmem((2, RANK, RANK), BF16),
        vmem((2, RANK, RANK), BF16),
        vmem((2, 4, 4, 2, 8, RANK), F32),
        vmem((2, 4, 4, 4, 8, RANK), F32),
        vmem((64, RANK), F32),
        vmem((256, RANK), F32),
        vmem((128, RANK), F32),
        vmem((64, RANK), F32),
        vmem((8, RANK), F32),
        dma((192,)),
        dma((1,)),
        dma((4, 4)),
        dma((4, 3)),
        dma((4, 6)),
        dma((4, 4)),
        dma((18,)),
        dma((15,)),
        dma((12,)),
        dma((22,)),
        dma,
    ]
    results = pl.pallas_call(
        kernel,
        out_shape=(
            jax.ShapeDtypeStruct((1, 1, 2, RANK), F32),
            jax.ShapeDtypeStruct((1, 1, 4, RANK), F32),
            jax.ShapeDtypeStruct((1, 1, 4, RANK), F32),
        ),
        in_specs=[
            pl.BlockSpec(memory_space=pl.ANY),
            pl.BlockSpec(memory_space=pltpu.VMEM),
            pl.BlockSpec(memory_space=pltpu.VMEM),
        ],
        out_specs=[pl.BlockSpec(memory_space=pltpu.VMEM)] * 3,
        scratch_shapes=scratch,
        compiler_params=pltpu.CompilerParams(
            collective_id=0, has_side_effects=True, vmem_limit_bytes=58 * 1024 * 1024
        ),
        name="sweep",
    )(tensor, factor_b, factor_c)
    return pl.pallas_call(
        hand_over,
        out_shape=tuple(jax.ShapeDtypeStruct(r.shape, F32) for r in results),
        name="hand_over",
    )(*results)


def solution(mesh):
    in_specs = (
        P("ia", "ja", "ka"),
        P("ja", ("ia", "ka"), None, None),
        P("ka", ("ia", "ja"), None, None),
    )
    out_specs = (
        P("ia", ("ja", "ka"), None, None),
        P("ja", ("ia", "ka"), None, None),
        P("ka", ("ia", "ja"), None, None),
    )
    return jax.shard_map(shards, mesh=mesh, in_specs=in_specs, out_specs=out_specs, check_vma=False)
```

```python
import functools

import jax
import jax.numpy as jnp
from jax import lax
from jax.experimental import pallas as pl
from jax.experimental.pallas import tpu as pltpu
from jax.sharding import PartitionSpec as P

RIDGE = 0.1
EPS = 1e-06
F32 = jnp.float32
BF16 = jnp.bfloat16
RANK = 512
STEPS = 9


def dot(left, right):
    return jnp.dot(left, right, preferred_element_type=F32)


def dot_rows(left, right):
    return lax.dot_general(left, right, (((0,), (0,)), ((), ())), preferred_element_type=F32)


def split_two(value):
    high = value.astype(BF16)
    low = (value - high.astype(F32)).astype(BF16)
    return high, low


def remote(src, dst, send_sem, recv_sem, device):
    return pltpu.make_async_remote_copy(
        src_ref=src,
        dst_ref=dst,
        send_sem=send_sem,
        recv_sem=recv_sem,
        device_id=device,
        device_id_type=pl.DeviceIdType.MESH,
    )


class Sender:
    def __init__(self, sems):
        self.sems = sems
        self.used = 0
        self.pending = []

    def send(self, src, dst, recv_sem, device, cond=None):
        sem = self.sems.at[self.used]
        self.used += 1
        copy = remote(src, dst, sem, recv_sem, device)
        if cond is None:
            copy.start()
        else:
            pl.when(cond)(copy.start)
        self.pending.append((copy, cond))

    def finish(self):
        for copy, cond in self.pending:
            if cond is None:
                copy.wait_send()
            else:
                pl.when(cond)(copy.wait_send)


def kernel(
    t_hbm, fb_ref, fc_ref, a_out, b_out, c_out,
    t_ref, tt, mixed, arep, own8, sib8, g_b, g_c, ga, gb,
    pa, pb, pc, ra1, ra2, rb1, rc0, rc1, sc, rc2, tc,
    rq1, rq3, sq1, sq3,
    mh, ml, gram_b, gram_c, gram_a, gram_b2, dmat, dh, dl, low_b, low_c, yvec, xmat, xh, xl, raw_a, raw_b,
    bblk, cblk, ablk, b2blk, pvec,
    send_sems, r_sib, r_p0, r_p1, r_p2, r_p3, r_a, r_b, r_c, r_q, t_sem,
):
    ia = lax.axis_index("ia")
    ja = lax.axis_index("ja")
    ka = lax.axis_index("ka")
    core = lax.rem(ja, 2)
    zlo = lax.rem(ja // 2, 2)
    x = ja // 4
    y = ka
    z = ia * 2 + zlo
    half = ia // 2
    sel0 = 1 - core

    def dev(px, py, pz, pcore):
        return (pz // 2, px * 4 + lax.rem(pz, 2) * 2 + pcore, py)

    sibling = dev(x, y, z, 1 - core)

    def at_x(d):
        return dev(lax.rem(x + d, 4), y, z, core)

    def at_xy(n):
        return dev(lax.rem(x + n // 4, 4), lax.rem(y + n % 4, 4), z, core)

    def at_iy(n):
        return dev(x, lax.rem(y + n % 4, 4), lax.rem(ia + n // 4, 4) * 2 + zlo, core)

    def at_z(d):
        return dev(x, y, lax.rem(z + d, 8), core)

    load_t = pltpu.make_async_copy(t_hbm, t_ref, t_sem)
    load_t.start()
    out = Sender(send_sems)

    barrier = pltpu.get_barrier_semaphore()
    partners = [sibling]
    partners += [at_xy(n) for n in range(1, 16)]
    partners += [at_z(d) for d in range(1, 8)]
    partners += [dev(x, y, lax.rem(z + d, 8), 1 - core) for d in range(1, 8)]
    partners += [at_iy(n) for n in range(1, 16) if n // 4 and n % 4]
    for partner in partners:
        pl.semaphore_signal(
            barrier, inc=1, device_id=partner, device_id_type=pl.DeviceIdType.MESH
        )

    own8[0:4, :] = fb_ref[0, 0]
    own8[4:8, :] = fc_ref[0, 0]
    pl.semaphore_wait(barrier, len(partners))

    def recv(ref, sem):
        return remote(ref, ref, send_sems.at[0], sem, sibling)

    class Gather:
        def __init__(self, buf, stage, slots, slot, contributes, u_is_x):
            self.buf, self.stage, self.slots, self.slot = buf, stage, slots, slot
            self.contributes = contributes
            self.u_is_x = u_is_x
            self.u = x * u_is_x + y * (1 - u_is_x)
            self.v = y * u_is_x + x * (1 - u_is_x)
            self.p0 = [r_p0.at[stage, n] for n in range(slots)]
            self.p1 = [r_p1.at[stage, n] for n in range(3)]
            self.p2 = [r_p2.at[stage, n] for n in range(6)]
            self.p3 = [r_p3.at[stage, n] for n in range(4)]

        def near(self, du, dv):
            pu, pv = lax.rem(self.u + du + 4, 4), lax.rem(self.v + dv + 4, 4)
            keep = self.u_is_x
            return dev(pu * keep + pv * (1 - keep), pv * keep + pu * (1 - keep), z, core)

        def move(self, ref, sem, device):
            out.send(ref, ref, sem, device)

        def chunk(self, du):
            return self.buf.at[core, self.v, lax.rem(self.u + du + 4, 4)]

        def slab(self, dv, first=None):
            pv = lax.rem(self.v + dv + 4, 4)
            if first is None:
                return self.buf.at[core, pv]
            return self.buf.at[core, pv, pl.ds(first * 2, 2)]

        def p0_send(self):
            ref = self.buf.at[core, self.v, self.u, self.slot]
            for d in (4, 3, 5, 2, 6, 1, 7):
                out.send(ref, ref, r_p0.at[self.stage, self.slot], at_z(d), self.contributes)

        def p0_wait(self):
            for s in range(self.slots):
                other = jnp.logical_not(jnp.logical_and(self.contributes, self.slot == s))
                copy = recv(self.buf.at[core, self.v, self.u, s], self.p0[s])
                pl.when(other)(copy.wait_recv)

        def p1_send(self):
            for d in (2, 1, 3):
                self.move(self.chunk(0), self.p1[d - 1], self.near(d, 0))

        def p1_wait(self):
            for d in (1, 3, 2):
                recv(self.chunk(-d), self.p1[d - 1]).wait_recv()

        def p2_send(self):
            self.move(self.slab(0, 0), self.p2[0], self.near(0, 1))
            self.move(self.slab(0, 1), self.p2[2], self.near(0, -1))
            self.move(self.slab(0, 1), self.p2[1], self.near(0, 1))
            self.move(self.slab(0, 0), self.p2[3], self.near(0, -1))

        def p3_send(self, dv, n):
            self.move(self.slab(dv), self.p3[n], sibling)

        def p2_forward(self):
            recv(self.slab(-1, 0), self.p2[0]).wait_recv()
            self.move(self.slab(-1, 0), self.p2[4], self.near(0, 1))
            recv(self.slab(1, 1), self.p2[2]).wait_recv()
            self.move(self.slab(1, 1), self.p2[5], self.near(0, -1))

        def p2_mid(self):
            recv(self.slab(-1, 1), self.p2[1]).wait_recv()
            self.p3_send(-1, 1)
            recv(self.slab(1, 0), self.p2[3]).wait_recv()
            self.p3_send(1, 2)

        def p2_finish(self):
            recv(self.slab(2, 0), self.p2[4]).wait_recv()
            recv(self.slab(2, 1), self.p2[5]).wait_recv()
            self.p3_send(2, 3)

        def p3_wait(self, n):
            recv(self.buf.at[1 - core, n], self.p3[n]).wait_recv()

        def rows(self, n):
            step = (0, -1, 1, 2)[n]
            other = self.v if self.stage < 2 else self.u
            mine = self.buf[core, lax.rem(self.v + step + 4, 4)]
            theirs = self.buf[1 - core, lax.rem(other + step + 4, 4)]
            count = 4 * self.slots * 8
            return [mine.reshape(count, RANK), theirs.reshape(count, RANK)]

    def close_gram(out_ref, low_ref):
        value = low_ref[...]
        out_ref[...] += value + value.T

    def add_gram(out_ref, parts, first, low_ref=None):
        size = parts[0].shape[0]
        for n, part in enumerate(parts):
            high, low = split_two(part)
            mh[n * size:(n + 1) * size, :] = high
            ml[n * size:(n + 1) * size, :] = low
        high, low = mh[...], ml[...]
        value = dot_rows(high, high)
        cross = dot_rows(high, low)
        if low_ref is None:
            value += cross + dot_rows(low, high)
        else:
            low_ref[...] = cross if first else low_ref[...] + cross
        out_ref[...] = value if first else out_ref[...] + value

    def diagonal(n, value):
        row = lax.broadcasted_iota(jnp.int32, (64, RANK), 0) + n * 64
        col = lax.broadcasted_iota(jnp.int32, (64, RANK), 1)
        return jnp.where(row == col, value, 0.0)

    def normal_gram(ref, count):
        def squares(n, total):
            rs = pl.ds(pl.multiple_of(n * 64, 64), 64)
            return total + jnp.sum(diagonal(n, ref[rs, :]), axis=0, keepdims=True)

        total = lax.fori_loop(0, 8, squares, jnp.zeros((1, RANK), F32))
        inverse = 1.0 / jnp.sqrt(total / count + EPS)

        def body(n, carry):
            rs = pl.ds(pl.multiple_of(n * 64, 64), 64)
            value = ref[rs, :]
            mine = jnp.sum(diagonal(n, value), axis=1, keepdims=True)
            ref[rs, :] = value * (1.0 / jnp.sqrt(mine / count + EPS)) * inverse
            return carry

        lax.fori_loop(0, 8, body, 0)
        return inverse

    def start_chain(one, two):
        def first(n, carry):
            trace, frob = carry
            rs = pl.ds(pl.multiple_of(n * 64, 64), 64)
            value = one[rs, :] * two[rs, :]
            dmat[rs, :] = value
            trace += jnp.sum(diagonal(n, value), axis=0, keepdims=True)
            frob += jnp.sum(value * value, axis=0, keepdims=True)
            return trace, frob

        zero = jnp.zeros((1, RANK), F32)
        trace, frob = lax.fori_loop(0, 8, first, (zero, zero))
        ridge = RIDGE * jnp.sum(trace, axis=1, keepdims=True) / RANK
        top = ridge + jnp.sqrt(jnp.sum(frob, axis=1, keepdims=True))
        scale = 2.0 / (top + ridge)
        sigma = (top + ridge) / (top - ridge)

        def second(n, carry):
            rs = pl.ds(pl.multiple_of(n * 64, 64), 64)
            value = (dmat[rs, :] + diagonal(n, ridge)) * scale
            dmat[rs, :] = value
            high, low = split_two(value)
            dh[0, rs, :] = high
            dl[0, rs, :] = low
            return carry

        lax.fori_loop(0, 8, second, 0)
        factors = []
        for q in range(STEPS):
            twice = 2.0 * sigma * sigma
            factors.append(twice / (twice - 1.0))
            sigma = twice - 1.0
        return scale, factors

    def set_rows(q, value):
        yvec[...] = value
        high, low = split_two(value)
        dh[q, 512:528, :] = jnp.concatenate(
            [high.astype(F32), low.astype(F32)], axis=0
        ).astype(BF16)

    def chain_step(q, factor, with_rows):
        tall = 528 if with_rows else 512
        for n in range(2):
            cs = slice(n * 256, n * 256 + 256)
            high, low = dh[q, 0:tall, :], dl[q]
            right_high, right_low = dh[q, 0:512, cs], dl[q, :, cs]
            one = dot(high, right_high)
            two = dot(high, right_low)
            square = one[0:512] + two[0:512] + dot(low, right_high)
            value = factor * (2.0 * dmat[:, cs] - square)
            dmat[:, cs] = value
            if q + 1 < STEPS - 1:
                high, low = split_two(value)
                dh[q + 1, 0:512, cs] = high
                dl[q + 1, :, cs] = low
            else:
                row = lax.broadcasted_iota(jnp.int32, (RANK, 256), 0)
                col = lax.broadcasted_iota(jnp.int32, (RANK, 256), 1) + n * 256
                dh[q + 1, 0:512, cs] = (jnp.where(row == col, 1.0, 0.0) - value).astype(BF16)
            if with_rows:
                value = one[512:520] + one[520:528] + two[512:520]
                value = factor * (2.0 * yvec[:, cs] - value)
                yvec[:, cs] = value
                high, low = split_two(value)
                dh[q + 1, 512:528, cs] = jnp.concatenate(
                    [high.astype(F32), low.astype(F32)], axis=0
                ).astype(BF16)

    def start_inverse(scale, factor):
        def body(n, carry):
            rs = pl.ds(pl.multiple_of(n * 64, 64), 64)
            value = (diagonal(n, 2.0) - dmat[rs, :]) * (scale * factor)
            xmat[rs, :] = value
            high, low = split_two(value)
            xh[1, rs, :] = high
            xl[1, rs, :] = low
            return carry

        lax.fori_loop(0, 8, body, 0)

    def inverse_step(q, factor):
        now, later = q % 2, (q + 1) % 2
        for n in range(2):
            cs = slice(n * 256, n * 256 + 256)
            right_high, right_low = dh[q, 0:512, cs], dl[q, :, cs]
            value = dot(xh[now], right_high)
            if q < STEPS - 1:
                value += dot(xh[now], right_low) + dot(xl[now], right_high)
                value = factor * (2.0 * xmat[:, cs] - value)
            else:
                value = factor * (xmat[:, cs] + value)
            xmat[:, cs] = value
            high, low = split_two(value)
            xh[later, :, cs] = high
            xl[later, :, cs] = low

    def times_inverse(rows):
        high, low = split_two(rows)
        last = STEPS % 2
        return dot(high, xh[last]) + dot(high, xl[last]) + dot(low, xh[last])

    def both_steps(q, factors):
        inverse_step(q, factors[q])
        if q < STEPS - 1:
            chain_step(q, factors[q], False)

    def apply_step(q, factor, value):
        high, low = split_two(value)
        both = jnp.concatenate([high.astype(F32), low.astype(F32)], axis=0).astype(BF16)
        wide = dot(both, dh[q, 0:512, :])
        narrow = dot(both, dl[q])
        return factor * (2.0 * value - (wide[0:8] + wide[8:16] + narrow[0:8]))

    def join(q, rows, scale, factors):
        value = rows * scale
        for n in range(q):
            value = apply_step(n, factors[n], value)
        set_rows(q, value)

    def last_step(factors):
        value = yvec[...]
        high, low = split_two(value)
        both = jnp.concatenate([high.astype(F32), low.astype(F32)], axis=0).astype(BF16)
        wide = dot(both, dh[STEPS - 1, 0:512, :])
        return factors[STEPS - 1] * (value + wide[0:8] + wide[8:16])

    yvec[...] = jnp.zeros_like(yvec)
    to_sib = remote(own8, sib8, send_sems.at[0], r_sib.at[0], sibling)
    to_sib.start()
    out.used = 1
    out.pending.append((to_sib, None))
    to_sib.wait_recv()
    slot = lax.rem(ia, 2) * 2 + zlo
    contributes = core == half
    all_b = Gather(g_b, 0, 4, slot, contributes, 0)
    all_c = Gather(g_c, 1, 4, slot, contributes, 1)

    for c in range(2):
        @pl.when(jnp.logical_and(contributes, core == c))
        def _():
            for gather, at in ((all_b, 0), (all_c, 4)):
                mine = own8[at:at + 4, :]
                theirs = sib8[at:at + 4, :]
                first, second = (mine, theirs) if c == 0 else (theirs, mine)
                gather.buf[core, gather.v, gather.u, slot, 0:4, :] = first
                gather.buf[core, gather.v, gather.u, slot, 4:8, :] = second

    both = (all_b, all_c)

    def turn(g, carry):
        tt[g] = t_ref[pl.ds(g * 16, 16)].reshape(1024, 256).T
        return carry

    for gather in both:
        gather.p0_send()
    load_t.wait()
    lax.fori_loop(0, 4, turn, 0)
    for gather in both:
        gather.p0_wait()
        gather.p1_send()
    lax.fori_loop(4, 8, turn, 0)
    for gather in both:
        gather.p1_wait()
        gather.p2_send()
        gather.p3_send(0, 0)

    def fill_c(n, carry):
        pia, rest = n // 8, lax.rem(n, 8)
        px, pzlo = rest // 2, lax.rem(rest, 2)
        ps = lax.rem(pia, 2) * 2 + pzlo
        cblk[pl.ds(pl.multiple_of(n * 8, 8), 8), :] = g_c[pia // 2, y, px, ps]
        return carry

    def fill_b(n, carry):
        pia, py = n // 2, lax.rem(n, 2) * 2
        ps = lax.rem(pia, 2) * 2 + zlo
        one, two = g_b[pia // 2, x, py, ps], g_b[pia // 2, x, py + 1, ps]

        @pl.when(core == 0)
        def _():
            pvec[0:4, :] = one[0:4]
            pvec[4:8, :] = two[0:4]

        @pl.when(core == 1)
        def _():
            pvec[0:4, :] = one[4:8]
            pvec[4:8, :] = two[4:8]

        bblk[pl.ds(pl.multiple_of(n * 8, 8), 8), :] = pvec[...].astype(BF16).astype(F32)
        return carry

    for gather in both:
        gather.p3_wait(0)
    lax.fori_loop(0, 32, fill_c, 0)
    lax.fori_loop(0, 8, fill_b, 0)

    def contract(g, carry):
        half_c = cblk[...].astype(BF16)
        weight = bblk[...]
        parts = []
        for s in range(2):
            piece = t_ref[pl.ds(g * 8 + s * 4, 4)].reshape(256, 256)
            value = dot(piece, half_c).reshape(4, 64, RANK)
            mixed[pl.ds(g * 8 + s * 4, 4)] = value.astype(BF16)
            parts.append(jnp.sum(value * weight[None], axis=1))
        px = g // 4
        pa[lax.rem(px, 2), px // 2, lax.rem(g, 4)] = jnp.concatenate(parts, axis=0)
        return carry

    lax.fori_loop(0, 4, contract, 0)
    for gather in both:
        gather.p2_forward()
    lax.fori_loop(4, 10, contract, 0)
    for gather in both:
        gather.p2_mid()
    lax.fori_loop(10, 16, contract, 0)

    beside = 1 - zlo
    out.send(pa.at[zlo], ra1.at[0], r_a.at[0], sibling, core != half)
    out.send(
        pa.at[beside], ra1.at[1], r_a.at[1], dev(x, y, ia * 2 + beside, core), core == half
    )
    out.send(
        pa.at[beside], ra1.at[2], r_a.at[2], dev(x, y, ia * 2 + beside, 1 - core), core != half
    )
    a_owner = jnp.logical_and(core == half, lax.rem(x, 2) == zlo)
    add_gram(gram_b, all_b.rows(0), True, low_b)
    add_gram(gram_c, all_c.rows(0), True, low_c)
    for gather in both:
        gather.p2_finish()

    all_b.p3_wait(1)
    add_gram(gram_b, all_b.rows(1), False, low_b)
    all_c.p3_wait(1)
    add_gram(gram_c, all_c.rows(1), False, low_c)

    @pl.when(core == half)
    def _():
        for m in range(3):
            recv(ra1.at[m], r_a.at[m]).wait_recv()
        pa[zlo] += ra1[0] + ra1[1] + ra1[2]

    for n in range(1, 16):
        px, py = lax.rem(x + n // 4, 4), lax.rem(y + n % 4, 4)
        out.send(
            pa.at[zlo, px // 2, py], ra2.at[n - 1], r_a.at[2 + n], at_xy(n),
            jnp.logical_and(core == half, lax.rem(px, 2) == zlo),
        )
    all_b.p3_wait(2)
    add_gram(gram_b, all_b.rows(2), False, low_b)
    all_c.p3_wait(2)
    add_gram(gram_c, all_c.rows(2), False, low_c)

    all_b.p3_wait(3)
    add_gram(gram_b, all_b.rows(3), False, low_b)
    all_c.p3_wait(3)
    add_gram(gram_c, all_c.rows(3), False, low_c)
    aslot = lax.rem(ia, 2)
    all_a = Gather(ga, 2, 2, aslot, a_owner, sel0)

    def invert(one, two, gather, begin):
        scale, factors = start_chain(one, two)
        start_inverse(scale, factors[0])
        early = begin()

        def first_axis():
            gather.p0_wait()
            gather.p1_send()

        def second_axis():
            gather.p1_wait()
            gather.p2_send()
            gather.p3_send(0, 0)

        if early:
            first_axis()
        chain_step(0, factors[0], False)
        both_steps(1, factors)
        if not early:
            first_axis()
        both_steps(2, factors)
        if early:
            second_axis()
        both_steps(3, factors)
        if not early:
            second_axis()
        both_steps(4, factors)
        if early:
            gather.p2_forward()
        both_steps(5, factors)
        if early:
            gather.p2_mid()
        else:
            gather.p2_forward()
        both_steps(6, factors)
        if not early:
            gather.p2_mid()
        gather.p2_finish()
        both_steps(7, factors)
        both_steps(8, factors)
        for n in range(4):
            gather.p3_wait(n)

    def begin_a():
        @pl.when(a_owner)
        def _():
            total = pa[zlo, x // 2, y]
            for n in range(1, 16):
                recv(ra2.at[n - 1], r_a.at[2 + n]).wait_recv()
                total = total + ra2[n - 1]
            ga[core, all_a.v, all_a.u, aslot] = total

        all_a.p0_send()
        return False

    close_gram(gram_b, low_b)
    close_gram(gram_c, low_c)
    invert(gram_b, gram_c, all_a, begin_a)
    for n in range(2):
        raw_a[n] = times_inverse(ga[n].reshape(256, RANK)).reshape(4, 4, 2, 8, RANK)

    def fill_a(n, carry):
        px, py = n // 4, lax.rem(n, 4)
        pu = px * (1 - half) + py * half
        pv = py * (1 - half) + px * half
        ablk[pl.ds(pl.multiple_of(n * 8, 8), 8), :] = raw_a[half, pv, pu, aslot]
        return carry

    lax.fori_loop(0, 16, fill_a, 0)

    def second_mode(g, total):
        rows = ablk[pl.ds(pl.multiple_of(g * 8, 8), 8), :].astype(BF16).astype(F32)
        for s in range(8):
            total = total + mixed[g * 8 + s].astype(F32) * rows[s:s + 1, :]
        return total

    part_b = lax.fori_loop(0, 16, second_mode, jnp.zeros((64, RANK), F32))
    pb[...] = part_b.reshape(8, 8, RANK)
    for n in range(1, 16):
        pia, py = lax.rem(ia + n // 4, 4), lax.rem(y + n % 4, 4)
        out.send(
            pb.at[lax.rem(pia, 2) * 4 + py], rb1.at[n - 1], r_b.at[n - 1], at_iy(n),
            pia // 2 == core,
        )
    for n in range(2):
        add_gram(gram_a, [raw_a[n].reshape(256, RANK)], n == 0)

    all_b2 = Gather(gb, 3, 4, slot, contributes, sel0)

    @pl.when(core == half)
    def _():
        rows = pb[lax.rem(ia, 2) * 4 + y]
        for n in range(1, 16):
            recv(rb1.at[n - 1], r_b.at[n - 1]).wait_recv()
            rows = rows + rb1[n - 1]
        gb[core, all_b2.v, all_b2.u, slot] = rows

    all_b2.p0_send()
    inverse_a = normal_gram(gram_a, 512)

    def repeat_a(g, carry):
        rows = ablk[pl.ds(pl.multiple_of(g * 8, 8), 8), :].astype(BF16).astype(F32)
        for s in range(8):
            arep[g * 8 + s] = jnp.broadcast_to(rows[s:s + 1, :], (16, RANK)).astype(BF16)
        return carry

    lax.fori_loop(0, 16, repeat_a, 0)

    own_a = ablk[pl.ds(pl.multiple_of(ja * 8, 8), 8), :] * inverse_a
    for s in range(4):
        @pl.when(ka == s)
        def _():
            a_out[0, 0] = own_a[2 * s:2 * s + 2]

    invert(gram_a, gram_c, all_b2, lambda: True)

    def fill_b2(n, carry):
        py = lax.rem(n, 4)
        pu = x * sel0 + py * core
        pv = py * sel0 + x * core
        rows = gb[core, pv, pu, (n // 4) * 2 + zlo] * inverse_a
        b2blk[pl.ds(pl.multiple_of(n * 8, 8), 8), :] = rows
        return carry

    lax.fori_loop(0, 8, fill_b2, 0)
    b2blk[...] = times_inverse(b2blk[...])

    pc[...] = jnp.zeros_like(pc)

    def third_mode(g, carry):
        half_b2 = b2blk[...].astype(BF16).reshape(4, 16, RANK)
        weight = jnp.concatenate(
            [(half_b2 * arep[g * 16 + n][None]).reshape(64, RANK) for n in range(16)], axis=0
        )
        pc[...] += dot(tt[g], weight).reshape(4, 4, 2, 8, RANK)
        return carry

    lax.fori_loop(0, 8, third_mode, 0)
    out.send(pc.at[pl.ds(2 * (1 - core), 2)], rc0, r_c.at[0], sibling)

    def all_rows(n, carry):
        h, pair = n // 2, lax.rem(n, 2) * 2
        rows = times_inverse(gb[h, pl.ds(pair, 2)].reshape(256, RANK) * inverse_a)
        high, low = split_two(rows)
        mh[...] = high
        ml[...] = low
        high, low = mh[...], ml[...]
        gram_b2[...] += dot_rows(high, high)
        low_b[...] += dot_rows(high, low)
        return carry

    gram_b2[...] = jnp.zeros_like(gram_b2)
    low_b[...] = jnp.zeros_like(low_b)
    lax.fori_loop(0, 3, all_rows, 0)
    recv(rc0, r_c.at[0]).wait_recv()
    pc[pl.ds(2 * core, 2)] += rc0[...]
    for d in (1, 2, 3):
        out.send(
            pc.at[pl.ds(2 * core, 2), lax.rem(x + d, 4)], rc1.at[d - 1], r_c.at[d], at_x(d)
        )
    lax.fori_loop(3, 4, all_rows, 0)
    close_gram(gram_b2, low_b)
    inverse_b = normal_gram(gram_b2, 1024)
    own_b = b2blk[pl.ds(pl.multiple_of((ia * 2 + ka // 2) * 8, 8), 8), :] * inverse_b
    for s in range(2):
        @pl.when(lax.rem(ka, 2) == s)
        def _():
            b_out[0, 0] = own_b[4 * s:4 * s + 4]

    scale, factors = start_chain(gram_a, gram_b2)
    for q in (0, 1):
        chain_step(q, factors[q], False)
    for d in (1, 2, 3):
        recv(rc1.at[d - 1], r_c.at[d]).wait_recv()
    sc[...] = pc[pl.ds(2 * core, 2), x] + rc1[0] + rc1[1] + rc1[2]
    for d in range(8):
        pz = lax.rem(z + d, 8)
        for other in range(2):
            if d == 0 and not other:
                continue
            out.send(
                sc.at[lax.rem(pz // 2, 2), lax.rem(pz, 2)], rc2.at[d], r_c.at[4 + d],
                dev(x, y, pz, core * (1 - other) + (1 - core) * other), pz // 4 == core,
            )
    for q in (2, 3, 4):
        chain_step(q, factors[q], False)
    for d in range(1, 8):
        recv(rc2.at[d], r_c.at[4 + d]).wait_recv()

    @pl.when(core == half)
    def _():
        tc[...] = sc[lax.rem(ia, 2), zlo]

    @pl.when(core != half)
    def _():
        recv(rc2.at[0], r_c.at[4]).wait_recv()
        tc[...] = rc2[0]

    total = tc[...]
    for d in range(1, 8):
        total = total + rc2[d]
    join(5, total * (inverse_a * inverse_b), scale, factors)
    for q in range(5, STEPS - 1):
        chain_step(q, factors[q], True)
    raw = last_step(factors)

    sq1[...] = jnp.sum(raw * raw, axis=0, keepdims=True)
    for n in range(1, 16):
        out.send(sq1, rq1.at[n - 1], r_q.at[n - 1], at_xy(n))
    total = sq1[...]
    for n in range(1, 16):
        recv(rq1.at[n - 1], r_q.at[n - 1]).wait_recv()
        total = total + rq1[n - 1]
    sq3[...] = total
    for d in range(1, 8):
        out.send(sq3, rq3.at[d - 1], r_q.at[14 + d], at_z(d))
    out.finish()
    for d in range(1, 8):
        recv(rq3.at[d - 1], r_q.at[14 + d]).wait_recv()
    total = sq3[...]
    for d in range(7):
        total = total + rq3[d]
    spread = jnp.sqrt(total / 1024 + EPS)
    final = raw / spread
    for s in range(2):
        @pl.when(core == s)
        def _():
            c_out[0, 0] = final[4 * s:4 * s + 4]


def hand_over(a_ref, b_ref, c_ref, a_out, b_out, c_out):
    a_out[...] = a_ref[...]
    b_out[...] = b_ref[...]
    c_out[...] = c_ref[...]


def shards(tensor, factor_b, factor_c):
    vmem = pltpu.VMEM
    dma = pltpu.SemaphoreType.DMA
    scratch = [
        vmem((128, 64, 256), BF16),
        vmem((8, 256, 1024), BF16),
        vmem((128, 64, RANK), BF16),
        vmem((128, 16, RANK), BF16),
        vmem((8, RANK), F32),
        vmem((8, RANK), F32),
        vmem((2, 4, 4, 4, 8, RANK), F32),
        vmem((2, 4, 4, 4, 8, RANK), F32),
        vmem((2, 4, 4, 2, 8, RANK), F32),
        vmem((2, 4, 4, 4, 8, RANK), F32),
        vmem((2, 2, 4, 8, RANK), F32),
        vmem((8, 8, RANK), F32),
        vmem((4, 4, 2, 8, RANK), F32),
        vmem((3, 2, 4, 8, RANK), F32),
        vmem((15, 8, RANK), F32),
        vmem((15, 8, RANK), F32),
        vmem((2, 4, 2, 8, RANK), F32),
        vmem((3, 2, 2, 8, RANK), F32),
        vmem((2, 2, 8, RANK), F32),
        vmem((8, 8, RANK), F32),
        vmem((8, RANK), F32),
        vmem((15, 1, RANK), F32),
        vmem((7, 1, RANK), F32),
        vmem((1, RANK), F32),
        vmem((1, RANK), F32),
        vmem((256, RANK), BF16),
        vmem((256, RANK), BF16),
        vmem((RANK, RANK), F32),
        vmem((RANK, RANK), F32),
        vmem((RANK, RANK), F32),
        vmem((RANK, RANK), F32),
        vmem((RANK, RANK), F32),
        vmem((STEPS, RANK + 16, RANK), BF16),
        vmem((STEPS, RANK, RANK), BF16),
        vmem((RANK, RANK), F32),
        vmem((RANK, RANK), F32),
        vmem((8, RANK), F32),
        vmem((RANK, RANK), F32),
        vmem((2, RANK, RANK), BF16),
        vmem((2, RANK, RANK), BF16),
        vmem((2, 4, 4, 2, 8, RANK), F32),
        vmem((2, 4, 4, 4, 8, RANK), F32),
        vmem((64, RANK), F32),
        vmem((256, RANK), F32),
        vmem((128, RANK), F32),
        vmem((64, RANK), F32),
        vmem((8, RANK), F32),
        dma((192,)),
        dma((1,)),
        dma((4, 4)),
        dma((4, 3)),
        dma((4, 6)),
        dma((4, 4)),
        dma((18,)),
        dma((15,)),
        dma((12,)),
        dma((22,)),
        dma,
    ]
    results = pl.pallas_call(
        kernel,
        out_shape=(
            jax.ShapeDtypeStruct((1, 1, 2, RANK), F32),
            jax.ShapeDtypeStruct((1, 1, 4, RANK), F32),
            jax.ShapeDtypeStruct((1, 1, 4, RANK), F32),
        ),
        in_specs=[
            pl.BlockSpec(memory_space=pl.ANY),
            pl.BlockSpec(memory_space=pltpu.VMEM),
            pl.BlockSpec(memory_space=pltpu.VMEM),
        ],
        out_specs=[pl.BlockSpec(memory_space=pltpu.VMEM)] * 3,
        scratch_shapes=scratch,
        compiler_params=pltpu.CompilerParams(
            collective_id=0, has_side_effects=True, vmem_limit_bytes=58 * 1024 * 1024
        ),
        name="sweep",
    )(tensor, factor_b, factor_c)
    return pl.pallas_call(
        hand_over,
        out_shape=tuple(jax.ShapeDtypeStruct(r.shape, F32) for r in results),
        name="hand_over",
    )(*results)


def solution(mesh):
    in_specs = (
        P("ia", "ja", "ka"),
        P("ja", ("ia", "ka"), None, None),
        P("ka", ("ia", "ja"), None, None),
    )
    out_specs = (
        P("ia", ("ja", "ka"), None, None),
        P("ja", ("ia", "ka"), None, None),
        P("ka", ("ia", "ja"), None, None),
    )
    return jax.shard_map(shards, mesh=mesh, in_specs=in_specs, out_specs=out_specs, check_vma=False)
```
